32 devices in a mesh: sp: 16 (over z, y, core), dp: 2 (over x).
Axes of the slice: x: 2, y: 2, z: 4, core: 2. Of those that a mesh axis runs over, the one named last changes fastest.
Arguments:
- section_two: bfloat16 [3, 2, 112, 224, 192], P(None, 'dp', 'sp'), may hold values from -6 to 6
- widths: int32 [3, 2], P(None, 'dp'), may hold values from 7 to 112, as said below
- red_gain: float32 [768], replicated, may hold values from 0.5 to 1.5
- red_shift: float32 [768], replicated, may hold values from -1.8 to 1.8
- w_red: bfloat16 [768, 384], P('dp', 'sp'), may hold values from -0.21875 to 0.21875
- norm1_gain: float32 [384], replicated, may hold values from 0.5 to 1.5
- norm1_shift: float32 [384], replicated, may hold values from -1.8 to 1.8
- w_qkv: bfloat16 [384, 1152], P('dp', 'sp'), may hold values from -0.3125 to 0.3125
- b_qkv: float32 [1152], replicated, may hold values from -3 to 3
- bias_table: float32 [169, 12], replicated, may hold values from -4 to 4
- w_proj: bfloat16 [384, 384], P('dp', 'sp'), may hold values from -1.25 to 1.25
- b_proj: float32 [384], replicated, may hold values from -3 to 3
- norm2_gain: float32 [384], replicated, may hold values from 0.5 to 1.5
- norm2_shift: float32 [384], replicated, may hold values from -1.8 to 1.8
- w_fc1: bfloat16 [384, 1536], P('dp', 'sp'), may hold values from -0.3125 to 0.3125
- b_fc1: float32 [1536], replicated, may hold values from -3 to 3
- w_fc2: bfloat16 [1536, 384], P('dp', 'sp'), may hold values from -0.15625 to 0.15625
- b_fc2: float32 [384], replicated, may hold values from -3 to 3
- cotangent: float32 [3, 2, 16, 7, 56, 384], P(None, 'dp', 'sp'), may hold values from -6 to 6
Outputs:
- output: float32 [3, 2, 16, 7, 56, 384], P(None, 'dp', 'sp')
- grad_input: bfloat16 [3, 2, 112, 224, 192], P(None, 'dp', 'sp')
- grad_red_gain: float32 [768], replicated
- grad_red_shift: float32 [768], replicated
- grad_w_red: float32 [768, 384], P('dp', 'sp')
- grad_norm1_gain: float32 [384], replicated
- grad_norm1_shift: float32 [384], replicated
- grad_w_qkv: float32 [384, 1152], P('dp', 'sp')
- grad_b_qkv: float32 [1152], replicated
- grad_bias_table: float32 [169, 12], replicated
- grad_w_proj: float32 [384, 384], P('dp', 'sp')
- grad_b_proj: float32 [384], replicated
- grad_norm2_gain: float32 [384], replicated
- grad_norm2_shift: float32 [384], replicated
- grad_w_fc1: float32 [384, 1536], P('dp', 'sp')
- grad_b_fc1: float32 [1536], replicated
- grad_w_fc2: float32 [1536, 384], P('dp', 'sp')
- grad_b_fc2: float32 [384], replicated
The draws below stay inside these ranges and needn't reach their ends.
Inputs may be any that keep to these rules, and one draw needn't show every extreme that they name: widths[m, n] is how many of the 112 section-3 columns hold tokens of image (m, n); image (0, 0) is 112 wide and the last image of the last micro-batch 7 wide.
All inputs are finite; a program needn't handle non-finite values.
Results may differ from the reference program's by a relative error of at most 0.018.
Values may be sent and summed in bfloat16 or wider, within the bound.
No kernel may reach another device: no remote copies, remote signals or barrier semaphores. Data moves between devices by JAX's collectives and lax.ppermute only.
A program may use at most 128 MiB of HBM per device.

```python
import jax
import jax.numpy as jnp
from jax import lax

C2 = 192
C = 384
HEADS = 12
HD = 32
FF = 1536
MB = 3
WH = 8
CM = 768
IMGS = 2
W3 = 112
W2 = 224
H2 = 112
N_SP = 16


def draw_widths(key, part):
    key = jax.random.fold_in(key, 11)
    values = jax.random.randint(key, (MB, IMGS), 7, W3 + 1, dtype=jnp.int32)
    values = values.at[0, 0].set(W3)
    values = values.at[MB - 1, IMGS - 1].set(7)
    return values


def levels(stream_key, extent, shards, least, high):
    factor_of, own = 1.0, jax.random.fold_in(stream_key, 6)
    for axis_at, parts in shards:
        draws = jnp.exp(jax.random.uniform(jax.random.fold_in(own, axis_at), (parts,), jnp.float32, least / len(shards), high / len(shards)))
        factor_of = factor_of * jnp.repeat(draws, extent[axis_at] // parts).reshape([-1 if axis == axis_at else 1 for axis in range(len(extent))])
    return factor_of


def bell_draw(key, extent, deviation, bound, split=(), kind=jnp.bfloat16):
    values = jax.random.normal(key, extent, jnp.float32) * deviation
    if len(split) > 0:
        values = levels(key, extent, split, -0.22, 0.18) * values
    return jnp.clip(values, min=-bound, max=bound).astype(kind)


def setup_inputs(seed: int = 0) -> dict:
    keys = jax.random.split(jax.random.key(seed), 20)
    return {
        "section_two": bell_draw(keys[0], (MB, IMGS, H2, W2, C2), 1.0, 6.0, ((1, 2), (2, 16))),
        "widths": draw_widths(jax.random.fold_in(keys[19], 71), 0),
        "red_gain": jnp.clip(1.0 + 0.1 * jax.random.normal(keys[2], (CM,), jnp.float32), 0.5, 1.5),
        "red_shift": bell_draw(keys[3], (CM,), 0.3, 1.8, (), jnp.float32),
        "w_red": bell_draw(keys[4], (CM, C), CM ** -0.5, 0.21875, ((0, 2), (1, 16))),
        "norm1_gain": jnp.clip(1.0 + 0.1 * jax.random.normal(keys[5], (C,), jnp.float32), 0.5, 1.5),
        "norm1_shift": bell_draw(keys[6], (C,), 0.3, 1.8, (), jnp.float32),
        "w_qkv": bell_draw(keys[7], (C, 3 * C), C ** -0.5, 0.3125, ((0, 2), (1, 16))),
        "b_qkv": bell_draw(keys[8], (3 * C,), 0.5, 3.0, (), jnp.float32),
        "bias_table": bell_draw(keys[9], (169, HEADS), 1.0, 4.0, (), jnp.float32),
        "w_proj": bell_draw(keys[10], (C, C), (max(C // 16, 1)) ** -0.5, 1.25, ((0, 2), (1, 16))),
        "b_proj": bell_draw(keys[11], (C,), 0.5, 3.0, (), jnp.float32),
        "norm2_gain": jnp.clip(1.0 + 0.1 * jax.random.normal(keys[12], (C,), jnp.float32), 0.5, 1.5),
        "norm2_shift": bell_draw(keys[13], (C,), 0.3, 1.8, (), jnp.float32),
        "w_fc1": bell_draw(keys[14], (C, FF), C ** -0.5, 0.3125, ((0, 2), (1, 16))),
        "b_fc1": bell_draw(keys[15], (FF,), 0.5, 3.0, (), jnp.float32),
        "w_fc2": bell_draw(keys[16], (FF, C), FF ** -0.5, 0.15625, ((0, 2), (1, 16))),
        "b_fc2": bell_draw(keys[17], (C,), 0.5, 3.0, (), jnp.float32),
        "cotangent": bell_draw(keys[18], (MB, IMGS, N_SP, 7, 7 * WH, C), 1.0, 6.0, ((1, 2), (2, 16)), jnp.float32),
    }


@jax.custom_vjp
def low(v):
    return lax.optimization_barrier(v.astype(jnp.bfloat16)).astype(jnp.float32)

@jax.custom_vjp
def low_back(v):
    return v

def low_keep(v):
    return (low(v), None)

def low_pass(kept, grad):
    return (grad,)

def back_keep(v):
    return (v, None)

def back_low(kept, grad):
    return (low(grad),)
low.defvjp(low_keep, low_pass)
low_back.defvjp(back_keep, back_low)
EPSILON = 1e-05
HIGHEST = lax.Precision.HIGHEST

def exact_dot(left, right):
    return jnp.dot(left, right, precision=HIGHEST, preferred_element_type=jnp.float32)

def layer_norm(values, scale_gain, offset):
    center = lax.optimization_barrier(jnp.mean(values, -1, keepdims=True))
    shifted = values - center
    spread = lax.optimization_barrier(jnp.mean(shifted * shifted, -1, keepdims=True))
    return shifted * lax.rsqrt(spread + EPSILON) * scale_gain + offset

def offset_table():
    places = jnp.arange(49, dtype=jnp.int32)
    row_place = places // 7
    col_place = places % 7
    rel_index = (row_place[:, None] - row_place[None, :] + 6) * 13 + (col_place[:, None] - col_place[None, :] + 6)
    return (rel_index[:, :, None] == jnp.arange(169, dtype=jnp.int32)[None, None, :]).astype(jnp.float32)

def forward(section_input, keep_mask, red_gain, red_shift, w_red, norm1_gain, norm1_shift, w_qkv, b_qkv, bias_table, w_proj, b_proj, norm2_gain, norm2_shift, w_fc1, b_fc1, w_fc2, b_fc2):
    images = section_input.shape[0]
    rows_three = section_input.shape[1] // 2
    cols_three = section_input.shape[2] // 2
    win_rows = rows_three // 7
    win_cols = cols_three // 7
    windows = win_rows * win_cols
    section_vals = low_back(section_input)
    merged = section_vals.reshape(images, rows_three, 2, cols_three, 2, C2).transpose(0, 1, 3, 4, 2, 5).reshape(images, rows_three, cols_three, 4 * C2)
    merged = merged.reshape(images, win_rows, 7, win_cols, 7, 4 * C2).transpose(0, 1, 3, 2, 4, 5).reshape(images, windows, 49, 4 * C2)
    stream = low_back(exact_dot(low(layer_norm(merged, red_gain, red_shift)), w_red))
    first_norm = layer_norm(stream, norm1_gain, norm1_shift)
    projected = low_back(exact_dot(low(first_norm), w_qkv) + b_qkv)
    query_rows = low(projected[..., :C] * HD ** (-0.5)).reshape(images, windows, 49, HEADS, HD)
    key_rows = low(projected[..., C:2 * C]).reshape(images, windows, 49, HEADS, HD)
    value_rows = low(projected[..., 2 * C:]).reshape(images, windows, 49, HEADS, HD)
    position_bias = jnp.einsum('ijt,th->hij', offset_table(), bias_table, precision=HIGHEST)

    def attend(pieces):
        part_query, part_keys, part_values, part_keep = pieces
        scores = jnp.einsum('nqhd,nkhd->nhqk', part_query, part_keys, precision=HIGHEST) + position_bias[None]
        scores = low_back(scores)
        scores = jnp.where(part_keep[:, None, None, :] > 0.5, scores, -1e+30)
        row_top = lax.optimization_barrier(jnp.max(scores, -1, keepdims=True))
        exponent = jnp.exp(scores - row_top)
        soft_weights = exponent / lax.optimization_barrier(jnp.sum(exponent, -1, keepdims=True))
        return jnp.einsum('nhqk,nkhd->nqhd', low(soft_weights), part_values, precision=HIGHEST)
    attended = lax.map(jax.checkpoint(attend), (query_rows, key_rows, value_rows, keep_mask))
    attended = low_back(attended.reshape(images, windows, 49, C))
    branch = low_back(exact_dot(low(attended), w_proj) + b_proj)
    middle = stream + branch
    second_norm = layer_norm(middle, norm2_gain, norm2_shift)
    hidden_pre = low_back(exact_dot(low(second_norm), w_fc1) + b_fc1)
    feed = low_back(exact_dot(low(jax.nn.gelu(hidden_pre, approximate=False)), w_fc2) + b_fc2)
    result = (middle + feed) * keep_mask[..., None]
    result = result.reshape(images, win_rows, 2, WH, 7, 7, C).transpose(0, 1, 2, 4, 3, 5, 6)
    return result.reshape(MB, IMGS, win_rows * 2, 7, 7 * WH, C)

def reference(section_two, widths, red_gain, red_shift, w_red, norm1_gain, norm1_shift, w_qkv, b_qkv, bias_table, w_proj, b_proj, norm2_gain, norm2_shift, w_fc1, b_fc1, w_fc2, b_fc2, cotangent):
    images = MB * IMGS
    columns = jnp.arange(W3, dtype=jnp.int32).reshape(2 * WH, 7)
    keep = (columns[None] < widths.reshape(images, 1, 1)).astype(jnp.float32)
    keep_mask = jnp.broadcast_to(keep[:, None, :, None, :], (images, N_SP // 2, 2 * WH, 7, 7)).reshape(images, N_SP // 2 * 2 * WH, 49)
    flat_input = section_two.astype(jnp.float32).reshape(images, H2, W2, C2)
    params = (red_gain, red_shift, w_red.astype(jnp.float32), norm1_gain, norm1_shift, w_qkv.astype(jnp.float32), b_qkv, bias_table, w_proj.astype(jnp.float32), b_proj, norm2_gain, norm2_shift, w_fc1.astype(jnp.float32), b_fc1, w_fc2.astype(jnp.float32), b_fc2)

    def wrapped(flat, *weights):
        return forward(flat, keep_mask, *weights)
    result, pull = jax.vjp(wrapped, flat_input, *params)
    grads = pull(cotangent)
    grad_input = grads[0].reshape(MB, IMGS, H2, W2, C2).astype(jnp.bfloat16)
    return (result, grad_input, grads[1], grads[2], grads[3], grads[4], grads[5], grads[6], grads[7], grads[8], grads[9], grads[10], grads[11], grads[12], grads[13], grads[14], grads[15], grads[16])
```

```python
import functools

import jax
import jax.numpy as jnp
import numpy as np
from jax import lax
from jax.experimental import pallas as pl
from jax.experimental.pallas import tpu as pltpu
from jax.sharding import PartitionSpec as P

C2 = 192
C = 384
HEADS = 12
HD = 32
FF = 1536
MB = 3
WH = 8
TOK = 7 * 7 * WH
SLOT = 64
WROWS = WH * SLOT
CHUNK = 512
EPSILON = 1e-05
DEAD = -1e30
HIGHEST = lax.Precision.HIGHEST
F32 = jnp.float32
BF16 = jnp.bfloat16
VMEM_BYTES = 56 * 1024 * 1024


def nn(left, right):
    return lax.dot_general(left, right, (((1,), (0,)), ((), ())), preferred_element_type=F32)


def nt(left, right):
    return lax.dot_general(left, right, (((1,), (1,)), ((), ())), preferred_element_type=F32)


def tn(left, right):
    return lax.dot_general(left, right, (((0,), (0,)), ((), ())), preferred_element_type=F32)


def constants():
    to_window = np.zeros((WROWS, TOK), np.float32)
    for w in range(WH):
        for r in range(7):
            for c in range(7):
                to_window[w * SLOT + 7 * r + c, r * 56 + 7 * w + c] = 1
    split = np.zeros((112, 112), np.float32)
    for j in range(56):
        split[j, 2 * j] = 1
        split[56 + j, 2 * j + 1] = 1
    head_mask = (np.arange(256)[:, None] // SLOT == np.arange(128)[None] // HD).astype(np.float32)
    group_ones = (np.arange(256)[:, None] // SLOT == np.arange(256)[None] // SLOT).astype(np.float32)
    key = np.arange(256) % SLOT
    key_col = np.where(key < 49, key % 7, 1 << 20).astype(np.int32)[None]
    nat_col = (np.arange(TOK) % 56).astype(np.int32)[:, None]
    low = lambda a: jnp.asarray(a, BF16)
    return dict(
        to_window=low(to_window),
        to_natural=low(to_window.T),
        split=low(split),
        join=low(split.T),
        head_mask=low(head_mask),
        group_ones=low(group_ones),
        key_col=jnp.asarray(key_col),
        nat_col=jnp.asarray(nat_col),
    )


def offset_onehot():
    place = np.arange(49)
    index = (place[:, None] // 7 - place[None] // 7 + 6) * 13 + (place[:, None] % 7 - place[None] % 7 + 6)
    table = np.zeros((SLOT, SLOT, 169), np.float32)
    table[:49, :49] = index[:, :, None] == np.arange(169)
    return table.reshape(SLOT * SLOT, 169)


def spread_bias(bias_table):
    pairs = jnp.dot(jnp.asarray(offset_onehot()), bias_table, precision=HIGHEST)
    pairs = pairs.reshape(SLOT, SLOT, 3, 4).transpose(2, 0, 3, 1).reshape(3, SLOT, 256)
    pad = np.where(np.arange(256) % SLOT < 49, 0.0, DEAD).astype(np.float32)
    return pairs + jnp.asarray(pad)


def gather_table(pair_sums):
    pairs = pair_sums.reshape(3, SLOT, 4, SLOT).transpose(1, 3, 0, 2).reshape(SLOT * SLOT, HEADS)
    return lax.dot_general(
        jnp.asarray(offset_onehot()), pairs, (((0,), (0,)), ((), ())), precision=HIGHEST
    )


def load_merged(core, section_ref, incoming_ref, split, parts_ref):
    column = pl.multiple_of(core * 112, 16)
    is_left = core == 0
    for r in range(14):
        own = section_ref[0, r % 7, pl.ds(column, 112), :]
        other = incoming_ref[0, r % 7]
        row = jnp.where(is_left, own, other) if r < 7 else jnp.where(is_left, other, own)
        apart = nn(split, row)
        parts_ref[r % 2, (r // 2) * 56 : (r // 2) * 56 + 56, :] = apart[:56]
        parts_ref[2 + r % 2, (r // 2) * 56 : (r // 2) * 56 + 56, :] = apart[56:]


def merge_norm(parts_ref):
    total = sum(jnp.sum(parts_ref[f], -1, keepdims=True) for f in range(4))
    center = total * (1.0 / (4 * C2))
    spread = 0.0
    for f in range(4):
        shifted = parts_ref[f] - center
        spread = spread + jnp.sum(shifted * shifted, -1, keepdims=True)
    return center, lax.rsqrt(spread * (1.0 / (4 * C2)) + EPSILON)


def norm_of(values):
    center = jnp.mean(values, -1, keepdims=True)
    shifted = values - center
    inverse = lax.rsqrt(jnp.mean(shifted * shifted, -1, keepdims=True) + EPSILON)
    return shifted * inverse, inverse


def norm_back(grad_out, normal, inverse, gain):
    grad_normal = grad_out * gain
    grad_in = inverse * (
        grad_normal
        - jnp.mean(grad_normal, -1, keepdims=True)
        - normal * jnp.mean(grad_normal * normal, -1, keepdims=True)
    )
    return (
        grad_in,
        jnp.sum(grad_out * normal, 0, keepdims=True),
        jnp.sum(grad_out, 0, keepdims=True),
    )


def four_heads(rows, head_mask):
    return jnp.concatenate([rows] * 4, axis=0) * head_mask


def fold_heads(rows, head_mask):
    picked = rows * head_mask.astype(F32)
    return picked[:64] + picked[64:128] + picked[128:192] + picked[192:]


def forward_kernel(
    core_ref, widths_ref, section_ref, incoming_ref, red_gain_ref, red_shift_ref, w_red_ref,
    gain_ref, shift_ref, w_qkv_ref, b_qkv_ref, bias_ref, to_window_ref, to_natural_ref,
    split_ref, head_mask_ref, group_ones_ref, key_col_ref,
    stream_ref, qkv_ref, soft_ref, attended_ref,
    parts_ref, window_ref,
):
    core = core_ref[0]
    width = widths_ref[pl.program_id(0)]
    load_merged(core, section_ref, incoming_ref, split_ref[...], parts_ref)
    center, inverse = merge_norm(parts_ref)
    stream = 0.0
    for f in range(4):
        normed = (parts_ref[f] - center) * inverse * red_gain_ref[f : f + 1] + red_shift_ref[f : f + 1]
        stream = stream + nt(normed.astype(BF16), w_red_ref[f])
    stream_ref[0] = stream
    normal, _ = norm_of(stream)
    first = (normal * gain_ref[...] + shift_ref[...]).astype(BF16)
    projected = nt(first, w_qkv_ref[...]) + b_qkv_ref[...]
    query = (projected[:, :C] * (HD**-0.5)).astype(BF16)
    rest = projected[:, C:].astype(BF16)
    to_window = to_window_ref[...]
    qkv_ref[0, :, :C] = nn(to_window, query).astype(BF16)
    qkv_ref[0, :, C:] = nn(to_window, rest).astype(BF16)
    key_col = key_col_ref[...]

    def window(w, carry):
        rows = pl.ds(pl.multiple_of(w * SLOT, SLOT), SLOT)
        live = jnp.where(key_col + (core * 56 + w * 7) < width, 0.0, DEAD)
        low_half = lax.broadcasted_iota(jnp.int32, (SLOT, 128), 1) < SLOT
        for t in range(3):
            lanes = slice(128 * t, 128 * t + 128)
            q = qkv_ref[0, rows, 128 * t : 128 * t + 128]
            k = qkv_ref[0, rows, C + 128 * t : C + 128 * t + 128]
            v = qkv_ref[0, rows, 2 * C + 128 * t : 2 * C + 128 * t + 128]
            head_mask = head_mask_ref[...]
            scores = nt(q, four_heads(k, head_mask)) + bias_ref[t] + live
            tops = []
            for half in range(2):
                part = scores[:, 128 * half : 128 * half + 128]
                first_top = jnp.max(jnp.where(low_half, part, 2 * DEAD), -1, keepdims=True)
                second_top = jnp.max(jnp.where(low_half, 2 * DEAD, part), -1, keepdims=True)
                tops.append(jnp.where(low_half, first_top, second_top))
            exponent = jnp.exp(scores - jnp.concatenate(tops, axis=1))
            total = nn(exponent.astype(BF16), group_ones_ref[...])
            soft = (exponent / total).astype(BF16)
            soft_ref[0, w, t] = soft
            window_ref[rows, lanes] = nn(soft, four_heads(v, head_mask)).astype(BF16)
        return carry

    lax.fori_loop(0, WH, window, 0)
    attended_ref[0] = nn(to_natural_ref[...], window_ref[...]).astype(BF16)


def feed_kernel(
    core_ref, widths_ref, stream_ref, attended_ref, cotangent_ref, nat_col_ref,
    w_proj_ref, b_proj_ref, gain_ref, shift_ref, w_fc1_ref, b_fc1_ref, w_fc2_ref, b_fc2_ref,
    output_ref, grad_middle_ref, grad_att_ref, g_proj_ref, g_fc1_ref, g_fc2_ref,
    g_bproj_ref, g_gain_ref, g_shift_ref, g_bfc1_ref, g_bfc2_ref,
    second_ref, grad_feed_ref, grad_second_ref,
):
    step = pl.program_id(0)

    @pl.when(step == 0)
    def _():
        for ref in (g_proj_ref, g_fc1_ref, g_fc2_ref, g_bproj_ref, g_gain_ref, g_shift_ref, g_bfc1_ref, g_bfc2_ref):
            ref[...] = jnp.zeros_like(ref)

    keep = jnp.where(nat_col_ref[...] + core_ref[0] * 56 < widths_ref[step], 1.0, 0.0)
    attended = attended_ref[0]
    middle = stream_ref[0] + nt(attended, w_proj_ref[...]) + b_proj_ref[...]
    normal, inverse = norm_of(middle)
    second_ref[...] = (normal * gain_ref[...] + shift_ref[...]).astype(BF16)
    grad_sum = cotangent_ref[0] * keep
    grad_feed = grad_sum.astype(BF16)
    grad_feed_ref[...] = grad_feed
    g_bfc2_ref[...] += jnp.sum(grad_feed.astype(F32), 0, keepdims=True)
    output_ref[0] = middle + b_fc2_ref[...]
    grad_second_ref[...] = jnp.zeros_like(grad_second_ref)

    def hidden(j, carry):
        units = pl.ds(pl.multiple_of(j * CHUNK, CHUNK), CHUNK)
        w_fc1 = w_fc1_ref[units, :]
        w_fc2 = w_fc2_ref[:, units]
        second = second_ref[...]
        feed = grad_feed_ref[...]
        pre = nt(second, w_fc1) + b_fc1_ref[:, units]
        cdf = 0.5 * (1.0 + lax.erf(pre * 0.7071067811865476))
        act = (pre * cdf).astype(BF16)
        slope = cdf + pre * jnp.exp(-0.5 * pre * pre) * 0.3989422804014327
        output_ref[0] += nt(act, w_fc2)
        g_fc2_ref[:, units] += tn(feed, act)
        grad_pre = (nn(feed, w_fc2) * slope).astype(BF16)
        g_bfc1_ref[:, units] += jnp.sum(grad_pre.astype(F32), 0, keepdims=True)
        g_fc1_ref[units, :] += tn(grad_pre, second)
        grad_second_ref[...] += nn(grad_pre, w_fc1)
        return carry

    lax.fori_loop(0, FF // CHUNK, hidden, 0)
    output_ref[0] = output_ref[0] * keep
    grad_norm, g_gain, g_shift = norm_back(grad_second_ref[...], normal, inverse, gain_ref[...])
    g_gain_ref[...] += g_gain
    g_shift_ref[...] += g_shift
    grad_middle = grad_sum + grad_norm
    grad_middle_ref[0] = grad_middle
    branch = grad_middle.astype(BF16)
    g_bproj_ref[...] += jnp.sum(branch.astype(F32), 0, keepdims=True)
    g_proj_ref[...] += tn(branch, attended)
    grad_att_ref[0] = nn(branch, w_proj_ref[...]).astype(BF16)


def backward_kernel(
    core_ref, section_ref, incoming_ref, red_gain_ref, red_shift_ref, w_red_ref,
    gain_ref, shift_ref, w_qkv_ref, to_window_ref, to_natural_ref, split_ref, join_ref,
    head_mask_ref, group_ones_ref, stream_ref, qkv_ref, soft_ref, grad_middle_ref, grad_att_ref,
    own_ref, send_ref, g_red_ref, g_qkv_ref, g_pairs_ref,
    g_rgain_ref, g_rshift_ref, g_gain_ref, g_shift_ref, g_bqkv_ref,
    parts_ref, window_ref, grad_window_ref,
):
    core = core_ref[0]

    @pl.when(pl.program_id(0) == 0)
    def _():
        for ref in (g_red_ref, g_qkv_ref, g_pairs_ref, g_rgain_ref, g_rshift_ref, g_gain_ref, g_shift_ref, g_bqkv_ref):
            ref[...] = jnp.zeros_like(ref)

    window_ref[...] = nn(to_window_ref[...], grad_att_ref[0]).astype(BF16)

    def window(w, carry):
        rows = pl.ds(pl.multiple_of(w * SLOT, SLOT), SLOT)
        for t in range(3):
            q = qkv_ref[0, rows, 128 * t : 128 * t + 128]
            k = qkv_ref[0, rows, C + 128 * t : C + 128 * t + 128]
            v = qkv_ref[0, rows, 2 * C + 128 * t : 2 * C + 128 * t + 128]
            grad = window_ref[rows, 128 * t : 128 * t + 128]
            head_mask = head_mask_ref[...]
            soft = soft_ref[0, w, t]
            grad_soft = nt(grad, four_heads(v, head_mask))
            weighted = grad_soft * soft.astype(F32)
            inner = nn(weighted.astype(BF16), group_ones_ref[...])
            scores = (weighted - soft.astype(F32) * inner).astype(BF16)
            g_pairs_ref[t] += scores.astype(F32)
            grad_query = nn(scores, four_heads(k, head_mask)) * (HD**-0.5)
            grad_key = fold_heads(tn(scores, q), head_mask)
            grad_value = fold_heads(tn(soft, grad), head_mask)
            grad_window_ref[rows, 128 * t : 128 * t + 128] = grad_query.astype(BF16)
            grad_window_ref[rows, C + 128 * t : C + 128 * t + 128] = grad_key.astype(BF16)
            grad_window_ref[rows, 2 * C + 128 * t : 2 * C + 128 * t + 128] = grad_value.astype(BF16)
        return carry

    lax.fori_loop(0, WH, window, 0)
    grad_projected = nn(to_natural_ref[...], grad_window_ref[...])
    g_bqkv_ref[...] += jnp.sum(grad_projected, 0, keepdims=True)
    grad_projected = grad_projected.astype(BF16)
    normal, inverse = norm_of(stream_ref[0])
    first = (normal * gain_ref[...] + shift_ref[...]).astype(BF16)
    g_qkv_ref[...] += tn(grad_projected, first)
    grad_norm, g_gain, g_shift = norm_back(nn(grad_projected, w_qkv_ref[...]), normal, inverse, gain_ref[...])
    g_gain_ref[...] += g_gain
    g_shift_ref[...] += g_shift
    grad_stream = (grad_middle_ref[0] + grad_norm).astype(BF16)

    load_merged(core, section_ref, incoming_ref, split_ref[...], parts_ref)
    center, merge_inverse = merge_norm(parts_ref)
    mean_one = 0.0
    mean_two = 0.0
    grads = []
    for f in range(4):
        part = (parts_ref[f] - center) * merge_inverse
        parts_ref[f] = part
        gain = red_gain_ref[f : f + 1]
        normed = (part * gain + red_shift_ref[f : f + 1]).astype(BF16)
        g_red_ref[f] += tn(grad_stream, normed)
        grad = nn(grad_stream, w_red_ref[f])
        g_rgain_ref[f : f + 1] += jnp.sum(grad * part, 0, keepdims=True)
        g_rshift_ref[f : f + 1] += jnp.sum(grad, 0, keepdims=True)
        grad = grad * gain
        mean_one = mean_one + jnp.sum(grad, -1, keepdims=True)
        mean_two = mean_two + jnp.sum(grad * part, -1, keepdims=True)
        grads.append(grad)
    mean_one = mean_one * (1.0 / (4 * C2))
    mean_two = mean_two * (1.0 / (4 * C2))
    for f in range(4):
        parts_ref[f] = merge_inverse * (grads[f] - mean_one - parts_ref[f] * mean_two)
    join = join_ref[...]
    for r in range(14):
        at = slice((r // 2) * 56, (r // 2) * 56 + 56)
        apart = jnp.concatenate([parts_ref[r % 2, at, :], parts_ref[2 + r % 2, at, :]], axis=0).astype(BF16)
        row = nn(join, apart).astype(BF16)

        @pl.when(core == r // 7)
        def _():
            own_ref[0, r % 7] = row

        @pl.when(core != r // 7)
        def _():
            send_ref[0, r % 7] = row


def whole(shape):
    return pl.BlockSpec(shape, lambda m: (0,) * len(shape))


def each(shape):
    return pl.BlockSpec((1,) + shape, lambda m: (m,) + (0,) * len(shape))


SCALARS = pl.BlockSpec(memory_space=pltpu.SMEM)


def run_kernel(kernel, ins, outs, scratch):
    return pl.pallas_call(
        kernel,
        grid=(MB,),
        in_specs=[spec for _, spec in ins],
        out_specs=[spec for _, _, spec in outs],
        out_shape=[jax.ShapeDtypeStruct(shape, dtype) for shape, dtype, _ in outs],
        scratch_shapes=scratch,
        compiler_params=pltpu.CompilerParams(vmem_limit_bytes=VMEM_BYTES),
    )(*[array for array, _ in ins])


def fixed(array):
    return (array, whole(array.shape))


def stepped(array):
    return (array, each(array.shape[1:]))


def gather_weight(shard):
    rows = lax.all_gather(shard.T, "sp", axis=0, tiled=True)
    return lax.all_gather(rows, "dp", axis=1, tiled=True)


def scatter_grad(grad):
    share = lax.psum_scatter(grad.astype(BF16), "sp", scatter_dimension=0, tiled=True)
    share = lax.psum_scatter(share, "dp", scatter_dimension=1, tiled=True)
    return share.astype(F32).T


ROWS_ONE = 64
ROWS_TWO = 112
SMALL = 8832
SMALL_ROWS = SMALL // C
BOTH_ROWS = 2 * SMALL_ROWS


def beside(upper, lower):
    return jnp.concatenate([upper, lower], axis=1)


def pad_rows(rows, count):
    return jnp.concatenate([rows, jnp.zeros((count - rows.shape[0], rows.shape[1]), F32)], axis=0)


def turned(ref):
    count = ref.shape[1]
    one = lax.broadcasted_iota(jnp.int32, (count, count), 0) == lax.broadcasted_iota(jnp.int32, (count, count), 1)
    return nt(jnp.where(one, 1.0, 0.0).astype(BF16), ref[...])


def pack_kernel(red_ref, qkv_ref, proj_ref, fc1_ref, fc2_ref, one_ref, two_ref):
    qkv = turned(qkv_ref)
    one = [turned(red_ref), beside(qkv[:40], pad_rows(qkv[40:], 40))]
    one_ref[...] = jnp.concatenate(one, axis=0).astype(BF16)
    proj, fc1, fc2 = turned(proj_ref), turned(fc1_ref), turned(fc2_ref)
    two = [beside(proj[:16], pad_rows(proj[16:], 16)), beside(fc1[:48], fc1[48:]), fc2[:, :C], fc2[:, C:]]
    two_ref[...] = jnp.concatenate(two, axis=0).astype(BF16)


def pack_weights(*weights):
    return pl.pallas_call(
        pack_kernel,
        out_shape=[
            jax.ShapeDtypeStruct((ROWS_ONE, C), BF16),
            jax.ShapeDtypeStruct((ROWS_TWO, C), BF16),
        ],
    )(*weights)


def place(place_ref):
    spot = place_ref[0]
    return place_ref[1], spot // 4, spot // 2 % 2, spot % 2


def each_block(place_ref):
    x, z, y, core = place(place_ref)
    for dc in range(2):
        for dy in range(2):
            for dz in range(4):
                yield dc, dz, dy, ((z ^ dz) * 2 + (y ^ dy)) * 2 + (core ^ dc)


def spots(block, count):
    return pl.ds(pl.multiple_of(block * count, 8), count)


def two_halves(refs, first, dc, dz, dy):
    near = refs[4 * dc + 2 * dy][dz].astype(F32)
    far = refs[4 * dc + 2 * dy + 1][dz].astype(F32)
    return jnp.where(first, near, far), jnp.where(first, far, near)


def unpack_one_kernel(place_ref, *refs):
    ins, (red_ref, qkv_ref, red_f32, qkv_f32) = refs[:8], refs[8:]
    first = place_ref[1] == 0
    for dc, dz, dy, block in each_block(place_ref):
        halves = two_halves(ins, first, dc, dz, dy)
        for d in range(2):
            red_f32[2 * d, spots(block, 24), :] = halves[d][:24, :C2]
            red_f32[2 * d + 1, spots(block, 24), :] = halves[d][:24, C2:]
        rows = pl.multiple_of(block * 72, 8)
        qkv_f32[pl.ds(rows, 40), :] = beside(halves[0][24:, :C2], halves[1][24:, :C2])
        qkv_f32[pl.ds(rows + 40, 32), :] = beside(halves[0][24:56, C2:], halves[1][24:56, C2:])
    red_ref[...] = red_f32[...].astype(BF16)
    qkv_ref[...] = qkv_f32[...].astype(BF16)


def unpack_two_kernel(place_ref, *refs):
    ins, (proj_ref, fc1_ref, fc2_ref, proj_f32, fc1_f32, fc2_f32) = refs[:8], refs[8:]
    first = place_ref[1] == 0
    for dc, dz, dy, block in each_block(place_ref):
        halves = two_halves(ins, first, dc, dz, dy)
        a, b = halves
        rows = pl.multiple_of(block * 24, 8)
        proj_f32[pl.ds(rows, 16), :] = beside(a[:16, :C2], b[:16, :C2])
        proj_f32[pl.ds(rows + 16, 8), :] = beside(a[:8, C2:], b[:8, C2:])
        units = pl.multiple_of(block * 96, 8)
        fc1_f32[pl.ds(units, 48), :] = beside(a[16:64, :C2], b[16:64, :C2])
        fc1_f32[pl.ds(units + 48, 48), :] = beside(a[16:64, C2:], b[16:64, C2:])
        for d in range(2):
            fc2_f32[pl.ds(rows, 24), 2 * d * C : 2 * d * C + C] = halves[d][64:88]
            fc2_f32[pl.ds(rows, 24), 2 * d * C + C : 2 * d * C + 2 * C] = halves[d][88:]
    proj_ref[...] = proj_f32[...].astype(BF16)
    fc1_ref[...] = fc1_f32[...].astype(BF16)
    fc2_ref[...] = fc2_f32[...].astype(BF16)


def local_call(kernel, place_arr, ins, outs, scratch=()):
    return pl.pallas_call(
        kernel,
        in_specs=[SCALARS] + [pl.BlockSpec(memory_space=pltpu.VMEM)] * len(ins),
        out_specs=[pl.BlockSpec(memory_space=pltpu.VMEM)] * len(outs),
        out_shape=[jax.ShapeDtypeStruct(shape, dtype) for shape, dtype in outs],
        scratch_shapes=scratch,
        compiler_params=pltpu.CompilerParams(vmem_limit_bytes=VMEM_BYTES),
    )(place_arr, *ins)


def move(block, dz, dy, dx, dc):
    route = []
    for x in range(2):
        for spot in range(16):
            other = spot ^ (dz * 4 + dy * 2 + dc)
            route.append((spot * 2 + x, other * 2 + (x ^ dx)))
    return lax.ppermute(block, ("sp", "dp"), route)


PLANE = [(0, 0), (0, 1), (1, 0), (1, 1)]


def spread_pack(pack):
    column = jnp.stack([pack] + [move(pack, dz, 0, 0, 0) for dz in range(1, 4)])
    mine = [column] + [move(column, 0, dy, dx, 0) for dy, dx in PLANE[1:]]
    return mine + [move(part, 0, 0, 0, 1) for part in mine]


def pack_one_grads_kernel(place_ref, red_ref, qkv_ref, mine_ref, theirs_ref):
    first = place_ref[1] == 0
    for dc, dz, dy, block in each_block(place_ref):
        rows = pl.multiple_of(block * 72, 8)
        top, low = qkv_ref[pl.ds(rows, 40), :], pad_rows(qkv_ref[pl.ds(rows + 40, 32), :], 40)
        halves = []
        for d in range(2):
            red = beside(red_ref[2 * d, spots(block, 24), :], red_ref[2 * d + 1, spots(block, 24), :])
            lanes = slice(d * C2, d * C2 + C2)
            halves.append(jnp.concatenate([red, beside(top[:, lanes], low[:, lanes])], axis=0))
        out_ref = theirs_ref if dc else mine_ref
        out_ref[2 * dy, dz] = jnp.where(first, halves[0], halves[1]).astype(BF16)
        out_ref[2 * dy + 1, dz] = jnp.where(first, halves[1], halves[0]).astype(BF16)


def pack_two_grads_kernel(place_ref, proj_ref, fc1_ref, fc2_ref, mine_ref, theirs_ref):
    first = place_ref[1] == 0
    for dc, dz, dy, block in each_block(place_ref):
        rows = pl.multiple_of(block * 24, 8)
        units = pl.multiple_of(block * 96, 8)
        proj_top, proj_low = proj_ref[pl.ds(rows, 16), :], pad_rows(proj_ref[pl.ds(rows + 16, 8), :], 16)
        fc1_top, fc1_low = fc1_ref[pl.ds(units, 48), :], fc1_ref[pl.ds(units + 48, 48), :]
        halves = []
        for d in range(2):
            lanes = slice(d * C2, d * C2 + C2)
            halves.append(
                jnp.concatenate(
                    [
                        beside(proj_top[:, lanes], proj_low[:, lanes]),
                        beside(fc1_top[:, lanes], fc1_low[:, lanes]),
                        fc2_ref[pl.ds(rows, 24), 2 * d * C : 2 * d * C + C],
                        fc2_ref[pl.ds(rows, 24), 2 * d * C + C : 2 * d * C + 2 * C],
                    ],
                    axis=0,
                )
            )
        out_ref = theirs_ref if dc else mine_ref
        out_ref[2 * dy, dz] = jnp.where(first, halves[0], halves[1]).astype(BF16)
        out_ref[2 * dy + 1, dz] = jnp.where(first, halves[1], halves[0]).astype(BF16)


def collect(mine, theirs):
    other = move(theirs, 0, 0, 0, 1)
    sums = [(mine[k].astype(F32) + other[k].astype(F32)).astype(BF16) for k in range(4)]
    total = sums[0].astype(F32)
    for k in range(1, 4):
        dy, dx = PLANE[k]
        total = total + move(sums[k], 0, dy, dx, 0).astype(F32)
    last = total[0]
    for dz in range(1, 4):
        last = last + move(total[dz].astype(BF16), dz, 0, 0, 0).astype(F32)
    return last


def shares_one_kernel(sum_ref, red_ref, qkv_ref):
    rows = sum_ref[...]
    red_ref[...] = rows[:24].T
    qkv_ref[...] = jnp.concatenate([rows[24:, :C2], rows[24:56, C2:]], axis=0).T


def shares_two_kernel(sum_ref, proj_ref, fc1_ref, fc2_ref):
    rows = sum_ref[...]
    proj_ref[...] = jnp.concatenate([rows[:16, :C2], rows[:8, C2:]], axis=0).T
    fc1_ref[...] = jnp.concatenate([rows[16:64, :C2], rows[16:64, C2:]], axis=0).T
    fc2_ref[...] = jnp.concatenate([rows[64:88], rows[88:]], axis=1).T


def shares(kernel, total, outs):
    return pl.pallas_call(kernel, out_shape=[jax.ShapeDtypeStruct(shape, F32) for shape in outs])(total)


def from_core(block):
    count = lax.axis_size("sp")
    return lax.ppermute(block, "sp", [(i, i ^ 1) for i in range(count)])


def shards(
    section_two, widths, red_gain, red_shift, w_red, norm1_gain, norm1_shift, w_qkv, b_qkv,
    bias_table, w_proj, b_proj, norm2_gain, norm2_shift, w_fc1, b_fc1, w_fc2, b_fc2, cotangent,
):
    const = constants()
    core = lax.axis_index("sp") % 2
    core_arr = core.astype(jnp.int32).reshape(1)
    width_arr = widths.reshape(MB)
    section = section_two.reshape(MB, 7, 4 * 7 * WH, C2)
    zero = jnp.int32(0)
    outgoing = lax.dynamic_slice(section, (zero, zero, (1 - core) * 112, zero), (MB, 7, 112, C2))
    incoming = from_core(outgoing)
    row = lambda v: v.reshape(1, -1)

    direct = lax.axis_size("sp") == 16 and lax.axis_size("dp") == 2
    place_arr = jnp.stack([lax.axis_index("sp"), lax.axis_index("dp")]).astype(jnp.int32)
    if direct:
        pack_one, pack_two = pack_weights(w_red, w_qkv, w_proj, w_fc1, w_fc2)
        wt_red, wt_qkv = local_call(
            unpack_one_kernel,
            place_arr,
            spread_pack(pack_one),
            [((4, C, C2), BF16), ((3 * C, C), BF16)],
            [pltpu.VMEM((4, C, C2), F32), pltpu.VMEM((3 * C, C), F32)],
        )
        wt_proj, wt_fc1, wt_fc2 = local_call(
            unpack_two_kernel,
            place_arr,
            spread_pack(pack_two),
            [((C, C), BF16), ((FF, C), BF16), ((C, FF), BF16)],
            [pltpu.VMEM((C, C), F32), pltpu.VMEM((FF, C), F32), pltpu.VMEM((C, FF), F32)],
        )
    else:
        wt_red = gather_weight(w_red).reshape(C, 4, C2).transpose(1, 0, 2)
        wt_qkv, wt_proj, wt_fc1, wt_fc2 = (gather_weight(w) for w in (w_qkv, w_proj, w_fc1, w_fc2))
    bias = spread_bias(bias_table)
    scalar = lambda a: (a, SCALARS)

    stream, qkv, soft, attended = run_kernel(
        forward_kernel,
        [
            scalar(core_arr), scalar(width_arr), stepped(section), stepped(incoming),
            fixed(red_gain.reshape(4, C2)), fixed(red_shift.reshape(4, C2)), fixed(wt_red),
            fixed(row(norm1_gain)), fixed(row(norm1_shift)), fixed(wt_qkv), fixed(row(b_qkv)),
            fixed(bias), fixed(const["to_window"]), fixed(const["to_natural"]), fixed(const["split"]),
            fixed(const["head_mask"]), fixed(const["group_ones"]), fixed(const["key_col"]),
        ],
        [
            ((MB, TOK, C), F32, each((TOK, C))),
            ((MB, WROWS, 3 * C), BF16, each((WROWS, 3 * C))),
            ((MB, WH, 3, SLOT, 256), BF16, each((WH, 3, SLOT, 256))),
            ((MB, TOK, C), BF16, each((TOK, C))),
        ],
        [pltpu.VMEM((4, TOK, C2), F32), pltpu.VMEM((WROWS, C), BF16)],
    )

    small = lambda n: ((1, n), F32, whole((1, n)))
    (
        output, grad_middle, grad_att, g_proj, g_fc1, g_fc2, g_bproj, g_n2g, g_n2b, g_bfc1, g_bfc2,
    ) = run_kernel(
        feed_kernel,
        [
            scalar(core_arr), scalar(width_arr), stepped(stream), stepped(attended),
            stepped(cotangent.reshape(MB, TOK, C)), fixed(const["nat_col"]),
            fixed(wt_proj), fixed(row(b_proj)), fixed(row(norm2_gain)), fixed(row(norm2_shift)),
            fixed(wt_fc1), fixed(row(b_fc1)), fixed(wt_fc2), fixed(row(b_fc2)),
        ],
        [
            ((MB, TOK, C), F32, each((TOK, C))),
            ((MB, TOK, C), F32, each((TOK, C))),
            ((MB, TOK, C), BF16, each((TOK, C))),
            ((C, C), F32, whole((C, C))),
            ((FF, C), F32, whole((FF, C))),
            ((C, FF), F32, whole((C, FF))),
            small(C), small(C), small(C), small(FF), small(C),
        ],
        [pltpu.VMEM((TOK, C), BF16), pltpu.VMEM((TOK, C), BF16), pltpu.VMEM((TOK, C), F32)],
    )

    (
        grad_own, grad_send, g_red, g_qkv, g_pairs, g_rgain, g_rshift, g_n1g, g_n1b, g_bqkv,
    ) = run_kernel(
        backward_kernel,
        [
            scalar(core_arr), stepped(section), stepped(incoming),
            fixed(red_gain.reshape(4, C2)), fixed(red_shift.reshape(4, C2)), fixed(wt_red),
            fixed(row(norm1_gain)), fixed(row(norm1_shift)), fixed(wt_qkv),
            fixed(const["to_window"]), fixed(const["to_natural"]), fixed(const["split"]), fixed(const["join"]),
            fixed(const["head_mask"]), fixed(const["group_ones"]),
            stepped(stream), stepped(qkv), stepped(soft), stepped(grad_middle), stepped(grad_att),
        ],
        [
            ((MB, 7, 112, C2), BF16, each((7, 112, C2))),
            ((MB, 7, 112, C2), BF16, each((7, 112, C2))),
            ((4, C, C2), F32, whole((4, C, C2))),
            ((3 * C, C), F32, whole((3 * C, C))),
            ((3, SLOT, 256), F32, whole((3, SLOT, 256))),
            ((4, C2), F32, whole((4, C2))),
            ((4, C2), F32, whole((4, C2))),
            small(C), small(C), small(3 * C),
        ],
        [
            pltpu.VMEM((4, TOK, C2), F32),
            pltpu.VMEM((WROWS, C), BF16),
            pltpu.VMEM((WROWS, 3 * C), BF16),
        ],
    )

    grad_back = from_core(grad_send)
    is_left = core == 0
    grad_input = jnp.where(
        is_left,
        jnp.concatenate([grad_own, grad_back], axis=2),
        jnp.concatenate([grad_back, grad_own], axis=2),
    )
    if direct:
        packed = [((4, 4, ROWS_TWO, C), BF16)] * 2
        mine, theirs = local_call(pack_two_grads_kernel, place_arr, [g_proj, g_fc1, g_fc2], packed)
        s_proj, s_fc1, s_fc2 = shares(
            shares_two_kernel, collect(mine, theirs), [w_proj.shape, w_fc1.shape, w_fc2.shape]
        )
        packed = [((4, 4, ROWS_ONE, C), BF16)] * 2
        mine, theirs = local_call(pack_one_grads_kernel, place_arr, [g_red, g_qkv], packed)
        s_red, s_qkv = shares(shares_one_kernel, collect(mine, theirs), [w_red.shape, w_qkv.shape])
    else:
        s_red = scatter_grad(g_red.transpose(1, 0, 2).reshape(C, 4 * C2))
        s_qkv, s_proj, s_fc1, s_fc2 = (scatter_grad(g) for g in (g_qkv, g_proj, g_fc1, g_fc2))
    g_table = gather_table(g_pairs)
    smalls = lax.psum(
        (g_rgain, g_rshift, g_n1g, g_n1b, g_bqkv, g_table, g_bproj, g_n2g, g_n2b, g_bfc1, g_bfc2),
        ("sp", "dp"),
    )
    flat = [v.reshape(-1) for v in smalls]
    return (
        output.reshape(MB, 1, 1, 7, 7 * WH, C),
        grad_input.reshape(MB, 1, 7, 4 * 7 * WH, C2),
        flat[0], flat[1], s_red, flat[2], flat[3], s_qkv, flat[4], smalls[5], s_proj, flat[6],
        flat[7], flat[8], s_fc1, flat[9], s_fc2, flat[10],
    )


def solution(mesh):
    weight = P("dp", "sp")
    placed = (
        P(None, "dp", "sp", None, None), P(None, "dp"), P(), P(), weight, P(), P(), weight, P(), P(),
        weight, P(), P(), P(), weight, P(), weight, P(), P(None, "dp", "sp", None, None, None),
    )
    out_specs = (
        P(None, "dp", "sp", None, None, None), P(None, "dp", "sp", None, None), P(), P(), weight,
        P(), P(), weight, P(), P(), weight, P(), P(), P(), weight, P(), weight, P(),
    )
    return jax.shard_map(shards, mesh=mesh, in_specs=placed, out_specs=out_specs, check_vma=False)
```

```python
import jax
import jax.numpy as jnp
import numpy as np
from jax import lax
from jax.experimental import pallas as pl
from jax.experimental.pallas import tpu as pltpu
from jax.sharding import PartitionSpec as P

C2 = 192
C = 384
HEADS = 12
HD = 32
FF = 1536
MB = 3
WH = 8
TOK = 7 * 7 * WH
SLOT = 64
WROWS = WH * SLOT
W2 = 4 * 7 * WH
CHUNK = 1536
EPSILON = 1e-05
DEAD = -1e30
HIGHEST = lax.Precision.HIGHEST
F32 = jnp.float32
BF16 = jnp.bfloat16
UNROLL = 4
COST_NORM, COST_FORWARD, COST_FEED, COST_ATTENTION, COST_REDUCTION, COST_MERGE = 5, 16, 24, 13, 11, 7
MIB = 1024 * 1024
VMEM_NORM, VMEM_FORWARD, VMEM_FEED, VMEM_ATTENTION, VMEM_REDUCTION, VMEM_MERGE, VMEM_SUM = 8, 20, 28, 8, 10, 10, 10

ROWS_ONE = 64
ROWS_TWO = 112
SMALL_ONE = 24
SMALL_TWO = 8
PLANE = [(0, 0), (0, 1), (1, 0), (1, 1)]


def nn(left, right):
    return lax.dot_general(left, right, (((1,), (0,)), ((), ())), preferred_element_type=F32)


def nt(left, right):
    return lax.dot_general(left, right, (((1,), (1,)), ((), ())), preferred_element_type=F32)


def tn(left, right):
    return lax.dot_general(left, right, (((0,), (0,)), ((), ())), preferred_element_type=F32)


def constants():
    to_window = np.zeros((WROWS, TOK), np.float32)
    for w in range(WH):
        for r in range(7):
            for c in range(7):
                to_window[w * SLOT + 7 * r + c, r * 56 + 7 * w + c] = 1
    split = np.zeros((2, 112, W2), np.float32)
    for core in range(2):
        for j in range(56):
            split[core, j, core * 112 + 2 * j] = 1
            split[core, 56 + j, core * 112 + 2 * j + 1] = 1
    head_mask = (np.arange(256)[:, None] // SLOT == np.arange(128)[None] // HD).astype(np.float32)
    regroup = np.zeros((SLOT, SLOT), np.float32)
    ungroup = np.zeros((SLOT, SLOT), np.float32)
    reach = np.zeros((256, 1024), np.float32)
    for p in range(49):
        regroup[p // 7 * 8 + 7 - p % 7, p] = 1
        ungroup[p, p // 7 * 8 + p % 7] = 1
        for h in range(4):
            reach[h * SLOT + p, h * 256 + 84 + 13 * (p // 7) + p % 7] = 1
    low = lambda a: jnp.asarray(a, BF16)
    return dict(
        to_window=low(to_window),
        to_natural=low(to_window.T),
        split=low(split),
        head_mask=low(head_mask),
        regroup=low(regroup),
        ungroup=low(ungroup),
        reach=low(reach),
    )


def column_of(shape, width, factor, shift):
    at = lax.broadcasted_iota(jnp.int32, shape, 0)
    return at - width * ((at * factor) >> shift)


def key_column(shape):
    return jnp.where(lax.broadcasted_iota(jnp.int32, shape, 0) < 49, column_of(shape, 7, 37, 8), 1 << 20)


def row(ref):
    return ref[...].reshape(1, -1)


def norm_of(values):
    center = jnp.mean(values, -1, keepdims=True)
    shifted = values - center
    inverse = lax.rsqrt(jnp.mean(shifted * shifted, -1, keepdims=True) + EPSILON)
    return shifted * inverse, inverse


def norm_back(grad_out, normal, inverse, gain):
    grad_normal = grad_out * gain
    grad_in = inverse * (
        grad_normal
        - jnp.mean(grad_normal, -1, keepdims=True)
        - normal * jnp.mean(grad_normal * normal, -1, keepdims=True)
    )
    return (
        grad_in,
        jnp.sum(grad_out * normal, 0, keepdims=True),
        jnp.sum(grad_out, 0, keepdims=True),
    )


def four_heads(rows, head_mask):
    return jnp.concatenate([rows] * 4, axis=0) * head_mask


def own_blocks(full):
    return [full[HD * h : HD * h + HD, SLOT * h : SLOT * h + SLOT] for h in range(4)]


def beside(upper, lower):
    return jnp.concatenate([upper, lower], axis=1)


def pad_rows(rows, count):
    return jnp.concatenate([rows, jnp.zeros((count - rows.shape[0], rows.shape[1]), F32)], axis=0)


def pack_kernel(red_ref, qkv_ref, proj_ref, fc1_ref, fc2_ref, one_ref, two_ref):
    qkv = qkv_ref[...].astype(F32)
    one = [red_ref[...].astype(F32), beside(qkv[:40], pad_rows(qkv[40:], 40))]
    one_ref[...] = jnp.concatenate(one, axis=0).astype(BF16)
    proj, fc2 = proj_ref[...].astype(F32), fc2_ref[...].astype(F32)
    count = fc1_ref.shape[1]
    same = lax.broadcasted_iota(jnp.int32, (count, count), 0) == lax.broadcasted_iota(jnp.int32, (count, count), 1)
    fc1 = nt(jnp.where(same, 1.0, 0.0).astype(BF16), fc1_ref[...])
    two = [beside(proj[:16], pad_rows(proj[16:], 16)), beside(fc1[:48], fc1[48:]), fc2[:, :C], fc2[:, C:]]
    two_ref[...] = jnp.concatenate(two, axis=0).astype(BF16)


def pack_weights(w_red, w_qkv, w_proj, w_fc1, w_fc2):
    return pl.pallas_call(
        pack_kernel,
        out_shape=[jax.ShapeDtypeStruct((ROWS_ONE, C), BF16), jax.ShapeDtypeStruct((ROWS_TWO, C), BF16)],
    )(w_red.T, w_qkv.T, w_proj.T, w_fc1, w_fc2.T)


def each_block(place_ref):
    spot = place_ref[0]
    z, y, core = spot // 4, spot // 2 % 2, spot % 2
    for dc in range(2):
        for dy in range(2):
            for dz in range(4):
                yield dc, dz, dy, ((z ^ dz) * 2 + (y ^ dy)) * 2 + (core ^ dc)


def spots(block, stride, first, count):
    return pl.ds(pl.multiple_of(block * stride + first, 8), count)


def two_halves(refs, first, dc, dz, dy):
    near = refs[4 * dc + 2 * dy][dz].astype(F32)
    far = refs[4 * dc + 2 * dy + 1][dz].astype(F32)
    return jnp.where(first, near, far), jnp.where(first, far, near)


def unpack_one(place_ref, packs, red_ref, qkv_ref, red_f32, qkv_f32):
    first = place_ref[1] == 0
    for dc, dz, dy, block in each_block(place_ref):
        a, b = two_halves(packs, first, dc, dz, dy)
        red_f32[0, spots(block, 24, 0, 24), :] = a[:24]
        red_f32[1, spots(block, 24, 0, 24), :] = b[:24]
        qkv_f32[spots(block, 72, 0, 40), :] = beside(a[24:, :C2], b[24:, :C2])
        qkv_f32[spots(block, 72, 40, 32), :] = beside(a[24:56, C2:], b[24:56, C2:])
    red_ref[...] = red_f32[...].astype(BF16)
    qkv_ref[...] = qkv_f32[...].astype(BF16)


def unpack_two(place_ref, packs, proj_ref, fc1_ref, fc2_ref, proj_f32, fc1_f32, fc2_f32):
    first = place_ref[1] == 0
    for dc, dz, dy, block in each_block(place_ref):
        a, b = two_halves(packs, first, dc, dz, dy)
        proj_f32[spots(block, 24, 0, 16), :] = beside(a[:16, :C2], b[:16, :C2])
        proj_f32[spots(block, 24, 16, 8), :] = beside(a[:8, C2:], b[:8, C2:])
        fc1_f32[spots(block, 96, 0, 48), :] = beside(a[16:64, :C2], b[16:64, :C2])
        fc1_f32[spots(block, 96, 48, 48), :] = beside(a[16:64, C2:], b[16:64, C2:])
        for d, half in enumerate((a, b)):
            fc2_f32[spots(block, 24, 0, 24), 2 * d * C : 2 * d * C + C] = half[64:88]
            fc2_f32[spots(block, 24, 0, 24), 2 * d * C + C : 2 * d * C + 2 * C] = half[88:]
    proj_ref[...] = proj_f32[...].astype(BF16)
    fc1_ref[...] = fc1_f32[...].astype(BF16)
    fc2_ref[...] = fc2_f32[...].astype(BF16)


def put_block(place_ref, dc, dz, dy, halves, mine_ref, theirs_ref):
    first = place_ref[1] == 0
    out_ref = theirs_ref if dc else mine_ref
    count = halves[0].shape[0]
    for dx in range(2):
        at = ((2 * dy + dx) * 4 + dz) * count
        out_ref[at : at + count, :] = jnp.where(first, halves[dx], halves[1 - dx]).astype(BF16)


def two_terms(values):
    high = values.astype(BF16)
    return jnp.concatenate([high.astype(F32), values - high.astype(F32)], axis=0).astype(BF16)


def pack_one_grads(place_ref, red_ref, qkv_ref, small, mine_ref, theirs_ref):
    for dc, dz, dy, block in each_block(place_ref):
        top, low = qkv_ref[spots(block, 72, 0, 40), :], pad_rows(qkv_ref[spots(block, 72, 40, 32), :], 40)
        halves = []
        for d in range(2):
            lanes = slice(d * C2, d * C2 + C2)
            red = red_ref[d, spots(block, 24, 0, 24), :]
            halves.append(jnp.concatenate([red, beside(top[:, lanes], low[:, lanes])], axis=0))
        put_block(place_ref, dc, dz, dy, halves, mine_ref, theirs_ref)
    theirs_ref[16 * ROWS_ONE :, :] = two_terms(small)


def pack_two_grads(place_ref, proj_ref, fc1_ref, fc2_ref, small, mine_ref, theirs_ref):
    for dc, dz, dy, block in each_block(place_ref):
        proj_top, proj_low = proj_ref[spots(block, 24, 0, 16), :], pad_rows(proj_ref[spots(block, 24, 16, 8), :], 16)
        fc1_top, fc1_low = fc1_ref[spots(block, 96, 0, 48), :], fc1_ref[spots(block, 96, 48, 48), :]
        fc2 = fc2_ref[spots(block, 24, 0, 24), :]
        halves = []
        for d in range(2):
            lanes = slice(d * C2, d * C2 + C2)
            parts = [beside(proj_top[:, lanes], proj_low[:, lanes]), beside(fc1_top[:, lanes], fc1_low[:, lanes])]
            parts += [fc2[:, 2 * d * C : 2 * d * C + C], fc2[:, 2 * d * C + C : 2 * d * C + 2 * C]]
            halves.append(jnp.concatenate(parts, axis=0))
        put_block(place_ref, dc, dz, dy, halves, mine_ref, theirs_ref)
    theirs_ref[16 * ROWS_TWO :, :] = two_terms(small)


def small_sum(small, refs, first, count):
    for ref in refs:
        small = small + (ref[first : first + count, :].astype(F32) + ref[first + count : first + 2 * count, :].astype(F32))
    return small


def core_sum_kernel(rows, count, mine_ref, other_ref, small_ref, own_ref, small_out_ref, *send_refs):
    small = small_sum(small_ref[...], [other_ref], 16 * rows, count)
    small_out_ref[...] = small
    for k in range(4):
        at = slice(4 * k * rows, 4 * k * rows + 4 * rows)
        total = mine_ref[at, :].astype(F32) + other_ref[at, :].astype(F32)
        if k == 0:
            own_ref[...] = total
        else:
            send_refs[k - 1][: 4 * rows, :] = total.astype(BF16)
            send_refs[k - 1][4 * rows :, :] = two_terms(small)


def plane_sum_kernel(rows, count, own_ref, small_ref, *refs):
    got, own_out_ref, small_out_ref, send_refs = refs[:3], refs[3], refs[4], refs[5:]
    small = small_sum(small_ref[...], got, 4 * rows, count)
    small_out_ref[...] = small
    for k in range(4):
        at = slice(k * rows, k * rows + rows)
        total = own_ref[at, :]
        for ref in got:
            total = total + ref[at, :].astype(F32)
        if k == 0:
            own_out_ref[...] = total
        else:
            send_refs[k - 1][:rows, :] = total.astype(BF16)
            send_refs[k - 1][rows:, :] = two_terms(small)


def line_sum(rows, count, own_ref, small_ref, got):
    total = own_ref[...]
    for ref in got:
        total = total + ref[:rows, :].astype(F32)
    return total, small_sum(small_ref[...], got, rows, count)


def finish_one_kernel(own_ref, small_ref, g1, g2, g3, red_ref, qkv_ref, rgain_ref, rshift_ref, gain_ref, shift_ref, bqkv_ref, table_ref):
    rows, small = line_sum(ROWS_ONE, SMALL_ONE, own_ref, small_ref, (g1, g2, g3))
    red_ref[...] = rows[:24]
    qkv_ref[...] = jnp.concatenate([rows[24:, :C2], rows[24:56, C2:]], axis=0)
    for at, ref in ((0, rgain_ref), (2, rshift_ref), (4, gain_ref), (5, shift_ref), (6, bqkv_ref)):
        for k in range(ref.shape[0] // C):
            ref[pl.ds(k * C, C)] = small[at + k]
    table_ref[...] = small[9 : 9 + HEADS, :169]


def finish_two_kernel(own_ref, small_ref, g1, g2, g3, near_ref, far_ref, grad_input_ref, proj_ref, fc1_ref, fc2_ref, bfc1_ref, bproj_ref, gain_ref, shift_ref, bfc2_ref):
    grad_input_ref[...] = near_ref[...] + far_ref[...]
    rows, small = line_sum(ROWS_TWO, SMALL_TWO, own_ref, small_ref, (g1, g2, g3))
    proj_ref[...] = jnp.concatenate([rows[:16, :C2], rows[:8, C2:]], axis=0)
    fc1_ref[...] = jnp.concatenate([rows[16:64, :C2], rows[16:64, C2:]], axis=0).T
    fc2_ref[...] = beside(rows[64:88], rows[88:])
    for at, ref in ((0, bfc1_ref), (4, bproj_ref), (5, gain_ref), (6, shift_ref), (7, bfc2_ref)):
        for k in range(ref.shape[0] // C):
            ref[pl.ds(k * C, C)] = small[at + k]


def merge_norm_kernel(
    place_ref, split_ref, section_ref, incoming_ref, gain_ref, shift_ref, normed_ref, normal_ref, inverse_ref, parts_ref,
):
    is_left = place_ref[0] % 2 == 0
    split = split_ref[place_ref[0] % 2]
    bands = []
    for r in range(14):
        own, other = section_ref[0, r % 7], incoming_ref[0, r % 7]
        bands.append(jnp.where(is_left, own, other) if r < 7 else jnp.where(is_left, other, own))
    for r in range(7):
        apart = nt(split, jnp.concatenate(bands[2 * r : 2 * r + 2], axis=0))
        parts_ref[0, r * 56 : r * 56 + 56, :] = apart[:56]
        parts_ref[1, r * 56 : r * 56 + 56, :] = apart[56:]
    total = jnp.sum(parts_ref[0] + parts_ref[1], -1, keepdims=True)
    shifted = [parts_ref[d] - total * (1.0 / (2 * C)) for d in range(2)]
    spread = jnp.sum(shifted[0] * shifted[0] + shifted[1] * shifted[1], -1, keepdims=True)
    inverse = lax.rsqrt(spread * (1.0 / (2 * C)) + EPSILON)
    inverse_ref[0] = inverse
    gain, shift = row(gain_ref), row(shift_ref)
    for d in range(2):
        normal = shifted[d] * inverse
        lanes = slice(d * C, d * C + C)
        normal_ref[0, d] = normal.astype(BF16)
        normed_ref[0, d] = (normal * gain[:, lanes] + shift[:, lanes]).astype(BF16)


def bias_kernel(table_ref, ungroup_ref, reach_ref, bias_ref, wide_ref):
    wide_ref[...] = jnp.zeros_like(wide_ref)
    wide_ref[:, :169] = table_ref[...]
    ungroup, reach = ungroup_ref[...], reach_ref[...]
    unused = jnp.where(lax.broadcasted_iota(jnp.int32, (SLOT, 256), 0) < 49, 0.0, DEAD)
    for t in range(3):
        heads = []
        for h in range(4):
            rows = jnp.broadcast_to(wide_ref[4 * t + h : 4 * t + h + 1, :], (8, 256))
            rows = pltpu.roll(rows, 0, axis=1, stride=1, stride_axis=0)
            blocks = [pltpu.roll(rows, 13 * r, axis=1) if r else rows for r in range(7)]
            heads.append(jnp.concatenate(blocks + [jnp.zeros((8, 256), F32)], axis=0))
        rest = jnp.concatenate(heads, axis=1)
        total = unused
        for _ in range(3):
            term = rest.astype(BF16)
            rest = rest - term.astype(F32)
            total = total + nt(nn(ungroup, term).astype(BF16), reach)
        bias_ref[t] = total


def stack_kernel(a_ref, b_ref, c_ref, d_ref, out_ref):
    for k, ref in enumerate((a_ref, b_ref, c_ref, d_ref)):
        out_ref[k] = ref[...]


def forward_kernel(direct, *refs):
    (
        place_ref, widths_ref, normed_ref, gain_ref, shift_ref,
        b_qkv_ref, bias_ref, to_window_ref, to_natural_ref, head_mask_ref,
    ) = refs[:10]
    cut = 18 if direct else 12
    packs, refs = refs[10:cut], refs[cut:]
    stream_ref, qkv_ref, soft_ref, attended_ref, w_red_ref, w_qkv_ref, turned_ref = refs[:7]
    step = pl.program_id(0)
    core = place_ref[0] % 2

    @pl.when(step == 0)
    def _():
        if direct:
            unpack_one(place_ref, packs, w_red_ref, w_qkv_ref, *refs[7:])
        else:
            w_red_ref[...] = packs[0][...]
            w_qkv_ref[...] = packs[1][...]

    stream = nt(normed_ref[0, 0], w_red_ref[0]) + nt(normed_ref[0, 1], w_red_ref[1])
    stream_ref[0] = stream
    normal, _ = norm_of(stream)
    first = (normal * row(gain_ref) + row(shift_ref)).astype(BF16)
    projected = nt(first, w_qkv_ref[...]) + row(b_qkv_ref)
    query = (projected[:, :C] * (HD**-0.5)).astype(BF16)
    rest = projected[:, C:].astype(BF16)
    to_window = to_window_ref[...]
    qkv_ref[0, :, :C] = nn(to_window, query).astype(BF16)
    qkv_ref[0, :, C:] = nn(to_window, rest).astype(BF16)
    width = widths_ref[step]
    key_col = key_column((SLOT, 128))

    def pair(i, carry):
        head_mask = head_mask_ref[...]
        outs = [[None, None] for _ in range(HEADS)]
        for j in range(2):
            w = 2 * i + j
            rows = pl.ds(pl.multiple_of(w * SLOT, SLOT), SLOT)
            live = jnp.where(key_col + (core * 56 + w * 7) < width, 0.0, DEAD)
            for t in range(3):
                q = qkv_ref[0, rows, 128 * t : 128 * t + 128]
                k = qkv_ref[0, rows, C + 128 * t : C + 128 * t + 128]
                v = qkv_ref[0, rows, 2 * C + 128 * t : 2 * C + 128 * t + 128]
                scores = nt(k, four_heads(q, head_mask)) + bias_ref[t]
                parts = []
                for half in range(2):
                    part = scores[:, 128 * half : 128 * half + 128] + live
                    exponent = jnp.exp(part - jnp.max(part, 0, keepdims=True))
                    share = 1.0 / jnp.sum(exponent, 0, keepdims=True)
                    parts.append((exponent * share).astype(BF16))
                soft = jnp.concatenate(parts, axis=1)
                soft_ref[0, w, t] = soft
                for h, block in enumerate(own_blocks(tn(v, soft))):
                    outs[4 * t + h][j] = block
        lanes = pl.ds(pl.multiple_of(i * 128, 128), 128)
        for h in range(HEADS):
            turned_ref[HD * h : HD * h + HD, lanes] = beside(*outs[h]).astype(BF16)
        return carry

    lax.fori_loop(0, WH // 2, pair, 0, unroll=UNROLL)
    attended_ref[0] = nt(to_natural_ref[...], turned_ref[...]).astype(BF16)


def feed_kernel(direct, *refs):
    (
        place_ref, widths_ref, stream_ref, attended_ref, cotangent_ref,
        b_proj_ref, gain_ref, shift_ref, b_fc1_ref, b_fc2_ref,
    ) = refs[:10]
    cut = 18 if direct else 13
    packs, refs = refs[10:cut], refs[cut:]
    output_ref, grad_middle_ref, grad_att_ref, small_ref = refs[:4]
    if direct:
        mine_ref, theirs_ref, g_proj_ref, g_fc1_ref, g_fc2_ref = refs[4:9]
        refs = refs[9:]
    else:
        g_proj_ref, g_fc1_ref, g_fc2_ref = refs[4:7]
        refs = refs[7:]
    second_ref, grad_feed_ref, grad_second_ref, bias_fc1_ref, g_bfc1_ref, w_proj_ref, w_fc1_ref, w_fc2_ref = refs[:8]
    step = pl.program_id(0)

    @pl.when(step == 0)
    def _():
        if direct:
            unpack_two(place_ref, packs, w_proj_ref, w_fc1_ref, w_fc2_ref, g_proj_ref, g_fc1_ref, g_fc2_ref)
        else:
            w_proj_ref[...] = packs[0][...]
            w_fc1_ref[...] = packs[1][...]
            w_fc2_ref[...] = packs[2][...]
        for ref in (g_proj_ref, g_fc1_ref, g_fc2_ref, small_ref, g_bfc1_ref):
            ref[...] = jnp.zeros_like(ref)
        bias_fc1_ref[...] = row(b_fc1_ref)

    keep = jnp.where(column_of((TOK, 1), 56, 1171, 16) + (place_ref[0] % 2) * 56 < widths_ref[step], 1.0, 0.0)
    attended = attended_ref[0]
    middle = stream_ref[0] + nt(attended, w_proj_ref[...]) + row(b_proj_ref)
    normal, inverse = norm_of(middle)
    gain = row(gain_ref)
    second_ref[...] = (normal * gain + row(shift_ref)).astype(BF16)
    grad_sum = cotangent_ref[0] * keep
    grad_feed = grad_sum.astype(BF16)
    grad_feed_ref[...] = grad_feed
    small_ref[7:8] += jnp.sum(grad_feed.astype(F32), 0, keepdims=True)
    output_ref[0] = middle + row(b_fc2_ref)
    grad_second_ref[...] = jnp.zeros_like(grad_second_ref)

    def hidden(j, carry):
        units = pl.ds(pl.multiple_of(j * CHUNK, CHUNK), CHUNK)
        w_fc1 = w_fc1_ref[units, :]
        w_fc2 = w_fc2_ref[:, units]
        second = second_ref[...]
        feed = grad_feed_ref[...]
        pre = nt(second, w_fc1) + bias_fc1_ref[:, units]
        cdf = 0.5 * (1.0 + lax.erf(pre * 0.7071067811865476))
        density = 0.3989422804014327 * jnp.exp(-0.5 * pre * pre)
        act = (pre * cdf).astype(BF16)
        output_ref[0] += nt(act, w_fc2)
        g_fc2_ref[:, units] += tn(feed, act)
        grad_pre = (nn(feed, w_fc2) * (cdf + pre * density)).astype(BF16)
        g_bfc1_ref[:, units] += jnp.sum(grad_pre.astype(F32), 0, keepdims=True)
        g_fc1_ref[units, :] += tn(grad_pre, second)
        grad_second_ref[...] += nn(grad_pre, w_fc1)
        return carry

    lax.fori_loop(0, FF // CHUNK, hidden, 0)
    output_ref[0] = output_ref[0] * keep
    grad_norm, g_gain, g_shift = norm_back(grad_second_ref[...], normal, inverse, gain)
    small_ref[5:6] += g_gain
    small_ref[6:7] += g_shift
    grad_middle = grad_sum + grad_norm
    grad_middle_ref[0] = grad_middle
    branch = grad_middle.astype(BF16)
    small_ref[4:5] += jnp.sum(branch.astype(F32), 0, keepdims=True)
    g_proj_ref[...] += tn(branch, attended)
    grad_att_ref[0] = nn(branch, w_proj_ref[...]).astype(BF16)

    @pl.when(step == MB - 1)
    def _():
        for k in range(4):
            small_ref[k : k + 1] = g_bfc1_ref[:, k * C : k * C + C]
        if direct:
            pack_two_grads(place_ref, g_proj_ref, g_fc1_ref, g_fc2_ref, small_ref[...], mine_ref, theirs_ref)


def table_rows(pairs_ref, regroup, reach):
    rows = []
    for t in range(3):
        sums = pairs_ref[t]
        high = sums.astype(BF16)
        low = (sums - high.astype(F32)).astype(BF16)
        spread = nn(nn(regroup, high).astype(BF16), reach) + nn(nn(regroup, low).astype(BF16), reach)
        for h in range(4):
            total = 0.0
            for r in range(7):
                part = spread[8 * r : 8 * r + 8, 256 * h : 256 * h + 256]
                total = total + (pltpu.roll(part, 256 - 13 * r, axis=1) if r else part)
            total = pltpu.roll(total, 249, axis=1, stride=1, stride_axis=0)
            rows.append(jnp.sum(total, 0, keepdims=True))
    rows = jnp.concatenate(rows, axis=0)
    return beside(rows, jnp.zeros((HEADS, C - 256), F32))


def attention_kernel(
    to_window_ref, to_natural_ref, head_mask_ref, regroup_ref, reach_ref, qkv_ref, soft_ref, grad_att_ref,
    grad_projected_ref, small_ref,
    window_ref, turned_ref, grad_window_ref, pairs_ref,
):
    step = pl.program_id(0)

    @pl.when(step == 0)
    def _():
        pairs_ref[...] = jnp.zeros_like(pairs_ref)
        small_ref[...] = jnp.zeros_like(small_ref)

    window_ref[...] = nn(to_window_ref[...], grad_att_ref[0]).astype(BF16)

    def pair(i, carry):
        head_mask = head_mask_ref[...]
        outs = [[None, None] for _ in range(HEADS)]
        for t in range(3):
            scores_sum = 0.0
            for j in range(2):
                w = 2 * i + j
                rows = pl.ds(pl.multiple_of(w * SLOT, SLOT), SLOT)
                q = qkv_ref[0, rows, 128 * t : 128 * t + 128]
                k = qkv_ref[0, rows, C + 128 * t : C + 128 * t + 128]
                v = qkv_ref[0, rows, 2 * C + 128 * t : 2 * C + 128 * t + 128]
                grad = four_heads(window_ref[rows, 128 * t : 128 * t + 128], head_mask)
                soft_low = soft_ref[0, w, t]
                soft = soft_low.astype(F32)
                grad_soft = nt(v, grad)
                inner = jnp.sum(grad_soft * soft, 0, keepdims=True)
                scores = (soft * (grad_soft - inner)).astype(BF16)
                scores_sum = scores_sum + scores.astype(F32)
                grad_key = nn(scores, four_heads(q, head_mask))
                grad_value = nn(soft_low, grad)
                grad_window_ref[rows, 128 * t : 128 * t + 128] = grad_key.astype(BF16)
                grad_window_ref[rows, C + 128 * t : C + 128 * t + 128] = grad_value.astype(BF16)
                for h, block in enumerate(own_blocks(tn(k, scores))):
                    outs[4 * t + h][j] = block
            pairs_ref[t] += scores_sum
        lanes = pl.ds(pl.multiple_of(i * 128, 128), 128)
        for h in range(HEADS):
            turned_ref[HD * h : HD * h + HD, lanes] = (beside(*outs[h]) * (HD**-0.5)).astype(BF16)
        return carry

    lax.fori_loop(0, WH // 2, pair, 0, unroll=UNROLL)
    to_natural = to_natural_ref[...]
    grad_query = nt(to_natural, turned_ref[...])
    grad_rest = nn(to_natural, grad_window_ref[...])
    grad_projected_ref[0, :, :C] = grad_query.astype(BF16)
    grad_projected_ref[0, :, C:] = grad_rest.astype(BF16)
    small_ref[0:1] += jnp.sum(grad_query, 0, keepdims=True)
    sums = jnp.sum(grad_rest, 0, keepdims=True)
    small_ref[1:2] += sums[:, :C]
    small_ref[2:3] += sums[:, C:]

    @pl.when(step == MB - 1)
    def _():
        small_ref[3 : 3 + HEADS] = table_rows(pairs_ref, regroup_ref[...], reach_ref[...])


def reduction_kernel(direct, *refs):
    (
        place_ref, red_gain_ref, red_shift_ref, w_red_ref, gain_ref, shift_ref, w_qkv_ref,
        stream_ref, grad_middle_ref, grad_projected_ref, normal_ref, small_in_ref,
    ) = refs[:12]
    refs = refs[12:]
    grad_stream_ref, small_ref = refs[:2]
    if direct:
        mine_ref, theirs_ref, g_red_ref, g_qkv_ref, sums_ref = refs[2:]
    else:
        g_red_ref, g_qkv_ref, sums_ref = refs[2:]
    step = pl.program_id(0)

    @pl.when(step == 0)
    def _():
        for ref in (g_red_ref, g_qkv_ref, sums_ref, small_ref):
            ref[...] = jnp.zeros_like(ref)

    grad_projected = grad_projected_ref[0]
    normal, inverse = norm_of(stream_ref[0])
    gain = row(gain_ref)
    first = (normal * gain + row(shift_ref)).astype(BF16)
    g_qkv_ref[...] += tn(grad_projected, first)
    grad_norm, g_gain, g_shift = norm_back(nn(grad_projected, w_qkv_ref[...]), normal, inverse, gain)
    small_ref[4:5] += g_gain
    small_ref[5:6] += g_shift
    grad_stream = (grad_middle_ref[0] + grad_norm).astype(BF16)
    grad_stream_ref[0] = grad_stream
    for d in range(2):
        g_red_ref[d] += tn(grad_stream, normal_ref[0, d])
    sums_ref[...] += tn(grad_stream, jnp.ones((TOK, 128), BF16))

    @pl.when(step == MB - 1)
    def _():
        red_gain, red_shift = row(red_gain_ref), row(red_shift_ref)
        column = sums_ref[:, :1]
        for d in range(2):
            lanes = slice(d * C, d * C + C)
            weight = w_red_ref[d].astype(F32)
            product = g_red_ref[d]
            small_ref[d : d + 1] = jnp.sum(weight * product, 0, keepdims=True)
            small_ref[2 + d : 3 + d] = jnp.sum(weight * column, 0, keepdims=True)
            g_red_ref[d] = product * red_gain[:, lanes] + column * red_shift[:, lanes]
        small_ref[6:21] = small_in_ref[:15]
        if direct:
            pack_one_grads(place_ref, g_red_ref, g_qkv_ref, small_ref[...], mine_ref, theirs_ref)


def merge_kernel(
    place_ref, red_gain_ref, w_red_ref, split_ref, grad_stream_ref, normal_ref, inverse_ref, own_ref, send_ref,
    parts_ref, rows_ref,
):
    core = place_ref[0] % 2
    red_gain = row(red_gain_ref)
    grad_stream = grad_stream_ref[0]
    grads = [nn(grad_stream, w_red_ref[d]) * red_gain[:, d * C : d * C + C] for d in range(2)]
    normals = [normal_ref[0, d].astype(F32) for d in range(2)]
    mean_one = jnp.sum(grads[0] + grads[1], -1, keepdims=True) * (1.0 / (2 * C))
    mean_two = jnp.sum(grads[0] * normals[0] + grads[1] * normals[1], -1, keepdims=True) * (1.0 / (2 * C))
    for d in range(2):
        parts_ref[d] = inverse_ref[0] * (grads[d] - mean_one - normals[d] * mean_two)
    join = split_ref[core]
    for r in range(7):
        at = slice(r * 56, r * 56 + 56)
        apart = jnp.concatenate([parts_ref[0, at, :], parts_ref[1, at, :]], axis=0).astype(BF16)
        rows = tn(apart, join).astype(BF16)
        rows_ref[2 * r], rows_ref[2 * r + 1] = rows[:C2], rows[C2:]
    is_left = core == 0
    for r in range(7):
        upper, lower = rows_ref[r], rows_ref[7 + r]
        own_ref[0, r] = jnp.where(is_left, upper, lower)
        send_ref[0, r] = jnp.where(is_left, lower, upper)


SCALARS = pl.BlockSpec(memory_space=pltpu.SMEM)


def whole(shape):
    return pl.BlockSpec(shape, lambda m: (0,) * len(shape), pipeline_mode=pl.Buffered(1))


def each(shape):
    return pl.BlockSpec((1,) + shape, lambda m: (m,) + (0,) * len(shape))


def scalar(array):
    return (array, SCALARS)


def fixed(array):
    return (array, whole(array.shape))


def stepped(array):
    return (array, each(array.shape[1:]))


def out_fixed(shape, dtype):
    return (shape, dtype, whole(shape))


def out_stepped(shape, dtype):
    return ((MB,) + shape, dtype, each(shape))


def run_kernel(kernel, ins, outs, scratch, micros, vmem):
    return pl.pallas_call(
        kernel,
        grid=(MB,),
        in_specs=[spec for _, spec in ins],
        out_specs=[spec for _, _, spec in outs],
        out_shape=[jax.ShapeDtypeStruct(shape, dtype) for shape, dtype, _ in outs],
        scratch_shapes=scratch,
        compiler_params=pltpu.CompilerParams(vmem_limit_bytes=vmem * MIB),
        cost_estimate=pl.CostEstimate(flops=int(micros * 1.15e9), bytes_accessed=0, transcendentals=0),
    )(*[array for array, _ in ins])


def whole_call(kernel, ins, outs):
    return pl.pallas_call(
        kernel,
        out_shape=[jax.ShapeDtypeStruct(shape, dtype) for shape, dtype in outs],
        compiler_params=pltpu.CompilerParams(vmem_limit_bytes=VMEM_SUM * MIB),
    )(*ins)


def merge_norm_call(const, place, section, incoming, gain, shift):
    return run_kernel(
        merge_norm_kernel,
        [scalar(place), fixed(const["split"]), stepped(section), stepped(incoming), fixed(gain), fixed(shift)],
        [out_stepped((2, TOK, C), BF16), out_stepped((2, TOK, C), BF16), out_stepped((TOK, 1), F32)],
        [pltpu.VMEM((2, TOK, C), F32)],
        COST_NORM,
        VMEM_NORM,
    )


def bias_call(const, table):
    return pl.pallas_call(
        bias_kernel,
        out_shape=jax.ShapeDtypeStruct((3, SLOT, 256), F32),
        scratch_shapes=[pltpu.VMEM((HEADS, 256), F32)],
        compiler_params=pltpu.CompilerParams(vmem_limit_bytes=VMEM_SUM * MIB),
    )(table, const["ungroup"], const["reach"])


def stack(blocks):
    return whole_call(stack_kernel, blocks, [((4,) + blocks[0].shape, BF16)])[0]


def forward_call(const, place, widths, normed, gain, shift, b_qkv, bias, weights):
    direct = len(weights) == 8
    return run_kernel(
        lambda *refs: forward_kernel(direct, *refs),
        [
            scalar(place), scalar(widths), stepped(normed), fixed(gain), fixed(shift), fixed(b_qkv), fixed(bias), fixed(const["to_window"]),
            fixed(const["to_natural"]), fixed(const["head_mask"]),
        ] + [fixed(w) for w in weights],
        [
            out_stepped((TOK, C), F32),
            out_stepped((WROWS, 3 * C), BF16),
            out_stepped((WH, 3, SLOT, 256), BF16),
            out_stepped((TOK, C), BF16),
            out_fixed((2, C, C), BF16),
            out_fixed((3 * C, C), BF16),
        ],
        [pltpu.VMEM((C, WROWS), BF16)]
        + ([pltpu.VMEM((2, C, C), F32), pltpu.VMEM((3 * C, C), F32)] if direct else []),
        COST_FORWARD,
        VMEM_FORWARD,
    )


def feed_call(place, widths, stream, attended, cotangent, b_proj, gain, shift, b_fc1, b_fc2, weights):
    direct = len(weights) == 8
    grads = [((C, C), F32), ((FF, C), F32), ((C, FF), F32)]
    packed = [((16 * ROWS_TWO, C), BF16), ((16 * ROWS_TWO + 2 * SMALL_TWO, C), BF16)]
    scratch = [
        pltpu.VMEM((TOK, C), BF16), pltpu.VMEM((TOK, C), BF16), pltpu.VMEM((TOK, C), F32),
        pltpu.VMEM((1, FF), F32), pltpu.VMEM((1, FF), F32),
        pltpu.VMEM((C, C), BF16), pltpu.VMEM((FF, C), BF16), pltpu.VMEM((C, FF), BF16),
    ]
    if direct:
        scratch = [pltpu.VMEM(*g) for g in grads] + scratch
    return run_kernel(
        lambda *refs: feed_kernel(direct, *refs),
        [
            scalar(place), scalar(widths), stepped(stream), stepped(attended), stepped(cotangent),
            fixed(b_proj), fixed(gain), fixed(shift), fixed(b_fc1), fixed(b_fc2),
        ] + [fixed(w) for w in weights],
        [
            out_stepped((TOK, C), F32),
            out_stepped((TOK, C), F32),
            out_stepped((TOK, C), BF16),
            out_fixed((SMALL_TWO, C), F32),
        ] + [out_fixed(*o) for o in (packed if direct else grads)],
        scratch,
        COST_FEED,
        VMEM_FEED,
    )


def attention_call(const, qkv, soft, grad_att):
    return run_kernel(
        attention_kernel,
        [fixed(const[n]) for n in ("to_window", "to_natural", "head_mask", "regroup", "reach")]
        + [stepped(qkv), stepped(soft), stepped(grad_att)],
        [out_stepped((TOK, 3 * C), BF16), out_fixed((16, C), F32)],
        [
            pltpu.VMEM((WROWS, C), BF16),
            pltpu.VMEM((C, WROWS), BF16),
            pltpu.VMEM((WROWS, 2 * C), BF16),
            pltpu.VMEM((3, SLOT, 256), F32),
        ],
        COST_ATTENTION,
        VMEM_ATTENTION,
    )


def reduction_call(direct, place, red_gain, red_shift, w_red, gain, shift, w_qkv, stream, grad_middle, grad_projected, normal, small):
    grads = [((2, C, C), F32), ((3 * C, C), F32)]
    packed = [((16 * ROWS_ONE, C), BF16), ((16 * ROWS_ONE + 2 * SMALL_ONE, C), BF16)]
    return run_kernel(
        lambda *refs: reduction_kernel(direct, *refs),
        [
            scalar(place), fixed(red_gain), fixed(red_shift), fixed(w_red), fixed(gain), fixed(shift), fixed(w_qkv),
            stepped(stream), stepped(grad_middle), stepped(grad_projected), stepped(normal), fixed(small),
        ],
        [out_stepped((TOK, C), BF16), out_fixed((SMALL_ONE, C), F32)]
        + [out_fixed(*o) for o in (packed if direct else grads)],
        ([pltpu.VMEM(*g) for g in grads] if direct else []) + [pltpu.VMEM((C, 128), F32)],
        COST_REDUCTION,
        VMEM_REDUCTION,
    )


def merge_call(const, place, red_gain, w_red, grad_stream, normal, inverse):
    return run_kernel(
        merge_kernel,
        [
            scalar(place), fixed(red_gain), fixed(w_red), fixed(const["split"]),
            stepped(grad_stream), stepped(normal), stepped(inverse),
        ],
        [out_stepped((7, C2, W2), BF16), out_stepped((7, C2, W2), BF16)],
        [pltpu.VMEM((2, TOK, C), F32), pltpu.VMEM((14, C2, W2), BF16)],
        COST_MERGE,
        VMEM_MERGE,
    )


def from_core(block):
    count = lax.axis_size("sp")
    return lax.ppermute(block, "sp", [(i, i ^ 1) for i in range(count)])


def move(block, dz, dy, dx, dc):
    route = []
    for spot in range(16):
        for x in range(2):
            other = spot ^ (dz * 4 + dy * 2 + dc)
            route.append((spot * 2 + x, other * 2 + (x ^ dx)))
    return lax.ppermute(block, ("sp", "dp"), route)


def line_spread(pack):
    return [pack] + [move(pack, dz, 0, 0, 0) for dz in range(1, 4)]


def plane_spread(column):
    return [column] + [move(column, 0, dy, dx, 0) for dy, dx in PLANE[1:]]


def core_spread(mine):
    return mine + [core_move(part) for part in mine]


def after(value, *others):
    return lax.optimization_barrier((value,) + others)[0]


def core_move(block):
    return move(block, 0, 0, 0, 1)


def core_sum(rows, count, mine, other, small):
    send = ((4 * rows + 2 * count, C), BF16)
    own, small, *sends = whole_call(
        lambda *refs: core_sum_kernel(rows, count, *refs),
        [mine, other, small],
        [((4 * rows, C), F32), ((count, C), F32), send, send, send],
    )
    return own, small, sends


def plane_moves(sends):
    return [move(s, 0, dy, dx, 0) for s, (dy, dx) in zip(sends, PLANE[1:])]


def plane_sum(rows, count, own, small, got):
    send = ((rows + 2 * count, C), BF16)
    own, small, *sends = whole_call(
        lambda *refs: plane_sum_kernel(rows, count, *refs),
        [own, small, *got],
        [((rows, C), F32), ((count, C), F32), send, send, send],
    )
    return own, small, sends


def line_moves(sends):
    return [move(s, dz, 0, 0, 0) for dz, s in zip(range(1, 4), sends)]


def gather_weight(shard):
    rows = lax.all_gather(shard.T, "sp", axis=0, tiled=True)
    return lax.all_gather(rows, "dp", axis=1, tiled=True)


def scatter_grad(grad):
    share = lax.psum_scatter(grad.astype(BF16), "sp", scatter_dimension=0, tiled=True)
    share = lax.psum_scatter(share, "dp", scatter_dimension=1, tiled=True)
    return share.astype(F32).T


def shards(
    section_two, widths, red_gain, red_shift, w_red, norm1_gain, norm1_shift, w_qkv, b_qkv,
    bias_table, w_proj, b_proj, norm2_gain, norm2_shift, w_fc1, b_fc1, w_fc2, b_fc2, cotangent,
):
    direct = lax.axis_size("sp") == 16 and lax.axis_size("dp") == 2
    const = constants()
    place = jnp.stack([lax.axis_index("sp"), lax.axis_index("dp")]).astype(jnp.int32)
    widths = widths.reshape(MB)
    section = section_two.reshape(MB, 7, W2, C2).transpose(0, 1, 3, 2)
    incoming = from_core(section)
    if direct:
        pack_one, pack_two = pack_weights(w_red, w_qkv, w_proj, w_fc1, w_fc2)
        line_one, line_two = line_spread(pack_one), line_spread(pack_two)
        column_one = stack(line_one)
        bias_table = after(bias_table, column_one)
        plane_one = plane_spread(column_one)
    normed, normal, inverse = merge_norm_call(const, place, section, incoming, red_gain, red_shift)
    bias = bias_call(const, bias_table.T)
    if direct:
        plane_one = [plane_one[0]] + [after(part, normed, bias, *line_two) for part in plane_one[1:]]
        weights_one = core_spread(plane_one)
        line_two = [after(part, *weights_one) for part in line_two]
        plane_two = plane_spread(stack(line_two))
    else:
        wt_red = gather_weight(w_red)
        weights_one = [jnp.stack([wt_red[:, :C], wt_red[:, C:]]), gather_weight(w_qkv)]
        weights_two = [gather_weight(w) for w in (w_proj, w_fc1, w_fc2)]
    stream, qkv, soft, attended, wt_red, wt_qkv = forward_call(
        const, place, widths, normed, norm1_gain, norm1_shift, b_qkv, bias, weights_one,
    )
    if direct:
        plane_two = [after(part, stream) for part in plane_two]
        weights_two = core_spread(plane_two)
    output, grad_middle, grad_att, small_two, *large_two = feed_call(
        place, widths, stream, attended, cotangent.reshape(MB, TOK, C), b_proj, norm2_gain, norm2_shift,
        b_fc1, b_fc2, weights_two,
    )
    if direct:
        mine, theirs = large_two
        own_two, small_two, sends = core_sum(ROWS_TWO, SMALL_TWO, mine, core_move(theirs), small_two)
        got_two = plane_moves(sends)
        grad_att = after(grad_att, own_two)
    grad_projected, small = attention_call(const, qkv, soft, grad_att)
    grad_stream, small_one, *large_one = reduction_call(
        direct, place, red_gain, red_shift, wt_red, norm1_gain, norm1_shift, wt_qkv, stream, grad_middle,
        grad_projected, normal, small,
    )
    if direct:
        mine, theirs = large_one
        got_two = [after(got, grad_stream) for got in got_two]
        other = core_move(after(theirs, *got_two))
        own_two, small_two, sends = plane_sum(ROWS_TWO, SMALL_TWO, own_two, small_two, got_two)
        got_two = line_moves(sends)
        other = after(other, own_two)
        own_one, small_one, sends = core_sum(ROWS_ONE, SMALL_ONE, mine, other, small_one)
        got_one = plane_moves(sends)
        grad_stream = after(grad_stream, own_one, *got_two)
    grad_own, grad_send = merge_call(const, place, red_gain, wt_red, grad_stream, normal, inverse)
    if direct:
        grad_send = after(grad_send, *got_one)
    grad_far = from_core(grad_send)
    output = output.reshape(MB, 1, 1, 7, 7 * WH, C)

    if direct:
        own_one, small_one, sends = plane_sum(ROWS_ONE, SMALL_ONE, own_one, small_one, got_one)
        got_one = line_moves(sends)
        vector = lambda n: ((n,), F32)
        grad_input, g_proj, g_fc1, g_fc2, g_bfc1, g_bproj, g_n2g, g_n2b, g_bfc2 = whole_call(
            finish_two_kernel,
            [own_two, small_two, *got_two, grad_own, grad_far],
            [(grad_own.shape, BF16), (w_proj.T.shape, F32), (w_fc1.shape, F32), (w_fc2.T.shape, F32), vector(FF)] + [vector(C)] * 4,
        )
        g_red, g_qkv, g_rgain, g_rshift, g_n1g, g_n1b, g_bqkv, g_table = whole_call(
            finish_one_kernel,
            [after(own_one, g_proj), small_one, *got_one],
            [(w_red.T.shape, F32), (w_qkv.T.shape, F32), vector(2 * C), vector(2 * C), vector(C), vector(C)]
            + [vector(3 * C), ((HEADS, 169), F32)],
        )
        grad_input = grad_input.transpose(0, 1, 3, 2).reshape(MB, 1, 7, W2, C2)
        return (
            output, grad_input, g_rgain, g_rshift, g_red.T, g_n1g, g_n1b, g_qkv.T, g_bqkv, g_table.T, g_proj.T,
            g_bproj, g_n2g, g_n2b, g_fc1, g_bfc1, g_fc2.T, g_bfc2,
        )
    g_red, g_qkv, g_proj, g_fc1, g_fc2 = (
        scatter_grad(g) for g in (jnp.concatenate([large_one[0][0], large_one[0][1]], axis=1), large_one[1], *large_two)
    )
    one, two = lax.psum((small_one, small_two), ("sp", "dp"))
    grad_input = (grad_own + grad_far).transpose(0, 1, 3, 2).reshape(MB, 1, 7, W2, C2)
    flat = lambda rows: rows.reshape(-1)
    return (
        output, grad_input, flat(one[:2]), flat(one[2:4]), g_red, one[4], one[5], g_qkv, flat(one[6:9]),
        one[9 : 9 + HEADS, :169].T, g_proj, two[4], two[5], two[6], g_fc1, flat(two[:4]), g_fc2, two[7],
    )


def solution(mesh):
    weight = P("dp", "sp")
    placed = (
        P(None, "dp", "sp", None, None), P(None, "dp"), P(), P(), weight, P(), P(), weight, P(), P(),
        weight, P(), P(), P(), weight, P(), weight, P(), P(None, "dp", "sp", None, None, None),
    )
    out_specs = (
        P(None, "dp", "sp", None, None, None), P(None, "dp", "sp", None, None), P(), P(), weight,
        P(), P(), weight, P(), P(), weight, P(), P(), P(), weight, P(), weight, P(),
    )
    return jax.shard_map(shards, mesh=mesh, in_specs=placed, out_specs=out_specs, check_vma=False)
```

```python
import jax
import jax.numpy as jnp
import numpy as np
from jax import lax
from jax.experimental import pallas as pl
from jax.experimental.pallas import tpu as pltpu
from jax.sharding import PartitionSpec as P

C2 = 192
C = 384
HEADS = 12
HD = 32
FF = 1536
MB = 3
WH = 8
TOK = 7 * 7 * WH
ALL = MB * TOK
SLOT = 64
WROWS = WH * SLOT
W2 = 4 * 7 * WH
CHUNK = 768
EPSILON = 1e-05
DEAD = -1e30
HIGHEST = lax.Precision.HIGHEST
F32 = jnp.float32
BF16 = jnp.bfloat16
UNROLL = 4
MICRO_UNROLL = 1
COST_NORM, COST_FORWARD, COST_FEED, COST_ATTENTION, COST_REDUCTION, COST_MERGE = 3, 1, 20, 10, 9, 5
MIB = 1024 * 1024
VMEM_NORM, VMEM_FORWARD, VMEM_FEED, VMEM_ATTENTION, VMEM_REDUCTION, VMEM_MERGE, VMEM_SUM = 8, 24, 34, 24, 24, 10, 10

ROWS_ONE = 64
ROWS_TWO = 112
SMALL_ONE = 16
SMALL_TWO = 8
PLANE = [(0, 0), (0, 1), (1, 0), (1, 1)]


def nn(left, right):
    return lax.dot_general(left, right, (((1,), (0,)), ((), ())), preferred_element_type=F32)


def nt(left, right):
    return lax.dot_general(left, right, (((1,), (1,)), ((), ())), preferred_element_type=F32)


def tn(left, right):
    return lax.dot_general(left, right, (((0,), (0,)), ((), ())), preferred_element_type=F32)


def constants():
    to_window = np.zeros((WROWS, TOK), np.float32)
    for w in range(WH):
        for r in range(7):
            for c in range(7):
                to_window[w * SLOT + 7 * r + c, r * 56 + 7 * w + c] = 1
    head_mask = (np.arange(256)[:, None] // SLOT == np.arange(128)[None] // HD).astype(np.float32)
    regroup = np.zeros((SLOT, SLOT), np.float32)
    ungroup = np.zeros((SLOT, SLOT), np.float32)
    reach = np.zeros((256, 1024), np.float32)
    for p in range(49):
        regroup[p // 7 * 8 + 7 - p % 7, p] = 1
        ungroup[p, p // 7 * 8 + p % 7] = 1
        for h in range(4):
            reach[h * SLOT + p, h * 256 + 84 + 13 * (p // 7) + p % 7] = 1
    low = lambda a: jnp.asarray(a, BF16)
    return dict(
        to_window=low(to_window),
        to_natural=low(to_window.T),
        head_mask=low(head_mask),
        regroup=low(regroup),
        ungroup=low(ungroup),
        reach=low(reach),
    )


def column_of(shape, width, factor, shift):
    at = lax.broadcasted_iota(jnp.int32, shape, 0)
    return at - width * ((at * factor) >> shift)


def key_column(shape):
    return jnp.where(lax.broadcasted_iota(jnp.int32, shape, 0) < 49, column_of(shape, 7, 37, 8), 1 << 20)


def split_of(core):
    at = lax.broadcasted_iota(jnp.int32, (112, W2), 0)
    column = lax.broadcasted_iota(jnp.int32, (112, W2), 1) - core * 112
    return jnp.where(column == jnp.where(at < 56, 2 * at, 2 * at - 111), 1.0, 0.0).astype(BF16)


def row(ref):
    return ref[...].reshape(1, -1)


def norm_of(values):
    center = jnp.mean(values, -1, keepdims=True)
    shifted = values - center
    inverse = lax.rsqrt(jnp.mean(shifted * shifted, -1, keepdims=True) + EPSILON)
    return shifted * inverse, inverse


def norm_back(grad_out, normal, inverse, gain):
    grad_normal = grad_out * gain
    grad_in = inverse * (
        grad_normal
        - jnp.mean(grad_normal, -1, keepdims=True)
        - normal * jnp.mean(grad_normal * normal, -1, keepdims=True)
    )
    return (
        grad_in,
        jnp.sum(grad_out * normal, 0, keepdims=True),
        jnp.sum(grad_out, 0, keepdims=True),
    )


def four_heads(rows, head_mask):
    return jnp.concatenate([rows] * 4, axis=0) * head_mask


def own_blocks(full):
    return [full[HD * h : HD * h + HD, SLOT * h : SLOT * h + SLOT] for h in range(4)]


def beside(upper, lower):
    return jnp.concatenate([upper, lower], axis=1)


def pad_rows(rows, count):
    return jnp.concatenate([rows, jnp.zeros((count - rows.shape[0], rows.shape[1]), F32)], axis=0)


def pack_kernel(red_ref, qkv_ref, proj_ref, fc1_ref, fc2_ref, pack_ref):
    qkv = qkv_ref[...].astype(F32)
    one = [red_ref[...].astype(F32), beside(qkv[:40], pad_rows(qkv[40:], 40))]
    pack_ref[:ROWS_ONE, :] = jnp.concatenate(one, axis=0).astype(BF16)
    proj, fc2 = proj_ref[...].astype(F32), fc2_ref[...].astype(F32)
    count = fc1_ref.shape[1]
    same = lax.broadcasted_iota(jnp.int32, (count, count), 0) == lax.broadcasted_iota(jnp.int32, (count, count), 1)
    fc1 = nt(jnp.where(same, 1.0, 0.0).astype(BF16), fc1_ref[...])
    two = [beside(proj[:16], pad_rows(proj[16:], 16)), beside(fc1[:48], fc1[48:]), fc2[:, :C], fc2[:, C:]]
    pack_ref[ROWS_ONE:, :] = jnp.concatenate(two, axis=0).astype(BF16)


def pack_weights(w_red, w_qkv, w_proj, w_fc1, w_fc2):
    return pl.pallas_call(
        pack_kernel,
        out_shape=jax.ShapeDtypeStruct((ROWS_ONE + ROWS_TWO, C), BF16),
    )(w_red.T, w_qkv.T, w_proj.T, w_fc1, w_fc2.T)


def each_block(place_ref):
    spot = place_ref[0]
    z, y, core = spot // 4, spot // 2 % 2, spot % 2
    for dc in range(2):
        for dy in range(2):
            for dz in range(4):
                yield dc, dz, dy, ((z ^ dz) * 2 + (y ^ dy)) * 2 + (core ^ dc)


def spots(block, stride, first, count):
    return pl.ds(pl.multiple_of(block * stride + first, 8), count)


def two_halves(refs, first, dc, dz, dy):
    near = refs[4 * dc + 2 * dy][dz].astype(F32)
    far = refs[4 * dc + 2 * dy + 1][dz].astype(F32)
    return jnp.where(first, near, far), jnp.where(first, far, near)


def unpack_one(place_ref, packs, red_ref, qkv_ref, red_f32, qkv_f32):
    first = place_ref[1] == 0
    for dc, dz, dy, block in each_block(place_ref):
        a, b = two_halves(packs, first, dc, dz, dy)
        red_f32[0, spots(block, 24, 0, 24), :] = a[:24]
        red_f32[1, spots(block, 24, 0, 24), :] = b[:24]
        qkv_f32[spots(block, 72, 0, 40), :] = beside(a[24:, :C2], b[24:, :C2])
        qkv_f32[spots(block, 72, 40, 32), :] = beside(a[24:56, C2:], b[24:56, C2:])
    red_ref[...] = red_f32[...].astype(BF16)
    qkv_ref[...] = qkv_f32[...].astype(BF16)


def unpack_two(place_ref, packs, proj_ref, fc1_ref, fc2_ref, proj_f32, fc1_f32, fc2_f32):
    first = place_ref[1] == 0
    for dc, dz, dy, block in each_block(place_ref):
        a, b = two_halves(packs, first, dc, dz, dy)
        proj_f32[spots(block, 24, 0, 16), :] = beside(a[:16, :C2], b[:16, :C2])
        proj_f32[spots(block, 24, 16, 8), :] = beside(a[:8, C2:], b[:8, C2:])
        fc1_f32[spots(block, 96, 0, 48), :] = beside(a[16:64, :C2], b[16:64, :C2])
        fc1_f32[spots(block, 96, 48, 48), :] = beside(a[16:64, C2:], b[16:64, C2:])
        for d, half in enumerate((a, b)):
            fc2_f32[spots(block, 24, 0, 24), 2 * d * C : 2 * d * C + C] = half[64:88]
            fc2_f32[spots(block, 24, 0, 24), 2 * d * C + C : 2 * d * C + 2 * C] = half[88:]
    proj_ref[...] = proj_f32[...].astype(BF16)
    fc1_ref[...] = fc1_f32[...].astype(BF16)
    fc2_ref[...] = fc2_f32[...].astype(BF16)


def put_block(place_ref, dc, dz, dy, halves, mine_ref, theirs_ref):
    first = place_ref[1] == 0
    out_ref = theirs_ref if dc else mine_ref
    count = halves[0].shape[0]
    for dx in range(2):
        at = ((2 * dy + dx) * 4 + dz) * count
        out_ref[at : at + count, :] = jnp.where(first, halves[dx], halves[1 - dx]).astype(BF16)


def two_terms(values):
    high = values.astype(BF16)
    return jnp.concatenate([high.astype(F32), values - high.astype(F32)], axis=0).astype(BF16)


def pack_one_grads(place_ref, red_ref, qkv_ref, small, mine_ref, theirs_ref):
    for dc, dz, dy, block in each_block(place_ref):
        top, low = qkv_ref[spots(block, 72, 0, 40), :], pad_rows(qkv_ref[spots(block, 72, 40, 32), :], 40)
        halves = []
        for d in range(2):
            lanes = slice(d * C2, d * C2 + C2)
            red = red_ref[d, spots(block, 24, 0, 24), :]
            halves.append(jnp.concatenate([red, beside(top[:, lanes], low[:, lanes])], axis=0))
        put_block(place_ref, dc, dz, dy, halves, mine_ref, theirs_ref)
    theirs_ref[16 * ROWS_ONE :, :] = two_terms(small)


def pack_two_grads(place_ref, proj_ref, fc1_ref, fc2_ref, small, mine_ref, theirs_ref):
    for dc, dz, dy, block in each_block(place_ref):
        proj_top, proj_low = proj_ref[spots(block, 24, 0, 16), :], pad_rows(proj_ref[spots(block, 24, 16, 8), :], 16)
        fc1_top, fc1_low = fc1_ref[spots(block, 96, 0, 48), :], fc1_ref[spots(block, 96, 48, 48), :]
        fc2 = fc2_ref[spots(block, 24, 0, 24), :]
        halves = []
        for d in range(2):
            lanes = slice(d * C2, d * C2 + C2)
            parts = [beside(proj_top[:, lanes], proj_low[:, lanes]), beside(fc1_top[:, lanes], fc1_low[:, lanes])]
            parts += [fc2[:, 2 * d * C : 2 * d * C + C], fc2[:, 2 * d * C + C : 2 * d * C + 2 * C]]
            halves.append(jnp.concatenate(parts, axis=0))
        put_block(place_ref, dc, dz, dy, halves, mine_ref, theirs_ref)
    theirs_ref[16 * ROWS_TWO :, :] = two_terms(small)


def small_sum(small, refs, first, count):
    for ref in refs:
        small = small + (ref[first : first + count, :].astype(F32) + ref[first + count : first + 2 * count, :].astype(F32))
    return small


def core_sum_kernel(rows, count, mine_ref, other_ref, small_ref, own_ref, small_out_ref, *send_refs):
    small = small_sum(small_ref[...], [other_ref], 16 * rows, count)
    small_out_ref[...] = small
    for k in range(4):
        at = slice(4 * k * rows, 4 * k * rows + 4 * rows)
        total = mine_ref[at, :].astype(F32) + other_ref[at, :].astype(F32)
        if k == 0:
            own_ref[...] = total
        else:
            send_refs[k - 1][: 4 * rows, :] = total.astype(BF16)
            send_refs[k - 1][4 * rows :, :] = two_terms(small)


def plane_sum_kernel(rows, count, own_ref, small_ref, *refs):
    got, own_out_ref, small_out_ref, send_refs = refs[:3], refs[3], refs[4], refs[5:]
    small = small_sum(small_ref[...], got, 4 * rows, count)
    small_out_ref[...] = small
    for k in range(4):
        at = slice(k * rows, k * rows + rows)
        total = own_ref[at, :]
        for ref in got:
            total = total + ref[at, :].astype(F32)
        if k == 0:
            own_out_ref[...] = total
        else:
            send_refs[k - 1][:rows, :] = total.astype(BF16)
            send_refs[k - 1][rows:, :] = two_terms(small)


def line_sum(rows, count, own_ref, small_ref, got):
    total = own_ref[...]
    for ref in got:
        total = total + ref[:rows, :].astype(F32)
    return total, small_sum(small_ref[...], got, rows, count)


def finish_one_kernel(own_ref, small_ref, g1, g2, g3, red_ref, qkv_ref, rgain_ref, rshift_ref, gain_ref, shift_ref, bqkv_ref, table_ref):
    rows, small = line_sum(ROWS_ONE, SMALL_ONE, own_ref, small_ref, (g1, g2, g3))
    red_ref[...] = rows[:24]
    qkv_ref[...] = jnp.concatenate([rows[24:, :C2], rows[24:56, C2:]], axis=0)
    for at, ref in ((0, rgain_ref), (2, rshift_ref), (4, gain_ref), (5, shift_ref), (6, bqkv_ref)):
        for k in range(ref.shape[0] // C):
            ref[pl.ds(k * C, C)] = small[at + k]
    table_ref[: HEADS // 2, :] = small[9:15, :169]
    table_ref[HEADS // 2 :, :] = small[9:15, C2 : C2 + 169]


def finish_two_kernel(near_ref, far_ref, own_ref, small_ref, g1, g2, g3, grad_input_ref, proj_ref, fc1_ref, fc2_ref, bfc1_ref, bproj_ref, gain_ref, shift_ref, bfc2_ref):
    grad_input_ref[...] = near_ref[...] + far_ref[...]
    rows, small = line_sum(ROWS_TWO, SMALL_TWO, own_ref, small_ref, (g1, g2, g3))
    proj_ref[...] = jnp.concatenate([rows[:16, :C2], rows[:8, C2:]], axis=0)
    fc1_ref[...] = jnp.concatenate([rows[16:64, :C2], rows[16:64, C2:]], axis=0).T
    fc2_ref[...] = beside(rows[64:88], rows[88:])
    for at, ref in ((0, bfc1_ref), (4, bproj_ref), (5, gain_ref), (6, shift_ref), (7, bfc2_ref)):
        for k in range(ref.shape[0] // C):
            ref[pl.ds(k * C, C)] = small[at + k]


def merge_norm_kernel(
    place_ref, section_ref, incoming_ref, gain_ref, shift_ref, normed_ref, normal_ref, inverse_ref, parts_ref,
):
    is_left = place_ref[0] % 2 == 0
    split = split_of(place_ref[0] % 2)
    bands = []
    for r in range(14):
        own, other = section_ref[0, r % 7], incoming_ref[0, r % 7]
        bands.append(jnp.where(is_left, own, other) if r < 7 else jnp.where(is_left, other, own))
    for r in range(7):
        apart = nt(split, jnp.concatenate(bands[2 * r : 2 * r + 2], axis=0))
        parts_ref[0, r * 56 : r * 56 + 56, :] = apart[:56]
        parts_ref[1, r * 56 : r * 56 + 56, :] = apart[56:]
    total = jnp.sum(parts_ref[0] + parts_ref[1], -1, keepdims=True)
    shifted = [parts_ref[d] - total * (1.0 / (2 * C)) for d in range(2)]
    spread = jnp.sum(shifted[0] * shifted[0] + shifted[1] * shifted[1], -1, keepdims=True)
    inverse = lax.rsqrt(spread * (1.0 / (2 * C)) + EPSILON)
    inverse_ref[0] = inverse
    gain, shift = row(gain_ref), row(shift_ref)
    for d in range(2):
        normal = shifted[d] * inverse
        lanes = slice(d * C, d * C + C)
        normal_ref[0, d] = normal.astype(BF16)
        normed_ref[0, d] = (normal * gain[:, lanes] + shift[:, lanes]).astype(BF16)


def bias_kernel(table_ref, ungroup_ref, reach_ref, bias_ref, wide_ref):
    wide_ref[...] = jnp.zeros_like(wide_ref)
    wide_ref[:, :169] = table_ref[...]
    ungroup, reach = ungroup_ref[...], reach_ref[...]
    unused = jnp.where(lax.broadcasted_iota(jnp.int32, (SLOT, 256), 0) < 49, 0.0, DEAD)
    for t in range(3):
        heads = []
        for h in range(4):
            rows = jnp.broadcast_to(wide_ref[4 * t + h : 4 * t + h + 1, :], (8, 256))
            rows = pltpu.roll(rows, 0, axis=1, stride=1, stride_axis=0)
            blocks = [pltpu.roll(rows, 13 * r, axis=1) if r else rows for r in range(7)]
            heads.append(jnp.concatenate(blocks + [jnp.zeros((8, 256), F32)], axis=0))
        rest = jnp.concatenate(heads, axis=1)
        total = unused
        for _ in range(3):
            term = rest.astype(BF16)
            rest = rest - term.astype(F32)
            total = total + nt(nn(ungroup, term).astype(BF16), reach)
        bias_ref[t] = total


def stack_kernel(a_ref, b_ref, c_ref, d_ref, one_ref, two_ref):
    for k, ref in enumerate((a_ref, b_ref, c_ref, d_ref)):
        one_ref[k] = ref[:ROWS_ONE, :]
        two_ref[k] = ref[ROWS_ONE:, :]


def forward_kernel(direct, *refs):
    (
        place_ref, widths_ref, normed_ref, gain_ref, shift_ref,
        b_qkv_ref, bias_ref, to_window_ref, to_natural_ref, head_mask_ref,
    ) = refs[:10]
    cut = 18 if direct else 12
    packs, refs = refs[10:cut], refs[cut:]
    stream_ref, qkv_ref, soft_ref, attended_ref, w_red_ref, w_qkv_ref, turned_ref = refs[:7]
    core = place_ref[0] % 2
    if direct:
        unpack_one(place_ref, packs, w_red_ref, w_qkv_ref, *refs[7:])
    else:
        w_red_ref[...] = packs[0][...]
        w_qkv_ref[...] = packs[1][...]

    def micro(m, none):
        stream = nt(normed_ref[m, 0], w_red_ref[0]) + nt(normed_ref[m, 1], w_red_ref[1])
        stream_ref[m] = stream
        normal, _ = norm_of(stream)
        first = (normal * row(gain_ref) + row(shift_ref)).astype(BF16)
        first = nn(to_window_ref[...], first).astype(BF16)
        projected = nt(first, w_qkv_ref[...]) + row(b_qkv_ref)
        qkv_ref[m, :, :C] = (projected[:, :C] * (HD**-0.5)).astype(BF16)
        qkv_ref[m, :, C:] = projected[:, C:].astype(BF16)
        width = widths_ref[m]
        key_col = key_column((SLOT, 128))

        def pair(i, carry):
            head_mask = head_mask_ref[...]
            outs = [[None, None] for _ in range(HEADS)]
            for j in range(2):
                w = 2 * i + j
                rows = pl.ds(pl.multiple_of(w * SLOT, SLOT), SLOT)
                live = jnp.where(key_col + (core * 56 + w * 7) < width, 0.0, DEAD)
                for t in range(3):
                    q = qkv_ref[m, rows, 128 * t : 128 * t + 128]
                    k = qkv_ref[m, rows, C + 128 * t : C + 128 * t + 128]
                    v = qkv_ref[m, rows, 2 * C + 128 * t : 2 * C + 128 * t + 128]
                    scores = nt(k, four_heads(q, head_mask)) + bias_ref[t]
                    parts = []
                    for half in range(2):
                        part = scores[:, 128 * half : 128 * half + 128] + live
                        exponent = jnp.exp(part - jnp.max(part, 0, keepdims=True))
                        share = 1.0 / jnp.sum(exponent, 0, keepdims=True)
                        parts.append((exponent * share).astype(BF16))
                    soft = jnp.concatenate(parts, axis=1)
                    soft_ref[m, w, t] = soft
                    for h, block in enumerate(own_blocks(tn(v, soft))):
                        outs[4 * t + h][j] = block
            lanes = pl.ds(pl.multiple_of(i * 128, 128), 128)
            for h in range(HEADS):
                turned_ref[HD * h : HD * h + HD, lanes] = beside(*outs[h]).astype(BF16)
            return carry

        lax.fori_loop(0, WH // 2, pair, 0, unroll=UNROLL)
        attended_ref[m] = nt(to_natural_ref[...], turned_ref[...]).astype(BF16)
        return none

    lax.fori_loop(0, MB, micro, 0, unroll=MICRO_UNROLL)


def feed_kernel(direct, *refs):
    (
        place_ref, widths_ref, stream_ref, attended_ref, cotangent_ref,
        b_proj_ref, gain_ref, shift_ref, b_fc1_ref, b_fc2_ref,
    ) = refs[:10]
    cut = 18 if direct else 13
    packs, refs = refs[10:cut], refs[cut:]
    output_ref, grad_middle_ref, grad_att_ref, small_ref = refs[:4]
    if direct:
        mine_ref, theirs_ref, g_proj_ref, g_fc1_ref, g_fc2_ref = refs[4:9]
        refs = refs[9:]
    else:
        g_proj_ref, g_fc1_ref, g_fc2_ref = refs[4:7]
        refs = refs[7:]
    second_ref, grad_feed_ref, grad_second_ref, inverse_ref, bias_fc1_ref, g_bfc1_ref, w_proj_ref, w_fc1_ref, w_fc2_ref = refs
    step = pl.program_id(0)
    place_col = column_of((TOK, 1), 56, 1171, 16) + (place_ref[0] % 2) * 56
    keep = jnp.concatenate([jnp.where(place_col < widths_ref[m], 1.0, 0.0) for m in range(MB)], axis=0)

    @pl.when(step == 0)
    def _():
        if direct:
            unpack_two(place_ref, packs, w_proj_ref, w_fc1_ref, w_fc2_ref, g_proj_ref, g_fc1_ref, g_fc2_ref)
        else:
            w_proj_ref[...] = packs[0][...]
            w_fc1_ref[...] = packs[1][...]
            w_fc2_ref[...] = packs[2][...]
        bias_fc1_ref[...] = row(b_fc1_ref)
        middle = stream_ref[...] + nt(attended_ref[...], w_proj_ref[...]) + row(b_proj_ref)
        normal, inverse = norm_of(middle)
        inverse_ref[...] = inverse
        grad_middle_ref[...] = normal
        second_ref[...] = (normal * row(gain_ref) + row(shift_ref)).astype(BF16)
        grad_feed = (cotangent_ref[...] * keep).astype(BF16)
        grad_feed_ref[...] = grad_feed
        small_ref[7:8] = jnp.sum(grad_feed.astype(F32), 0, keepdims=True)
        output_ref[...] = middle + row(b_fc2_ref)
        grad_second_ref[...] = jnp.zeros_like(grad_second_ref)

    units = pl.ds(pl.multiple_of(step * CHUNK, CHUNK), CHUNK)
    w_fc1 = w_fc1_ref[units, :]
    w_fc2 = w_fc2_ref[:, units]
    second = second_ref[...]
    feed = grad_feed_ref[...]
    pre = nt(second, w_fc1) + bias_fc1_ref[:, units]
    cdf = 0.5 * (1.0 + lax.erf(pre * 0.7071067811865476))
    density = 0.3989422804014327 * jnp.exp(-0.5 * pre * pre)
    act = (pre * cdf).astype(BF16)
    output_ref[...] += nt(act, w_fc2)
    g_fc2_ref[:, units] = tn(feed, act)
    grad_pre = (nn(feed, w_fc2) * (cdf + pre * density)).astype(BF16)
    g_bfc1_ref[:, units] = jnp.sum(grad_pre.astype(F32), 0, keepdims=True)
    g_fc1_ref[units, :] = tn(grad_pre, second)
    grad_second_ref[...] += nn(grad_pre, w_fc1)

    @pl.when(step == FF // CHUNK - 1)
    def _():
        output_ref[...] = output_ref[...] * keep
        grad_norm, g_gain, g_shift = norm_back(grad_second_ref[...], grad_middle_ref[...], inverse_ref[...], row(gain_ref))
        small_ref[5:6] = g_gain
        small_ref[6:7] = g_shift
        grad_middle = cotangent_ref[...] * keep + grad_norm
        grad_middle_ref[...] = grad_middle
        branch = grad_middle.astype(BF16)
        small_ref[4:5] = jnp.sum(branch.astype(F32), 0, keepdims=True)
        g_proj_ref[...] = tn(branch, attended_ref[...])
        grad_att_ref[...] = nn(branch, w_proj_ref[...]).astype(BF16)
        for k in range(4):
            small_ref[k : k + 1] = g_bfc1_ref[:, k * C : k * C + C]
        if direct:
            pack_two_grads(place_ref, g_proj_ref, g_fc1_ref, g_fc2_ref, small_ref[...], mine_ref, theirs_ref)


def table_rows(pairs_ref, regroup, reach):
    rows = []
    for t in range(3):
        sums = pairs_ref[t]
        high = sums.astype(BF16)
        low = (sums - high.astype(F32)).astype(BF16)
        spread = nn(nn(regroup, high).astype(BF16), reach) + nn(nn(regroup, low).astype(BF16), reach)
        for h in range(4):
            total = 0.0
            for r in range(7):
                part = spread[8 * r : 8 * r + 8, 256 * h : 256 * h + 256]
                total = total + (pltpu.roll(part, 256 - 13 * r, axis=1) if r else part)
            total = pltpu.roll(total, 249, axis=1, stride=1, stride_axis=0)
            rows.append(jnp.sum(total, 0, keepdims=True))
    rows = jnp.concatenate(rows, axis=0)[:, :C2]
    return beside(rows[: HEADS // 2], rows[HEADS // 2 :])


def attention_kernel(
    to_window_ref, to_natural_ref, head_mask_ref, regroup_ref, reach_ref, qkv_ref, soft_ref, grad_att_ref,
    grad_projected_ref, small_ref,
    window_ref, turned_ref, grad_window_ref, pairs_ref,
):
    pairs_ref[...] = jnp.zeros_like(pairs_ref)
    small_ref[...] = jnp.zeros_like(small_ref)

    def micro(m, none):
        window_ref[...] = nn(to_window_ref[...], grad_att_ref[m]).astype(BF16)

        def pair(i, carry):
            head_mask = head_mask_ref[...]
            outs = [[None, None] for _ in range(HEADS)]
            for t in range(3):
                scores_sum = 0.0
                for j in range(2):
                    w = 2 * i + j
                    rows = pl.ds(pl.multiple_of(w * SLOT, SLOT), SLOT)
                    q = qkv_ref[m, rows, 128 * t : 128 * t + 128]
                    k = qkv_ref[m, rows, C + 128 * t : C + 128 * t + 128]
                    v = qkv_ref[m, rows, 2 * C + 128 * t : 2 * C + 128 * t + 128]
                    grad = four_heads(window_ref[rows, 128 * t : 128 * t + 128], head_mask)
                    soft_low = soft_ref[m, w, t]
                    soft = soft_low.astype(F32)
                    grad_soft = nt(v, grad)
                    inner = jnp.sum(grad_soft * soft, 0, keepdims=True)
                    scores = (soft * (grad_soft - inner)).astype(BF16)
                    scores_sum = scores_sum + scores.astype(F32)
                    grad_key = nn(scores, four_heads(q, head_mask))
                    grad_value = nn(soft_low, grad)
                    grad_window_ref[rows, 128 * t : 128 * t + 128] = grad_key.astype(BF16)
                    grad_window_ref[rows, C + 128 * t : C + 128 * t + 128] = grad_value.astype(BF16)
                    for h, block in enumerate(own_blocks(tn(k, scores))):
                        outs[4 * t + h][j] = block
                pairs_ref[t] += scores_sum
            lanes = pl.ds(pl.multiple_of(i * 128, 128), 128)
            for h in range(HEADS):
                turned_ref[HD * h : HD * h + HD, lanes] = (beside(*outs[h]) * (HD**-0.5)).astype(BF16)
            return carry

        lax.fori_loop(0, WH // 2, pair, 0, unroll=UNROLL)
        to_natural = to_natural_ref[...]
        grad_query = nt(to_natural, turned_ref[...])
        grad_rest = nn(to_natural, grad_window_ref[...])
        grad_projected_ref[m, :, :C] = grad_query.astype(BF16)
        grad_projected_ref[m, :, C:] = grad_rest.astype(BF16)
        small_ref[0:1] += jnp.sum(grad_query, 0, keepdims=True)
        sums = jnp.sum(grad_rest, 0, keepdims=True)
        small_ref[1:2] += sums[:, :C]
        small_ref[2:3] += sums[:, C:]
        return none

    lax.fori_loop(0, MB, micro, 0, unroll=MB)
    small_ref[3 : 3 + HEADS // 2] = table_rows(pairs_ref, regroup_ref[...], reach_ref[...])


def reduction_kernel(direct, *refs):
    (
        place_ref, red_gain_ref, red_shift_ref, w_red_ref, gain_ref, shift_ref, w_qkv_ref,
        stream_ref, grad_middle_ref, grad_projected_ref, normal_ref, small_in_ref,
    ) = refs[:12]
    refs = refs[12:]
    grad_stream_ref, small_ref = refs[:2]
    if direct:
        mine_ref, theirs_ref, g_red_ref, g_qkv_ref, sums_ref = refs[2:]
    else:
        g_red_ref, g_qkv_ref, sums_ref = refs[2:]
    grad_projected = grad_projected_ref[...]
    normal, inverse = norm_of(stream_ref[...])
    gain = row(gain_ref)
    first = (normal * gain + row(shift_ref)).astype(BF16)
    g_qkv_ref[...] = tn(grad_projected, first)
    grad_norm, g_gain, g_shift = norm_back(nn(grad_projected, w_qkv_ref[...]), normal, inverse, gain)
    grad_stream = (grad_middle_ref[...] + grad_norm).astype(BF16)
    grad_stream_ref[...] = grad_stream
    red_gain, red_shift = row(red_gain_ref), row(red_shift_ref)
    sums_ref[...] = tn(grad_stream, jnp.ones((ALL, 128), BF16))
    column = sums_ref[:, :1]
    small_ref[...] = jnp.zeros_like(small_ref)
    small_ref[4:5] = g_gain
    small_ref[5:6] = g_shift
    small_ref[6:15] = small_in_ref[:9]
    for d in range(2):
        lanes = slice(d * C, d * C + C)
        weight = w_red_ref[d].astype(F32)
        product = sum(tn(grad_stream[m * TOK : m * TOK + TOK], normal_ref[m, d]) for m in range(MB))
        small_ref[d : d + 1] = jnp.sum(weight * product, 0, keepdims=True)
        small_ref[2 + d : 3 + d] = jnp.sum(weight * column, 0, keepdims=True)
        g_red_ref[d] = product * red_gain[:, lanes] + column * red_shift[:, lanes]
    if direct:
        pack_one_grads(place_ref, g_red_ref, g_qkv_ref, small_ref[...], mine_ref, theirs_ref)


def merge_kernel(
    place_ref, red_gain_ref, w_red_ref, grad_stream_ref, normal_ref, inverse_ref, own_ref, send_ref,
    parts_ref, rows_ref,
):
    core = place_ref[0] % 2
    red_gain = row(red_gain_ref)
    grad_stream = grad_stream_ref[0]
    grads = [nn(grad_stream, w_red_ref[d]) * red_gain[:, d * C : d * C + C] for d in range(2)]
    normals = [normal_ref[0, d].astype(F32) for d in range(2)]
    mean_one = jnp.sum(grads[0] + grads[1], -1, keepdims=True) * (1.0 / (2 * C))
    mean_two = jnp.sum(grads[0] * normals[0] + grads[1] * normals[1], -1, keepdims=True) * (1.0 / (2 * C))
    for d in range(2):
        parts_ref[d] = inverse_ref[0] * (grads[d] - mean_one - normals[d] * mean_two)
    join = split_of(core)
    for r in range(7):
        at = slice(r * 56, r * 56 + 56)
        apart = jnp.concatenate([parts_ref[0, at, :], parts_ref[1, at, :]], axis=0).astype(BF16)
        rows = tn(apart, join).astype(BF16)
        rows_ref[2 * r], rows_ref[2 * r + 1] = rows[:C2], rows[C2:]
    is_left = core == 0
    for r in range(7):
        upper, lower = rows_ref[r], rows_ref[7 + r]
        own_ref[0, r] = jnp.where(is_left, upper, lower)
        send_ref[0, r] = jnp.where(is_left, lower, upper)


SCALARS = pl.BlockSpec(memory_space=pltpu.SMEM)


def whole(shape):
    return pl.BlockSpec(shape, lambda m: (0,) * len(shape), pipeline_mode=pl.Buffered(1))


def each(shape):
    return pl.BlockSpec((1,) + shape, lambda m: (m,) + (0,) * len(shape))


def scalar(array):
    return (array, SCALARS)


def fixed(array):
    return (array, whole(array.shape))


def stepped(array):
    return (array, each(array.shape[1:]))


def out_fixed(shape, dtype):
    return (shape, dtype, whole(shape))


def out_stepped(shape, dtype):
    return ((MB,) + shape, dtype, each(shape))


def run_kernel(kernel, ins, outs, scratch, micros, vmem, steps=MB):
    return pl.pallas_call(
        kernel,
        grid=(steps,),
        in_specs=[spec for _, spec in ins],
        out_specs=[spec for _, _, spec in outs],
        out_shape=[jax.ShapeDtypeStruct(shape, dtype) for shape, dtype, _ in outs],
        scratch_shapes=scratch,
        compiler_params=pltpu.CompilerParams(vmem_limit_bytes=vmem * MIB),
        cost_estimate=pl.CostEstimate(flops=int(micros * 1.15e9), bytes_accessed=0, transcendentals=0),
    )(*[array for array, _ in ins])


def whole_call(kernel, ins, outs):
    return pl.pallas_call(
        kernel,
        out_shape=[jax.ShapeDtypeStruct(shape, dtype) for shape, dtype in outs],
        compiler_params=pltpu.CompilerParams(vmem_limit_bytes=VMEM_SUM * MIB),
    )(*ins)


def merge_norm_call(place, section, incoming, gain, shift):
    return run_kernel(
        merge_norm_kernel,
        [scalar(place), stepped(section), stepped(incoming), fixed(gain), fixed(shift)],
        [out_stepped((2, TOK, C), BF16), out_stepped((2, TOK, C), BF16), out_stepped((TOK, 1), F32)],
        [pltpu.VMEM((2, TOK, C), F32)],
        COST_NORM,
        VMEM_NORM,
    )


def bias_call(const, table):
    return pl.pallas_call(
        bias_kernel,
        out_shape=jax.ShapeDtypeStruct((3, SLOT, 256), F32),
        scratch_shapes=[pltpu.VMEM((HEADS, 256), F32)],
        compiler_params=pltpu.CompilerParams(vmem_limit_bytes=VMEM_SUM * MIB),
    )(table, const["ungroup"], const["reach"])


def stack(blocks):
    return whole_call(stack_kernel, blocks, [((4, ROWS_ONE, C), BF16), ((4, ROWS_TWO, C), BF16)])


def forward_call(direct, const, place, widths, normed, gain, shift, b_qkv, bias, weights):
    return run_kernel(
        lambda *refs: forward_kernel(direct, *refs),
        [
            scalar(place), scalar(widths), fixed(normed), fixed(gain), fixed(shift), fixed(b_qkv), fixed(bias), fixed(const["to_window"]),
            fixed(const["to_natural"]), fixed(const["head_mask"]),
        ] + [fixed(w) for w in weights],
        [
            out_fixed((MB, TOK, C), F32),
            out_fixed((MB, WROWS, 3 * C), BF16),
            out_fixed((MB, WH, 3, SLOT, 256), BF16),
            out_fixed((MB, TOK, C), BF16),
            out_fixed((2, C, C), BF16),
            out_fixed((3 * C, C), BF16),
        ],
        [pltpu.VMEM((C, WROWS), BF16)]
        + ([pltpu.VMEM((2, C, C), F32), pltpu.VMEM((3 * C, C), F32)] if direct else []),
        COST_FORWARD,
        VMEM_FORWARD,
        1,
    )


def feed_call(direct, place, widths, stream, attended, cotangent, b_proj, gain, shift, b_fc1, b_fc2, weights):
    grads = [((C, C), F32), ((FF, C), F32), ((C, FF), F32)]
    packed = [((16 * ROWS_TWO, C), BF16), ((16 * ROWS_TWO + 2 * SMALL_TWO, C), BF16)]
    scratch = [
        pltpu.VMEM((ALL, C), BF16), pltpu.VMEM((ALL, C), BF16), pltpu.VMEM((ALL, C), F32), pltpu.VMEM((ALL, 1), F32),
        pltpu.VMEM((1, FF), F32), pltpu.VMEM((1, FF), F32),
        pltpu.VMEM((C, C), BF16), pltpu.VMEM((FF, C), BF16), pltpu.VMEM((C, FF), BF16),
    ]
    if direct:
        scratch = [pltpu.VMEM(*g) for g in grads] + scratch
    flat = lambda array: array.reshape(ALL, C)
    output, grad_middle, grad_att, *rest = run_kernel(
        lambda *refs: feed_kernel(direct, *refs),
        [
            scalar(place), scalar(widths), fixed(flat(stream)), fixed(flat(attended)), fixed(flat(cotangent)),
            fixed(b_proj), fixed(gain), fixed(shift), fixed(b_fc1), fixed(b_fc2),
        ] + [fixed(w) for w in weights],
        [
            out_fixed((ALL, C), F32),
            out_fixed((ALL, C), F32),
            out_fixed((ALL, C), BF16),
            out_fixed((SMALL_TWO, C), F32),
        ] + [out_fixed(*o) for o in (packed if direct else grads)],
        scratch,
        COST_FEED,
        VMEM_FEED,
        FF // CHUNK,
    )
    return output, grad_middle.reshape(MB, TOK, C), grad_att.reshape(MB, TOK, C), *rest


def attention_call(const, qkv, soft, grad_att):
    return run_kernel(
        attention_kernel,
        [fixed(const[n]) for n in ("to_window", "to_natural", "head_mask", "regroup", "reach")]
        + [fixed(qkv), fixed(soft), fixed(grad_att)],
        [out_fixed((MB, TOK, 3 * C), BF16), out_fixed((16, C), F32)],
        [
            pltpu.VMEM((WROWS, C), BF16),
            pltpu.VMEM((C, WROWS), BF16),
            pltpu.VMEM((WROWS, 2 * C), BF16),
            pltpu.VMEM((3, SLOT, 256), F32),
        ],
        COST_ATTENTION,
        VMEM_ATTENTION,
        1,
    )


def reduction_call(direct, place, red_gain, red_shift, w_red, gain, shift, w_qkv, stream, grad_middle, grad_projected, normal, small):
    grads = [((2, C, C), F32), ((3 * C, C), F32)]
    packed = [((16 * ROWS_ONE, C), BF16), ((16 * ROWS_ONE + 2 * SMALL_ONE, C), BF16)]
    flat = lambda array: array.reshape(ALL, array.shape[-1])
    grad_stream, *rest = run_kernel(
        lambda *refs: reduction_kernel(direct, *refs),
        [
            scalar(place), fixed(red_gain), fixed(red_shift), fixed(w_red), fixed(gain), fixed(shift), fixed(w_qkv),
            fixed(flat(stream)), fixed(flat(grad_middle)), fixed(flat(grad_projected)), fixed(normal), fixed(small),
        ],
        [out_fixed((ALL, C), BF16), out_fixed((SMALL_ONE, C), F32)]
        + [out_fixed(*o) for o in (packed if direct else grads)],
        ([pltpu.VMEM(*g) for g in grads] if direct else []) + [pltpu.VMEM((C, 128), F32)],
        COST_REDUCTION,
        VMEM_REDUCTION,
        1,
    )
    return grad_stream.reshape(MB, TOK, C), *rest


def merge_call(place, red_gain, w_red, grad_stream, normal, inverse):
    return run_kernel(
        merge_kernel,
        [
            scalar(place), fixed(red_gain), fixed(w_red),
            stepped(grad_stream), stepped(normal), stepped(inverse),
        ],
        [out_stepped((7, C2, W2), BF16), out_stepped((7, C2, W2), BF16)],
        [pltpu.VMEM((2, TOK, C), F32), pltpu.VMEM((14, C2, W2), BF16)],
        COST_MERGE,
        VMEM_MERGE,
    )


def from_core(block):
    count = lax.axis_size("sp")
    return lax.ppermute(block, "sp", [(i, i ^ 1) for i in range(count)])


def move(block, dz, dy, dx, dc):
    route = []
    for spot in range(16):
        for x in range(2):
            other = spot ^ (dz * 4 + dy * 2 + dc)
            route.append((spot * 2 + x, other * 2 + (x ^ dx)))
    return lax.ppermute(block, ("sp", "dp"), route)


def line_spread(pack):
    return [pack] + [move(pack, dz, 0, 0, 0) for dz in range(1, 4)]


def plane_spread(column):
    return [column] + [move(column, 0, dy, dx, 0) for dy, dx in PLANE[1:]]


def core_spread(mine):
    return mine + [core_move(part) for part in mine]


def after(value, *others):
    return lax.optimization_barrier((value,) + others)[0]


def core_move(block):
    return move(block, 0, 0, 0, 1)


def core_sum(rows, count, mine, other, small):
    send = ((4 * rows + 2 * count, C), BF16)
    own, small, *sends = whole_call(
        lambda *refs: core_sum_kernel(rows, count, *refs),
        [mine, other, small],
        [((4 * rows, C), F32), ((count, C), F32), send, send, send],
    )
    return own, small, sends


def plane_moves(sends):
    return [move(s, 0, dy, dx, 0) for s, (dy, dx) in zip(sends, PLANE[1:])]


def plane_sum(rows, count, own, small, got):
    send = ((rows + 2 * count, C), BF16)
    own, small, *sends = whole_call(
        lambda *refs: plane_sum_kernel(rows, count, *refs),
        [own, small, *got],
        [((rows, C), F32), ((count, C), F32), send, send, send],
    )
    return own, small, sends


def line_moves(sends):
    return [move(s, dz, 0, 0, 0) for dz, s in zip(range(1, 4), sends)]


def gather_weight(shard):
    rows = lax.all_gather(shard.T, "sp", axis=0, tiled=True)
    return lax.all_gather(rows, "dp", axis=1, tiled=True)


def scatter_grad(grad):
    share = lax.psum_scatter(grad.astype(BF16), "sp", scatter_dimension=0, tiled=True)
    share = lax.psum_scatter(share, "dp", scatter_dimension=1, tiled=True)
    return share.astype(F32).T


def shards(
    section_two, widths, red_gain, red_shift, w_red, norm1_gain, norm1_shift, w_qkv, b_qkv,
    bias_table, w_proj, b_proj, norm2_gain, norm2_shift, w_fc1, b_fc1, w_fc2, b_fc2, cotangent,
):
    direct = lax.axis_size("sp") == 16 and lax.axis_size("dp") == 2
    const = constants()
    place = jnp.stack([lax.axis_index("sp"), lax.axis_index("dp")]).astype(jnp.int32)
    widths = widths.reshape(MB)
    section = section_two.reshape(MB, 7, W2, C2).transpose(0, 1, 3, 2)
    incoming = from_core(section)
    if direct:
        pack = pack_weights(w_red, w_qkv, w_proj, w_fc1, w_fc2)
        line = line_spread(pack)
    normed, normal, inverse = merge_norm_call(place, section, incoming, red_gain, red_shift)
    bias = bias_call(const, after(bias_table, normed).T)
    if direct:
        line[1:] = [after(part, normed, bias) for part in line[1:]]
        column_one, column_two = stack(line)
        weights_one = core_spread(plane_spread(column_one))
        plane_two = plane_spread(column_two)
    else:
        wt_red = gather_weight(w_red)
        weights_one = [jnp.stack([wt_red[:, :C], wt_red[:, C:]]), gather_weight(w_qkv)]
        weights_two = [gather_weight(w) for w in (w_proj, w_fc1, w_fc2)]
    stream, qkv, soft, attended, wt_red, wt_qkv = forward_call(
        direct, const, place, widths, normed, norm1_gain, norm1_shift, b_qkv, bias, weights_one,
    )
    if direct:
        plane_two = [after(part, stream) for part in plane_two]
        weights_two = core_spread(plane_two)
    output, grad_middle, grad_att, small_two, *large_two = feed_call(
        direct, place, widths, stream, attended, cotangent, b_proj, norm2_gain, norm2_shift,
        b_fc1, b_fc2, weights_two,
    )
    if direct:
        mine, theirs = large_two
        own_two, small_two, sends = core_sum(ROWS_TWO, SMALL_TWO, mine, core_move(theirs), small_two)
        got_two = plane_moves(sends)
        grad_att = after(grad_att, own_two)
    grad_projected, small = attention_call(const, qkv, soft, grad_att)
    grad_stream, small_one, *large_one = reduction_call(
        direct, place, red_gain, red_shift, wt_red, norm1_gain, norm1_shift, wt_qkv, stream, grad_middle,
        grad_projected, normal, small,
    )
    if direct:
        mine, theirs = large_one
        got_two = [after(got, grad_stream) for got in got_two]
        other = core_move(after(theirs, *got_two))
        own_two, small_two, sends = plane_sum(ROWS_TWO, SMALL_TWO, own_two, small_two, got_two)
        got_two = line_moves(sends)
        other = after(other, own_two)
        own_one, small_one, sends = core_sum(ROWS_ONE, SMALL_ONE, mine, other, small_one)
        got_one = plane_moves(sends)
        grad_stream = after(grad_stream, own_one)
    grad_own, grad_send = merge_call(place, red_gain, wt_red, grad_stream, normal, inverse)
    if direct:
        grad_send = after(grad_send, *got_one, *got_two)
    grad_far = from_core(grad_send)
    output = output.reshape(MB, 1, 1, 7, 7 * WH, C)

    if direct:
        own_one, small_one, sends = plane_sum(ROWS_ONE, SMALL_ONE, own_one, small_one, got_one)
        got_one = line_moves(sends)
        vector = lambda n: ((n,), F32)
        grad_input, g_proj, g_fc1, g_fc2, g_bfc1, g_bproj, g_n2g, g_n2b, g_bfc2 = whole_call(
            finish_two_kernel,
            [grad_own, grad_far, own_two, small_two, *got_two],
            [(grad_own.shape, BF16), (w_proj.T.shape, F32), (w_fc1.shape, F32), (w_fc2.T.shape, F32), vector(FF)] + [vector(C)] * 4,
        )
        g_red, g_qkv, g_rgain, g_rshift, g_n1g, g_n1b, g_bqkv, g_table = whole_call(
            finish_one_kernel,
            [after(own_one, g_proj), small_one, *got_one],
            [(w_red.T.shape, F32), (w_qkv.T.shape, F32), vector(2 * C), vector(2 * C), vector(C), vector(C)]
            + [vector(3 * C), ((HEADS, 169), F32)],
        )
        grad_input = grad_input.transpose(0, 1, 3, 2).reshape(MB, 1, 7, W2, C2)
        return (
            output, grad_input, g_rgain, g_rshift, g_red.T, g_n1g, g_n1b, g_qkv.T, g_bqkv, g_table.T, g_proj.T,
            g_bproj, g_n2g, g_n2b, g_fc1, g_bfc1, g_fc2.T, g_bfc2,
        )
    g_red, g_qkv, g_proj, g_fc1, g_fc2 = (
        scatter_grad(g) for g in (jnp.concatenate([large_one[0][0], large_one[0][1]], axis=1), large_one[1], *large_two)
    )
    one, two = lax.psum((small_one, small_two), ("sp", "dp"))
    grad_input = (grad_own + grad_far).transpose(0, 1, 3, 2).reshape(MB, 1, 7, W2, C2)
    flat = lambda rows: rows.reshape(-1)
    return (
        output, grad_input, flat(one[:2]), flat(one[2:4]), g_red, one[4], one[5], g_qkv, flat(one[6:9]),
        jnp.concatenate([one[9:15, :169], one[9:15, C2 : C2 + 169]]).T, g_proj, two[4], two[5], two[6], g_fc1, flat(two[:4]), g_fc2, two[7],
    )


def solution(mesh):
    weight = P("dp", "sp")
    placed = (
        P(None, "dp", "sp", None, None), P(None, "dp"), P(), P(), weight, P(), P(), weight, P(), P(),
        weight, P(), P(), P(), weight, P(), weight, P(), P(None, "dp", "sp", None, None, None),
    )
    out_specs = (
        P(None, "dp", "sp", None, None, None), P(None, "dp", "sp", None, None), P(), P(), weight,
        P(), P(), weight, P(), P(), weight, P(), P(), P(), weight, P(), weight, P(),
    )
    return jax.shard_map(shards, mesh=mesh, in_specs=placed, out_specs=out_specs, check_vma=False)
```

```python
import jax
import jax.numpy as jnp
import numpy as np
from jax import lax
from jax.experimental import pallas as pl
from jax.experimental.pallas import tpu as pltpu
from jax.sharding import PartitionSpec as P

C2 = 192
C = 384
HEADS = 12
HD = 32
FF = 1536
MB = 3
WH = 8
TOK = 7 * 7 * WH
ALL = MB * TOK
SLOT = 64
WROWS = WH * SLOT
W2 = 4 * 7 * WH
CHUNK = 512
EPSILON = 1e-05
DEAD = -1e30
HIGHEST = lax.Precision.HIGHEST
F32 = jnp.float32
BF16 = jnp.bfloat16
UNROLL = 4
MICRO_UNROLL = 1
COST_NORM, COST_FORWARD, COST_FEED, COST_ATTENTION, COST_REDUCTION, COST_MERGE = 3, 1, 20, 10, 9, 5
MIB = 1024 * 1024
VMEM_NORM, VMEM_FORWARD, VMEM_FEED, VMEM_ATTENTION, VMEM_REDUCTION, VMEM_MERGE, VMEM_SUM = 12, 24, 32, 24, 24, 12, 10

ROWS_ONE = 64
ROWS_TWO = 112
SMALL_ONE = 16
SMALL_TWO = 8
PLANE = [(0, 0), (0, 1), (1, 0), (1, 1)]


def nn(left, right):
    return lax.dot_general(left, right, (((1,), (0,)), ((), ())), preferred_element_type=F32)


def nt(left, right):
    return lax.dot_general(left, right, (((1,), (1,)), ((), ())), preferred_element_type=F32)


def tn(left, right):
    return lax.dot_general(left, right, (((0,), (0,)), ((), ())), preferred_element_type=F32)


def constants():
    to_window = np.zeros((WROWS, TOK), np.float32)
    for w in range(WH):
        for r in range(7):
            for c in range(7):
                to_window[w * SLOT + 7 * r + c, r * 56 + 7 * w + c] = 1
    head_mask = (np.arange(256)[:, None] // SLOT == np.arange(128)[None] // HD).astype(np.float32)
    regroup = np.zeros((SLOT, SLOT), np.float32)
    reach = np.zeros((256, 1024), np.float32)
    for p in range(49):
        regroup[p // 7 * 8 + 7 - p % 7, p] = 1
        for h in range(4):
            reach[h * SLOT + p, h * 256 + 84 + 13 * (p // 7) + p % 7] = 1
    low = lambda a: jnp.asarray(a, BF16)
    return dict(
        to_window=low(to_window),
        to_natural=low(to_window.T),
        head_mask=low(head_mask),
        regroup=low(regroup),
        reach=low(reach),
    )


def column_of(shape, width, factor, shift):
    at = lax.broadcasted_iota(jnp.int32, shape, 0)
    return at - width * ((at * factor) >> shift)


def key_column(shape):
    return jnp.where(lax.broadcasted_iota(jnp.int32, shape, 0) < 49, column_of(shape, 7, 37, 8), 1 << 20)


def split_of(core):
    at = lax.broadcasted_iota(jnp.int32, (112, W2), 0)
    column = lax.broadcasted_iota(jnp.int32, (112, W2), 1) - core * 112
    return jnp.where(column == jnp.where(at < 56, 2 * at, 2 * at - 111), 1.0, 0.0).astype(BF16)


def row(ref):
    return ref[...].reshape(1, -1)


def norm_of(values):
    center = jnp.mean(values, -1, keepdims=True)
    shifted = values - center
    inverse = lax.rsqrt(jnp.mean(shifted * shifted, -1, keepdims=True) + EPSILON)
    return shifted * inverse, inverse


def norm_back(grad_out, normal, inverse, gain):
    grad_normal = grad_out * gain
    grad_in = inverse * (
        grad_normal
        - jnp.mean(grad_normal, -1, keepdims=True)
        - normal * jnp.mean(grad_normal * normal, -1, keepdims=True)
    )
    return (
        grad_in,
        jnp.sum(grad_out * normal, 0, keepdims=True),
        jnp.sum(grad_out, 0, keepdims=True),
    )


def four_heads(rows, head_mask):
    return jnp.concatenate([rows] * 4, axis=0) * head_mask


def own_blocks(full):
    return [full[HD * h : HD * h + HD, SLOT * h : SLOT * h + SLOT] for h in range(4)]


def beside(upper, lower):
    return jnp.concatenate([upper, lower], axis=1)


def pad_rows(rows, count):
    return jnp.concatenate([rows, jnp.zeros((count - rows.shape[0], rows.shape[1]), F32)], axis=0)


def pack_kernel(red_ref, qkv_ref, proj_ref, fc1_ref, fc2_ref, pack_ref):
    qkv = qkv_ref[...].astype(F32)
    one = [red_ref[...].astype(F32), beside(qkv[:40], pad_rows(qkv[40:], 40))]
    pack_ref[:ROWS_ONE, :] = jnp.concatenate(one, axis=0).astype(BF16)
    proj, fc2 = proj_ref[...].astype(F32), fc2_ref[...].astype(F32)
    count = fc1_ref.shape[1]
    same = lax.broadcasted_iota(jnp.int32, (count, count), 0) == lax.broadcasted_iota(jnp.int32, (count, count), 1)
    fc1 = nt(jnp.where(same, 1.0, 0.0).astype(BF16), fc1_ref[...])
    two = [beside(proj[:16], pad_rows(proj[16:], 16)), beside(fc1[:48], fc1[48:]), fc2[:, :C], fc2[:, C:]]
    pack_ref[ROWS_ONE:, :] = jnp.concatenate(two, axis=0).astype(BF16)


def pack_weights(w_red, w_qkv, w_proj, w_fc1, w_fc2):
    return pl.pallas_call(
        pack_kernel,
        out_shape=jax.ShapeDtypeStruct((ROWS_ONE + ROWS_TWO, C), BF16),
    )(w_red.T, w_qkv.T, w_proj.T, w_fc1, w_fc2.T)


def each_block(place_ref):
    spot = place_ref[0]
    z, y, core = spot // 4, spot // 2 % 2, spot % 2
    for dc in range(2):
        for dy in range(2):
            for dz in range(4):
                yield dc, dz, dy, ((z ^ dz) * 2 + (y ^ dy)) * 2 + (core ^ dc)


def spots(block, stride, first, count):
    return pl.ds(pl.multiple_of(block * stride + first, 8), count)


def two_halves(place_ref, refs, dc, dz, dy):
    even = (place_ref[0] + dc) % 2 == 0
    first = place_ref[1] == 0
    blocks = []
    for dx in range(2):
        plane = 2 * dy + dx
        if plane == dz:
            blocks.append(refs[4 * dc + plane][dz].astype(F32))
        else:
            blocks.append(jnp.where(even, refs[4 * dc + plane][dz], refs[4 * dc + dz][plane]).astype(F32))
    return jnp.where(first, blocks[0], blocks[1]), jnp.where(first, blocks[1], blocks[0])


def unpack_one(place_ref, packs, red_ref, qkv_ref, red_f32, qkv_f32):
    for dc, dz, dy, block in each_block(place_ref):
        a, b = two_halves(place_ref, packs, dc, dz, dy)
        red_f32[0, spots(block, 24, 0, 24), :] = a[:24]
        red_f32[1, spots(block, 24, 0, 24), :] = b[:24]
        qkv_f32[spots(block, 72, 0, 40), :] = beside(a[24:, :C2], b[24:, :C2])
        qkv_f32[spots(block, 72, 40, 32), :] = beside(a[24:56, C2:], b[24:56, C2:])
    red_ref[...] = red_f32[...].astype(BF16)
    qkv_ref[...] = qkv_f32[...].astype(BF16)


def unpack_two(place_ref, packs, proj_ref, fc1_ref, fc2_ref, proj_f32, fc1_f32, fc2_f32):
    for dc, dz, dy, block in each_block(place_ref):
        a, b = two_halves(place_ref, packs, dc, dz, dy)
        proj_f32[spots(block, 24, 0, 16), :] = beside(a[:16, :C2], b[:16, :C2])
        proj_f32[spots(block, 24, 16, 8), :] = beside(a[:8, C2:], b[:8, C2:])
        fc1_f32[spots(block, 96, 0, 48), :] = beside(a[16:64, :C2], b[16:64, :C2])
        fc1_f32[spots(block, 96, 48, 48), :] = beside(a[16:64, C2:], b[16:64, C2:])
        for d, half in enumerate((a, b)):
            fc2_f32[spots(block, 24, 0, 24), 2 * d * C : 2 * d * C + C] = half[64:88]
            fc2_f32[spots(block, 24, 0, 24), 2 * d * C + C : 2 * d * C + 2 * C] = half[88:]
    proj_ref[...] = proj_f32[...].astype(BF16)
    fc1_ref[...] = fc1_f32[...].astype(BF16)
    fc2_ref[...] = fc2_f32[...].astype(BF16)


def put_block(place_ref, dc, dz, dy, halves, mine_ref, theirs_ref):
    first = place_ref[1] == 0
    out_ref = theirs_ref if dc else mine_ref
    count = halves[0].shape[0]
    even = (place_ref[0] + dc) % 2 == 0
    for dx in range(2):
        plane = 2 * dy + dx
        at = jnp.where(even, plane * 4 + dz, dz * 4 + plane) * count
        out_ref[pl.ds(pl.multiple_of(at, 16), count), :] = jnp.where(first, halves[dx], halves[1 - dx]).astype(BF16)


def two_terms(values):
    high = values.astype(BF16)
    return jnp.concatenate([high.astype(F32), values - high.astype(F32)], axis=0).astype(BF16)


def pack_one_grads(place_ref, red_ref, qkv_ref, small, mine_ref, theirs_ref):
    for dc, dz, dy, block in each_block(place_ref):
        top, low = qkv_ref[spots(block, 72, 0, 40), :], pad_rows(qkv_ref[spots(block, 72, 40, 32), :], 40)
        halves = []
        for d in range(2):
            lanes = slice(d * C2, d * C2 + C2)
            red = red_ref[d, spots(block, 24, 0, 24), :]
            halves.append(jnp.concatenate([red, beside(top[:, lanes], low[:, lanes])], axis=0))
        put_block(place_ref, dc, dz, dy, halves, mine_ref, theirs_ref)
    theirs_ref[16 * ROWS_ONE :, :] = two_terms(small)


def pack_two_grads(place_ref, proj_ref, fc1_ref, fc2_ref, small, mine_ref, theirs_ref):
    for dc, dz, dy, block in each_block(place_ref):
        proj_top, proj_low = proj_ref[spots(block, 24, 0, 16), :], pad_rows(proj_ref[spots(block, 24, 16, 8), :], 16)
        fc1_top, fc1_low = fc1_ref[spots(block, 96, 0, 48), :], fc1_ref[spots(block, 96, 48, 48), :]
        fc2 = fc2_ref[spots(block, 24, 0, 24), :]
        halves = []
        for d in range(2):
            lanes = slice(d * C2, d * C2 + C2)
            parts = [beside(proj_top[:, lanes], proj_low[:, lanes]), beside(fc1_top[:, lanes], fc1_low[:, lanes])]
            parts += [fc2[:, 2 * d * C : 2 * d * C + C], fc2[:, 2 * d * C + C : 2 * d * C + 2 * C]]
            halves.append(jnp.concatenate(parts, axis=0))
        put_block(place_ref, dc, dz, dy, halves, mine_ref, theirs_ref)
    theirs_ref[16 * ROWS_TWO :, :] = two_terms(small)


def small_sum(small, refs, first, count):
    for ref in refs:
        small = small + (ref[first : first + count, :].astype(F32) + ref[first + count : first + 2 * count, :].astype(F32))
    return small


def core_sum_kernel(rows, count, mine_ref, other_ref, small_ref, own_ref, small_out_ref, *send_refs):
    small = small_sum(small_ref[...], [other_ref], 16 * rows, count)
    small_out_ref[...] = small
    for k in range(4):
        at = slice(4 * k * rows, 4 * k * rows + 4 * rows)
        total = mine_ref[at, :].astype(F32) + other_ref[at, :].astype(F32)
        if k == 0:
            own_ref[...] = total
        else:
            send_refs[k - 1][: 4 * rows, :] = total.astype(BF16)
            send_refs[k - 1][4 * rows :, :] = two_terms(small)


def plane_sum_kernel(rows, count, own_ref, small_ref, *refs):
    got, own_out_ref, small_out_ref, send_refs = refs[:3], refs[3], refs[4], refs[5:]
    small = small_sum(small_ref[...], got, 4 * rows, count)
    small_out_ref[...] = small
    for k in range(4):
        at = slice(k * rows, k * rows + rows)
        total = own_ref[at, :]
        for ref in got:
            total = total + ref[at, :].astype(F32)
        if k == 0:
            own_out_ref[...] = total
        else:
            send_refs[k - 1][:rows, :] = total.astype(BF16)
            send_refs[k - 1][rows:, :] = two_terms(small)


def line_sum(rows, count, own_ref, small_ref, got):
    total = own_ref[...]
    for ref in got:
        total = total + ref[:rows, :].astype(F32)
    return total, small_sum(small_ref[...], got, rows, count)


def finish_one_kernel(own_ref, small_ref, g1, g2, g3, red_ref, qkv_ref, rgain_ref, rshift_ref, gain_ref, shift_ref, bqkv_ref, table_ref):
    rows, small = line_sum(ROWS_ONE, SMALL_ONE, own_ref, small_ref, (g1, g2, g3))
    red_ref[...] = rows[:24]
    qkv_ref[...] = jnp.concatenate([rows[24:, :C2], rows[24:56, C2:]], axis=0)
    for at, ref in ((0, rgain_ref), (2, rshift_ref), (4, gain_ref), (5, shift_ref), (6, bqkv_ref)):
        for k in range(ref.shape[0] // C):
            ref[pl.ds(k * C, C)] = small[at + k]
    table_ref[: HEADS // 2, :] = small[9:15, :169]
    table_ref[HEADS // 2 :, :] = small[9:15, C2 : C2 + 169]


def finish_two_kernel(near_ref, far_ref, own_ref, small_ref, g1, g2, g3, grad_input_ref, proj_ref, fc1_ref, fc2_ref, bfc1_ref, bproj_ref, gain_ref, shift_ref, bfc2_ref):
    grad_input_ref[...] = near_ref[...] + far_ref[...]
    rows, small = line_sum(ROWS_TWO, SMALL_TWO, own_ref, small_ref, (g1, g2, g3))
    proj_ref[...] = jnp.concatenate([rows[:16, :C2], rows[:8, C2:]], axis=0)
    fc1_ref[...] = jnp.concatenate([rows[16:64, :C2], rows[16:64, C2:]], axis=0).T
    fc2_ref[...] = beside(rows[64:88], rows[88:])
    for at, ref in ((0, bfc1_ref), (4, bproj_ref), (5, gain_ref), (6, shift_ref), (7, bfc2_ref)):
        for k in range(ref.shape[0] // C):
            ref[pl.ds(k * C, C)] = small[at + k]


def merge_norm_kernel(
    place_ref, table_ref, section_ref, incoming_ref, normal_ref, inverse_ref, bias_ref,
    parts_ref, wide_ref, reach_ref,
):
    @pl.when(pl.program_id(0) == 0)
    def _():
        wide_ref[...] = jnp.zeros_like(wide_ref)
        wide_ref[:, :169] = table_ref[...]
        reach_ref[...] = reach_of()

    bias_part(pl.program_id(0), wide_ref, reach_ref, bias_ref)
    is_left = place_ref[0] % 2 == 0
    split = split_of(place_ref[0] % 2)
    bands = []
    for r in range(14):
        own, other = section_ref[0, r % 7], incoming_ref[0, r % 7]
        bands.append(jnp.where(is_left, own, other) if r < 7 else jnp.where(is_left, other, own))
    for r in range(7):
        apart = nt(split, jnp.concatenate(bands[2 * r : 2 * r + 2], axis=0))
        parts_ref[0, r * 56 : r * 56 + 56, :] = apart[:56]
        parts_ref[1, r * 56 : r * 56 + 56, :] = apart[56:]
    total = jnp.sum(parts_ref[0] + parts_ref[1], -1, keepdims=True)
    shifted = [parts_ref[d] - total * (1.0 / (2 * C)) for d in range(2)]
    spread = jnp.sum(shifted[0] * shifted[0] + shifted[1] * shifted[1], -1, keepdims=True)
    inverse = lax.rsqrt(spread * (1.0 / (2 * C)) + EPSILON)
    inverse_ref[0] = inverse
    for d in range(2):
        normal_ref[0, d] = shifted[d] * inverse


def reach_of():
    at = lax.broadcasted_iota(jnp.int32, (256, 1024), 0)
    lane = lax.broadcasted_iota(jnp.int32, (256, 1024), 1)
    query = at & (SLOT - 1)
    target = (at >> 6) * 256 + 84 + query + 6 * ((query * 37) >> 8)
    return jnp.where((lane == target) & (query < 49), 1.0, 0.0).astype(BF16)


def ungroup_of():
    at = lax.broadcasted_iota(jnp.int32, (SLOT, SLOT), 0)
    lane = lax.broadcasted_iota(jnp.int32, (SLOT, SLOT), 1)
    return jnp.where((lane == at + ((at * 37) >> 8)) & (at < 49), 1.0, 0.0).astype(BF16)


def bias_part(t, wide_ref, reach_ref, bias_ref):
    ungroup, reach = ungroup_of(), reach_ref[...]
    heads = []
    for h in range(4):
        rows = jnp.broadcast_to(wide_ref[pl.ds(4 * t + h, 1), :], (8, 256))
        rows = pltpu.roll(rows, 0, axis=1, stride=1, stride_axis=0)
        blocks = [pltpu.roll(rows, 13 * r, axis=1) if r else rows for r in range(7)]
        heads.append(jnp.concatenate(blocks + [jnp.zeros((8, 256), F32)], axis=0))
    rest = jnp.concatenate(heads, axis=1)
    total = jnp.where(lax.broadcasted_iota(jnp.int32, (SLOT, 256), 0) < 49, 0.0, DEAD)
    for _ in range(3):
        term = rest.astype(BF16)
        rest = rest - term.astype(F32)
        total = total + nt(nn(ungroup, term).astype(BF16), reach)
    bias_ref[0] = total


def stack_kernel(a_ref, b_ref, c_ref, d_ref, one_ref, two_ref):
    for k, ref in enumerate((a_ref, b_ref, c_ref, d_ref)):
        one_ref[k] = ref[:ROWS_ONE, :]
        two_ref[k] = ref[ROWS_ONE:, :]


def forward_kernel(direct, *refs):
    (
        place_ref, widths_ref, normal_ref, red_gain_ref, red_shift_ref, gain_ref, shift_ref,
        b_qkv_ref, bias_ref, to_window_ref, to_natural_ref, head_mask_ref,
    ) = refs[:12]
    cut = 20 if direct else 14
    packs, refs = refs[12:cut], refs[cut:]
    stream_ref, qkv_ref, soft_ref, attended_ref, w_red_ref, w_qkv_ref, turned_ref = refs[:7]
    core = place_ref[0] % 2
    if direct:
        unpack_one(place_ref, packs, w_red_ref, w_qkv_ref, *refs[7:])
    else:
        w_red_ref[...] = packs[0][...]
        w_qkv_ref[...] = packs[1][...]

    red_gain, red_shift = row(red_gain_ref), row(red_shift_ref)

    def micro(m, none):
        stream = 0.0
        for d in range(2):
            lanes = slice(d * C, d * C + C)
            normed = normal_ref[m, d] * red_gain[:, lanes] + red_shift[:, lanes]
            stream = stream + nt(normed.astype(BF16), w_red_ref[d])
        stream_ref[m] = stream
        normal, _ = norm_of(stream)
        first = (normal * row(gain_ref) + row(shift_ref)).astype(BF16)
        first = nn(to_window_ref[...], first).astype(BF16)
        projected = nt(first, w_qkv_ref[...]) + row(b_qkv_ref)
        qkv_ref[m, :, :C] = (projected[:, :C] * (HD**-0.5)).astype(BF16)
        qkv_ref[m, :, C:] = projected[:, C:].astype(BF16)
        width = widths_ref[m]
        key_col = key_column((SLOT, 128))

        def pair(i, carry):
            head_mask = head_mask_ref[...]
            outs = [[None, None] for _ in range(HEADS)]
            for j in range(2):
                w = 2 * i + j
                rows = pl.ds(pl.multiple_of(w * SLOT, SLOT), SLOT)
                live = jnp.where(key_col + (core * 56 + w * 7) < width, 0.0, DEAD)
                for t in range(3):
                    q = qkv_ref[m, rows, 128 * t : 128 * t + 128]
                    k = qkv_ref[m, rows, C + 128 * t : C + 128 * t + 128]
                    v = qkv_ref[m, rows, 2 * C + 128 * t : 2 * C + 128 * t + 128]
                    scores = nt(k, four_heads(q, head_mask)) + bias_ref[t]
                    parts = []
                    for half in range(2):
                        part = scores[:, 128 * half : 128 * half + 128] + live
                        exponent = jnp.exp(part - jnp.max(part, 0, keepdims=True))
                        share = 1.0 / jnp.sum(exponent, 0, keepdims=True)
                        parts.append((exponent * share).astype(BF16))
                    soft = jnp.concatenate(parts, axis=1)
                    soft_ref[m, w, t] = soft
                    for h, block in enumerate(own_blocks(tn(v, soft))):
                        outs[4 * t + h][j] = block
            lanes = pl.ds(pl.multiple_of(i * 128, 128), 128)
            for h in range(HEADS):
                turned_ref[HD * h : HD * h + HD, lanes] = beside(*outs[h]).astype(BF16)
            return carry

        lax.fori_loop(0, WH // 2, pair, 0, unroll=UNROLL)
        attended_ref[m] = nt(to_natural_ref[...], turned_ref[...]).astype(BF16)
        return none

    lax.fori_loop(0, MB, micro, 0, unroll=MICRO_UNROLL)


def feed_kernel(direct, *refs):
    (
        place_ref, widths_ref, stream_ref, attended_ref, cotangent_ref,
        b_proj_ref, gain_ref, shift_ref, b_fc1_ref, b_fc2_ref,
    ) = refs[:10]
    cut = 18 if direct else 13
    packs, refs = refs[10:cut], refs[cut:]
    output_ref, grad_middle_ref, grad_att_ref, small_ref = refs[:4]
    if direct:
        mine_ref, theirs_ref, g_proj_ref, g_fc1_ref, g_fc2_ref = refs[4:9]
        refs = refs[9:]
    else:
        g_proj_ref, g_fc1_ref, g_fc2_ref = refs[4:7]
        refs = refs[7:]
    second_ref, grad_feed_ref, grad_second_ref, inverse_ref, bias_fc1_ref, g_bfc1_ref, w_proj_ref, w_fc1_ref, w_fc2_ref = refs
    place_col = column_of((TOK, 1), 56, 1171, 16) + (place_ref[0] % 2) * 56
    keep = jnp.concatenate([jnp.where(place_col < widths_ref[m], 1.0, 0.0) for m in range(MB)], axis=0)

    if direct:
        unpack_two(place_ref, packs, w_proj_ref, w_fc1_ref, w_fc2_ref, g_proj_ref, g_fc1_ref, g_fc2_ref)
    else:
        w_proj_ref[...] = packs[0][...]
        w_fc1_ref[...] = packs[1][...]
        w_fc2_ref[...] = packs[2][...]
    bias_fc1_ref[...] = row(b_fc1_ref)
    middle = stream_ref[...] + nt(attended_ref[...], w_proj_ref[...]) + row(b_proj_ref)
    normal, inverse = norm_of(middle)
    inverse_ref[...] = inverse
    grad_middle_ref[...] = normal
    second_ref[...] = (normal * row(gain_ref) + row(shift_ref)).astype(BF16)
    grad_feed = (cotangent_ref[...] * keep).astype(BF16)
    grad_feed_ref[...] = grad_feed
    small_ref[7:8] = jnp.sum(grad_feed.astype(F32), 0, keepdims=True)
    output_ref[...] = middle + row(b_fc2_ref)
    grad_second_ref[...] = jnp.zeros_like(grad_second_ref)

    for at in range(0, FF, CHUNK):
        units = slice(at, at + CHUNK)
        w_fc1 = w_fc1_ref[units, :]
        w_fc2 = w_fc2_ref[:, units]
        second = second_ref[...]
        feed = grad_feed_ref[...]
        pre = nt(second, w_fc1) + bias_fc1_ref[:, units]
        cdf = 0.5 * (1.0 + lax.erf(pre * 0.7071067811865476))
        density = 0.3989422804014327 * jnp.exp(-0.5 * pre * pre)
        act = (pre * cdf).astype(BF16)
        output_ref[...] += nt(act, w_fc2)
        g_fc2_ref[:, units] = tn(feed, act)
        grad_pre = (nn(feed, w_fc2) * (cdf + pre * density)).astype(BF16)
        g_bfc1_ref[:, units] = jnp.sum(grad_pre.astype(F32), 0, keepdims=True)
        g_fc1_ref[units, :] = tn(grad_pre, second)
        grad_second_ref[...] += nn(grad_pre, w_fc1)

    output_ref[...] = output_ref[...] * keep
    grad_norm, g_gain, g_shift = norm_back(grad_second_ref[...], grad_middle_ref[...], inverse_ref[...], row(gain_ref))
    small_ref[5:6] = g_gain
    small_ref[6:7] = g_shift
    grad_middle = cotangent_ref[...] * keep + grad_norm
    grad_middle_ref[...] = grad_middle
    branch = grad_middle.astype(BF16)
    small_ref[4:5] = jnp.sum(branch.astype(F32), 0, keepdims=True)
    g_proj_ref[...] = tn(branch, attended_ref[...])
    grad_att_ref[...] = nn(branch, w_proj_ref[...]).astype(BF16)
    for k in range(4):
        small_ref[k : k + 1] = g_bfc1_ref[:, k * C : k * C + C]
    if direct:
        pack_two_grads(place_ref, g_proj_ref, g_fc1_ref, g_fc2_ref, small_ref[...], mine_ref, theirs_ref)


def table_rows(pairs_ref, regroup, reach):
    rows = []
    for t in range(3):
        sums = pairs_ref[t]
        high = sums.astype(BF16)
        low = (sums - high.astype(F32)).astype(BF16)
        spread = nn(nn(regroup, high).astype(BF16), reach) + nn(nn(regroup, low).astype(BF16), reach)
        for h in range(4):
            total = 0.0
            for r in range(7):
                part = spread[8 * r : 8 * r + 8, 256 * h : 256 * h + 256]
                total = total + (pltpu.roll(part, 256 - 13 * r, axis=1) if r else part)
            total = pltpu.roll(total, 249, axis=1, stride=1, stride_axis=0)
            rows.append(jnp.sum(total, 0, keepdims=True))
    rows = jnp.concatenate(rows, axis=0)[:, :C2]
    return beside(rows[: HEADS // 2], rows[HEADS // 2 :])


def attention_kernel(first, last, *refs):
    to_window_ref, to_natural_ref, head_mask_ref, regroup_ref, reach_ref, qkv_ref, soft_ref, grad_att_ref = refs[:8]
    refs = refs[8:]
    if first:
        before_ref, small_in_ref, pairs_in_ref = refs[:3]
        refs = refs[3:]
    grad_projected_ref, small_ref, pairs_ref, window_ref, turned_ref, grad_window_ref = refs
    if first:
        grad_projected_ref[:first] = before_ref[...]
        small_ref[...] = small_in_ref[...]
        pairs_ref[...] = pairs_in_ref[...]
    else:
        small_ref[...] = jnp.zeros_like(small_ref)
        pairs_ref[...] = jnp.zeros_like(pairs_ref)

    def micro(m, none):
        window_ref[...] = nn(to_window_ref[...], grad_att_ref[m]).astype(BF16)

        def pair(i, carry):
            head_mask = head_mask_ref[...]
            outs = [[None, None] for _ in range(HEADS)]
            for t in range(3):
                scores_sum = 0.0
                for j in range(2):
                    w = 2 * i + j
                    rows = pl.ds(pl.multiple_of(w * SLOT, SLOT), SLOT)
                    q = qkv_ref[m, rows, 128 * t : 128 * t + 128]
                    k = qkv_ref[m, rows, C + 128 * t : C + 128 * t + 128]
                    v = qkv_ref[m, rows, 2 * C + 128 * t : 2 * C + 128 * t + 128]
                    grad = four_heads(window_ref[rows, 128 * t : 128 * t + 128], head_mask)
                    soft_low = soft_ref[m, w, t]
                    soft = soft_low.astype(F32)
                    grad_soft = nt(v, grad)
                    inner = jnp.sum(grad_soft * soft, 0, keepdims=True)
                    scores = (soft * (grad_soft - inner)).astype(BF16)
                    scores_sum = scores_sum + scores.astype(F32)
                    grad_key = nn(scores, four_heads(q, head_mask))
                    grad_value = nn(soft_low, grad)
                    grad_window_ref[rows, 128 * t : 128 * t + 128] = grad_key.astype(BF16)
                    grad_window_ref[rows, C + 128 * t : C + 128 * t + 128] = grad_value.astype(BF16)
                    for h, block in enumerate(own_blocks(tn(k, scores))):
                        outs[4 * t + h][j] = block
                pairs_ref[t] += scores_sum
            lanes = pl.ds(pl.multiple_of(i * 128, 128), 128)
            for h in range(HEADS):
                turned_ref[HD * h : HD * h + HD, lanes] = (beside(*outs[h]) * (HD**-0.5)).astype(BF16)
            return carry

        lax.fori_loop(0, WH // 2, pair, 0, unroll=UNROLL)
        to_natural = to_natural_ref[...]
        grad_query = nt(to_natural, turned_ref[...])
        grad_rest = nn(to_natural, grad_window_ref[...])
        grad_projected_ref[m, :, :C] = grad_query.astype(BF16)
        grad_projected_ref[m, :, C:] = grad_rest.astype(BF16)
        small_ref[0:1] += jnp.sum(grad_query, 0, keepdims=True)
        sums = jnp.sum(grad_rest, 0, keepdims=True)
        small_ref[1:2] += sums[:, :C]
        small_ref[2:3] += sums[:, C:]
        return none

    lax.fori_loop(first, last, micro, 0, unroll=last - first)
    if last == MB:
        small_ref[3 : 3 + HEADS // 2] = table_rows(pairs_ref, regroup_ref[...], reach_ref[...])


def reduction_kernel(direct, *refs):
    (
        place_ref, red_gain_ref, red_shift_ref, w_red_ref, gain_ref, shift_ref, w_qkv_ref,
        stream_ref, grad_middle_ref, grad_projected_ref, normal_ref, small_in_ref,
    ) = refs[:12]
    refs = refs[12:]
    grad_stream_ref, small_ref = refs[:2]
    if direct:
        mine_ref, theirs_ref, g_red_ref, g_qkv_ref, sums_ref = refs[2:]
    else:
        g_red_ref, g_qkv_ref, sums_ref = refs[2:]
    grad_projected = grad_projected_ref[...]
    normal, inverse = norm_of(stream_ref[...])
    gain = row(gain_ref)
    first = (normal * gain + row(shift_ref)).astype(BF16)
    g_qkv_ref[...] = tn(grad_projected, first)
    grad_norm, g_gain, g_shift = norm_back(nn(grad_projected, w_qkv_ref[...]), normal, inverse, gain)
    grad_stream = (grad_middle_ref[...] + grad_norm).astype(BF16)
    grad_stream_ref[...] = grad_stream
    red_gain, red_shift = row(red_gain_ref), row(red_shift_ref)
    sums_ref[...] = tn(grad_stream, jnp.ones((ALL, 128), BF16))
    column = sums_ref[:, :1]
    small_ref[...] = jnp.zeros_like(small_ref)
    small_ref[4:5] = g_gain
    small_ref[5:6] = g_shift
    small_ref[6:15] = small_in_ref[:9]
    for d in range(2):
        lanes = slice(d * C, d * C + C)
        weight = w_red_ref[d].astype(F32)
        product = sum(tn(grad_stream[m * TOK : m * TOK + TOK], normal_ref[m, d].astype(BF16)) for m in range(MB))
        small_ref[d : d + 1] = jnp.sum(weight * product, 0, keepdims=True)
        small_ref[2 + d : 3 + d] = jnp.sum(weight * column, 0, keepdims=True)
        g_red_ref[d] = product * red_gain[:, lanes] + column * red_shift[:, lanes]
    if direct:
        pack_one_grads(place_ref, g_red_ref, g_qkv_ref, small_ref[...], mine_ref, theirs_ref)


def merge_kernel(
    place_ref, red_gain_ref, w_red_ref, grad_stream_ref, normal_ref, inverse_ref, own_ref, send_ref,
    parts_ref, rows_ref,
):
    core = place_ref[0] % 2
    red_gain = row(red_gain_ref)
    grad_stream = grad_stream_ref[0]
    grads = [nn(grad_stream, w_red_ref[d]) * red_gain[:, d * C : d * C + C] for d in range(2)]
    normals = [normal_ref[0, d] for d in range(2)]
    mean_one = jnp.sum(grads[0] + grads[1], -1, keepdims=True) * (1.0 / (2 * C))
    mean_two = jnp.sum(grads[0] * normals[0] + grads[1] * normals[1], -1, keepdims=True) * (1.0 / (2 * C))
    for d in range(2):
        parts_ref[d] = inverse_ref[0] * (grads[d] - mean_one - normals[d] * mean_two)
    join = split_of(core)
    for r in range(7):
        at = slice(r * 56, r * 56 + 56)
        apart = jnp.concatenate([parts_ref[0, at, :], parts_ref[1, at, :]], axis=0).astype(BF16)
        rows = tn(apart, join).astype(BF16)
        rows_ref[2 * r], rows_ref[2 * r + 1] = rows[:C2], rows[C2:]
    is_left = core == 0
    for r in range(7):
        upper, lower = rows_ref[r], rows_ref[7 + r]
        own_ref[0, r] = jnp.where(is_left, upper, lower)
        send_ref[0, r] = jnp.where(is_left, lower, upper)


SCALARS = pl.BlockSpec(memory_space=pltpu.SMEM)


def whole(shape):
    return pl.BlockSpec(shape, lambda m: (0,) * len(shape), pipeline_mode=pl.Buffered(1))


def each(shape):
    return pl.BlockSpec((1,) + shape, lambda m: (m,) + (0,) * len(shape))


def scalar(array):
    return (array, SCALARS)


def fixed(array):
    return (array, whole(array.shape))


def stepped(array):
    return (array, each(array.shape[1:]))


def out_fixed(shape, dtype):
    return (shape, dtype, whole(shape))


def out_stepped(shape, dtype):
    return ((MB,) + shape, dtype, each(shape))


def run_kernel(kernel, ins, outs, scratch, micros, vmem, steps=MB):
    return pl.pallas_call(
        kernel,
        grid=(steps,),
        in_specs=[spec for _, spec in ins],
        out_specs=[spec for _, _, spec in outs],
        out_shape=[jax.ShapeDtypeStruct(shape, dtype) for shape, dtype, _ in outs],
        scratch_shapes=scratch,
        compiler_params=pltpu.CompilerParams(vmem_limit_bytes=vmem * MIB),
        cost_estimate=pl.CostEstimate(flops=int(micros * 1.15e9), bytes_accessed=0, transcendentals=0),
    )(*[array for array, _ in ins])


def whole_call(kernel, ins, outs):
    return pl.pallas_call(
        kernel,
        out_shape=[jax.ShapeDtypeStruct(shape, dtype) for shape, dtype in outs],
        compiler_params=pltpu.CompilerParams(vmem_limit_bytes=VMEM_SUM * MIB),
    )(*ins)


def merge_norm_call(place, table, section, incoming):
    return run_kernel(
        merge_norm_kernel,
        [
            scalar(place), fixed(table), stepped(section), stepped(incoming),
        ],
        [out_stepped((2, TOK, C), F32), out_stepped((TOK, 1), F32), out_stepped((SLOT, 256), F32)],
        [pltpu.VMEM((2, TOK, C), F32), pltpu.VMEM((HEADS, 256), F32), pltpu.VMEM((256, 1024), BF16)],
        COST_NORM,
        VMEM_NORM,
    )


def stack(blocks):
    return whole_call(stack_kernel, blocks, [((4, ROWS_ONE, C), BF16), ((4, ROWS_TWO, C), BF16)])


def forward_call(direct, const, place, widths, normal, red_gain, red_shift, gain, shift, b_qkv, bias, weights):
    return run_kernel(
        lambda *refs: forward_kernel(direct, *refs),
        [
            scalar(place), scalar(widths), fixed(normal), fixed(red_gain), fixed(red_shift), fixed(gain), fixed(shift), fixed(b_qkv), fixed(bias), fixed(const["to_window"]),
            fixed(const["to_natural"]), fixed(const["head_mask"]),
        ] + [fixed(w) for w in weights],
        [
            out_fixed((MB, TOK, C), F32),
            out_fixed((MB, WROWS, 3 * C), BF16),
            out_fixed((MB, WH, 3, SLOT, 256), BF16),
            out_fixed((MB, TOK, C), BF16),
            out_fixed((2, C, C), BF16),
            out_fixed((3 * C, C), BF16),
        ],
        [pltpu.VMEM((C, WROWS), BF16)]
        + ([pltpu.VMEM((2, C, C), F32), pltpu.VMEM((3 * C, C), F32)] if direct else []),
        COST_FORWARD,
        VMEM_FORWARD,
        1,
    )


def feed_call(direct, place, widths, stream, attended, cotangent, b_proj, gain, shift, b_fc1, b_fc2, weights):
    grads = [((C, C), F32), ((FF, C), F32), ((C, FF), F32)]
    packed = [((16 * ROWS_TWO, C), BF16), ((16 * ROWS_TWO + 2 * SMALL_TWO, C), BF16)]
    scratch = [
        pltpu.VMEM((ALL, C), BF16), pltpu.VMEM((ALL, C), BF16), pltpu.VMEM((ALL, C), F32), pltpu.VMEM((ALL, 1), F32),
        pltpu.VMEM((1, FF), F32), pltpu.VMEM((1, FF), F32),
        pltpu.VMEM((C, C), BF16), pltpu.VMEM((FF, C), BF16), pltpu.VMEM((C, FF), BF16),
    ]
    if direct:
        scratch = [pltpu.VMEM(*g) for g in grads] + scratch
    flat = lambda array: array.reshape(ALL, C)
    output, grad_middle, grad_att, *rest = run_kernel(
        lambda *refs: feed_kernel(direct, *refs),
        [
            scalar(place), scalar(widths), fixed(flat(stream)), fixed(flat(attended)), fixed(flat(cotangent)),
            fixed(b_proj), fixed(gain), fixed(shift), fixed(b_fc1), fixed(b_fc2),
        ] + [fixed(w) for w in weights],
        [
            out_fixed((ALL, C), F32),
            out_fixed((ALL, C), F32),
            out_fixed((ALL, C), BF16),
            out_fixed((SMALL_TWO, C), F32),
        ] + [out_fixed(*o) for o in (packed if direct else grads)],
        scratch,
        COST_FEED,
        VMEM_FEED,
        1,
    )
    return output, grad_middle.reshape(MB, TOK, C), grad_att.reshape(MB, TOK, C), *rest


def attention_call(const, first, last, qkv, soft, grad_att, before=()):
    return run_kernel(
        lambda *refs: attention_kernel(first, last, *refs),
        [fixed(const[n]) for n in ("to_window", "to_natural", "head_mask", "regroup", "reach")]
        + [fixed(qkv), fixed(soft), fixed(grad_att)]
        + [fixed(part) for part in before],
        [out_fixed((last, TOK, 3 * C), BF16), out_fixed((16, C), F32), out_fixed((3, SLOT, 256), F32)],
        [
            pltpu.VMEM((WROWS, C), BF16),
            pltpu.VMEM((C, WROWS), BF16),
            pltpu.VMEM((WROWS, 2 * C), BF16),
        ],
        COST_ATTENTION * (last - first) // MB,
        VMEM_ATTENTION,
        1,
    )


def reduction_call(direct, place, red_gain, red_shift, w_red, gain, shift, w_qkv, stream, grad_middle, grad_projected, normal, small):
    grads = [((2, C, C), F32), ((3 * C, C), F32)]
    packed = [((16 * ROWS_ONE, C), BF16), ((16 * ROWS_ONE + 2 * SMALL_ONE, C), BF16)]
    flat = lambda array: array.reshape(ALL, array.shape[-1])
    grad_stream, *rest = run_kernel(
        lambda *refs: reduction_kernel(direct, *refs),
        [
            scalar(place), fixed(red_gain), fixed(red_shift), fixed(w_red), fixed(gain), fixed(shift), fixed(w_qkv),
            fixed(flat(stream)), fixed(flat(grad_middle)), fixed(flat(grad_projected)), fixed(normal), fixed(small),
        ],
        [out_fixed((ALL, C), BF16), out_fixed((SMALL_ONE, C), F32)]
        + [out_fixed(*o) for o in (packed if direct else grads)],
        ([pltpu.VMEM(*g) for g in grads] if direct else []) + [pltpu.VMEM((C, 128), F32)],
        COST_REDUCTION,
        VMEM_REDUCTION,
        1,
    )
    return grad_stream.reshape(MB, TOK, C), *rest


def merge_call(place, red_gain, w_red, grad_stream, normal, inverse):
    return run_kernel(
        merge_kernel,
        [
            scalar(place), fixed(red_gain), fixed(w_red),
            stepped(grad_stream), stepped(normal), stepped(inverse),
        ],
        [out_stepped((7, C2, W2), BF16), out_stepped((7, C2, W2), BF16)],
        [pltpu.VMEM((2, TOK, C), F32), pltpu.VMEM((14, C2, W2), BF16)],
        COST_MERGE,
        VMEM_MERGE,
    )


def from_core(block):
    count = lax.axis_size("sp")
    return lax.ppermute(block, "sp", [(i, i ^ 1) for i in range(count)])


def move(block, swapped, k):
    route = []
    for spot in range(16):
        for x in range(2):
            if (spot % 2 == 0) != swapped:
                other, far = spot ^ (4 * k), x
            else:
                other, far = spot ^ (2 * PLANE[k][0]), x ^ PLANE[k][1]
            route.append((2 * spot + x, 2 * other + far))
    return lax.ppermute(block, ("sp", "dp"), route)


def others(block, swapped):
    return [move(block, swapped, k) for k in range(1, 4)]


def core_spread(mine):
    return mine + [from_core(part) for part in mine]


def after(value, *others):
    return lax.optimization_barrier((value,) + others)[0]


def core_sum(rows, count, mine, other, small):
    send = ((4 * rows + 2 * count, C), BF16)
    own, small, *sends = whole_call(
        lambda *refs: core_sum_kernel(rows, count, *refs),
        [mine, other, small],
        [((4 * rows, C), F32), ((count, C), F32), send, send, send],
    )
    return own, small, sends


def plane_sum(rows, count, own, small, got):
    send = ((rows + 2 * count, C), BF16)
    own, small, *sends = whole_call(
        lambda *refs: plane_sum_kernel(rows, count, *refs),
        [own, small, *got],
        [((rows, C), F32), ((count, C), F32), send, send, send],
    )
    return own, small, sends


def exchange(sends, swapped):
    return [move(send, swapped, k) for k, send in zip(range(1, 4), sends)]


def gather_weight(shard):
    rows = lax.all_gather(shard.T, "sp", axis=0, tiled=True)
    return lax.all_gather(rows, "dp", axis=1, tiled=True)


def scatter_grad(grad):
    share = lax.psum_scatter(grad.astype(BF16), "sp", scatter_dimension=0, tiled=True)
    share = lax.psum_scatter(share, "dp", scatter_dimension=1, tiled=True)
    return share.astype(F32).T


def shards(
    section_two, widths, red_gain, red_shift, w_red, norm1_gain, norm1_shift, w_qkv, b_qkv,
    bias_table, w_proj, b_proj, norm2_gain, norm2_shift, w_fc1, b_fc1, w_fc2, b_fc2, cotangent,
):
    direct = lax.axis_size("sp") == 16 and lax.axis_size("dp") == 2
    const = constants()
    place = jnp.stack([lax.axis_index("sp"), lax.axis_index("dp")]).astype(jnp.int32)
    widths = widths.reshape(MB)
    section = section_two.reshape(MB, 7, W2, C2).transpose(0, 1, 3, 2)
    incoming = from_core(section)
    if direct:
        pack = pack_weights(w_red, w_qkv, w_proj, w_fc1, w_fc2)
        line = [pack] + others(pack, False)
    normal, inverse, bias = merge_norm_call(place, bias_table.T, section, incoming)
    if direct:
        line[1:] = [after(part, normal) for part in line[1:]]
        column_one, column_two = stack(line)
        weights_one = core_spread([column_one] + others(column_one, True))
        plane_two = [column_two] + others(column_two, True)
    else:
        wt_red = gather_weight(w_red)
        weights_one = [jnp.stack([wt_red[:, :C], wt_red[:, C:]]), gather_weight(w_qkv)]
        weights_two = [gather_weight(w) for w in (w_proj, w_fc1, w_fc2)]
    stream, qkv, soft, attended, wt_red, wt_qkv = forward_call(
        direct, const, place, widths, normal, red_gain, red_shift, norm1_gain, norm1_shift, b_qkv, bias, weights_one,
    )
    if direct:
        plane_two[1:] = [after(part, stream) for part in plane_two[1:]]
        weights_two = core_spread(plane_two)
    output, grad_middle, grad_att, small_two, *large_two = feed_call(
        direct, place, widths, stream, attended, cotangent, b_proj, norm2_gain, norm2_shift,
        b_fc1, b_fc2, weights_two,
    )
    if direct:
        mine, theirs = large_two
        other = from_core(theirs)
    before = attention_call(const, 0, 1, qkv, soft, grad_att)
    if direct:
        own_two, small_two, sends = core_sum(ROWS_TWO, SMALL_TWO, mine, after(other, before[0]), small_two)
        got_two = exchange(sends, True)
        grad_att = after(grad_att, own_two)
    grad_projected, small, _ = attention_call(const, 1, MB, qkv, soft, grad_att, before)
    grad_stream, small_one, *large_one = reduction_call(
        direct, place, red_gain, red_shift, wt_red, norm1_gain, norm1_shift, wt_qkv, stream, grad_middle,
        grad_projected, normal, small,
    )
    if direct:
        mine, theirs = large_one
        got_two = [after(got, grad_stream) for got in got_two]
        other = from_core(after(theirs, *got_two))
        own_two, small_two, sends = plane_sum(ROWS_TWO, SMALL_TWO, own_two, small_two, got_two)
        got_two = exchange(sends, False)
        other = after(other, own_two)
        own_one, small_one, sends = core_sum(ROWS_ONE, SMALL_ONE, mine, other, small_one)
        got_one = exchange(sends, True)
        grad_stream = after(grad_stream, own_one)
    grad_own, grad_send = merge_call(place, red_gain, wt_red, grad_stream, normal, inverse)
    if direct:
        grad_send = after(grad_send, *got_one, *got_two)
    grad_far = from_core(grad_send)
    output = output.reshape(MB, 1, 1, 7, 7 * WH, C)

    if direct:
        own_one, small_one, sends = plane_sum(ROWS_ONE, SMALL_ONE, own_one, small_one, got_one)
        got_one = exchange(sends, False)
        vector = lambda n: ((n,), F32)
        grad_input, g_proj, g_fc1, g_fc2, g_bfc1, g_bproj, g_n2g, g_n2b, g_bfc2 = whole_call(
            finish_two_kernel,
            [grad_own, grad_far, own_two, small_two, *got_two],
            [(grad_own.shape, BF16), (w_proj.T.shape, F32), (w_fc1.shape, F32), (w_fc2.T.shape, F32), vector(FF)] + [vector(C)] * 4,
        )
        g_red, g_qkv, g_rgain, g_rshift, g_n1g, g_n1b, g_bqkv, g_table = whole_call(
            finish_one_kernel,
            [after(own_one, g_proj), small_one, *got_one],
            [(w_red.T.shape, F32), (w_qkv.T.shape, F32), vector(2 * C), vector(2 * C), vector(C), vector(C)]
            + [vector(3 * C), ((HEADS, 169), F32)],
        )
        grad_input = grad_input.transpose(0, 1, 3, 2).reshape(MB, 1, 7, W2, C2)
        return (
            output, grad_input, g_rgain, g_rshift, g_red.T, g_n1g, g_n1b, g_qkv.T, g_bqkv, g_table.T, g_proj.T,
            g_bproj, g_n2g, g_n2b, g_fc1, g_bfc1, g_fc2.T, g_bfc2,
        )
    g_red, g_qkv, g_proj, g_fc1, g_fc2 = (
        scatter_grad(g) for g in (jnp.concatenate([large_one[0][0], large_one[0][1]], axis=1), large_one[1], *large_two)
    )
    one, two = lax.psum((small_one, small_two), ("sp", "dp"))
    grad_input = (grad_own + grad_far).transpose(0, 1, 3, 2).reshape(MB, 1, 7, W2, C2)
    flat = lambda rows: rows.reshape(-1)
    return (
        output, grad_input, flat(one[:2]), flat(one[2:4]), g_red, one[4], one[5], g_qkv, flat(one[6:9]),
        jnp.concatenate([one[9:15, :169], one[9:15, C2 : C2 + 169]]).T, g_proj, two[4], two[5], two[6], g_fc1, flat(two[:4]), g_fc2, two[7],
    )


def solution(mesh):
    weight = P("dp", "sp")
    placed = (
        P(None, "dp", "sp", None, None), P(None, "dp"), P(), P(), weight, P(), P(), weight, P(), P(),
        weight, P(), P(), P(), weight, P(), weight, P(), P(None, "dp", "sp", None, None, None),
    )
    out_specs = (
        P(None, "dp", "sp", None, None, None), P(None, "dp", "sp", None, None), P(), P(), weight,
        P(), P(), weight, P(), P(), weight, P(), P(), P(), weight, P(), weight, P(),
    )
    return jax.shard_map(shards, mesh=mesh, in_specs=placed, out_specs=out_specs, check_vma=False)
```

```python
import jax
import jax.numpy as jnp
import numpy as np
from jax import lax
from jax.experimental import pallas as pl
from jax.experimental.pallas import tpu as pltpu
from jax.sharding import PartitionSpec as P

C2 = 192
C = 384
HEADS = 12
HD = 32
FF = 1536
MB = 3
WH = 8
TOK = 7 * 7 * WH
ALL = MB * TOK
SLOT = 64
WROWS = WH * SLOT
W2 = 4 * 7 * WH
CHUNK = 768
EPSILON = 1e-05
DEAD = -1e30
HIGHEST = lax.Precision.HIGHEST
F32 = jnp.float32
BF16 = jnp.bfloat16
UNROLL = 4
MICRO_UNROLL = 1
COST_NORM, COST_FORWARD, COST_FEED, COST_ATTENTION, COST_REDUCTION, COST_MERGE = 3, 1, 20, 10, 9, 5
MIB = 1024 * 1024
VMEM_NORM, VMEM_FORWARD, VMEM_FEED, VMEM_ATTENTION, VMEM_REDUCTION, VMEM_MERGE, VMEM_SUM = 12, 24, 34, 24, 24, 12, 10

ROWS_ONE = 64
ROWS_TWO = 112
SMALL_ONE = 16
SMALL_TWO = 8
PLANE = [(0, 0), (0, 1), (1, 0), (1, 1)]


def nn(left, right):
    return lax.dot_general(left, right, (((1,), (0,)), ((), ())), preferred_element_type=F32)


def nt(left, right):
    return lax.dot_general(left, right, (((1,), (1,)), ((), ())), preferred_element_type=F32)


def tn(left, right):
    return lax.dot_general(left, right, (((0,), (0,)), ((), ())), preferred_element_type=F32)


def constants():
    to_window = np.zeros((WROWS, TOK), np.float32)
    for w in range(WH):
        for r in range(7):
            for c in range(7):
                to_window[w * SLOT + 7 * r + c, r * 56 + 7 * w + c] = 1
    head_mask = (np.arange(256)[:, None] // SLOT == np.arange(128)[None] // HD).astype(np.float32)
    regroup = np.zeros((SLOT, SLOT), np.float32)
    reach = np.zeros((256, 1024), np.float32)
    for p in range(49):
        regroup[p // 7 * 8 + 7 - p % 7, p] = 1
        for h in range(4):
            reach[h * SLOT + p, h * 256 + 84 + 13 * (p // 7) + p % 7] = 1
    low = lambda a: jnp.asarray(a, BF16)
    return dict(
        to_window=low(to_window),
        to_natural=low(to_window.T),
        head_mask=low(head_mask),
        regroup=low(regroup),
        reach=low(reach),
    )


def column_of(shape, width, factor, shift):
    at = lax.broadcasted_iota(jnp.int32, shape, 0)
    return at - width * ((at * factor) >> shift)


def key_column(shape):
    return jnp.where(lax.broadcasted_iota(jnp.int32, shape, 0) < 49, column_of(shape, 7, 37, 8), 1 << 20)


def split_of(core):
    at = lax.broadcasted_iota(jnp.int32, (112, W2), 0)
    column = lax.broadcasted_iota(jnp.int32, (112, W2), 1) - core * 112
    return jnp.where(column == jnp.where(at < 56, 2 * at, 2 * at - 111), 1.0, 0.0).astype(BF16)


def row(ref):
    return ref[...].reshape(1, -1)


def norm_of(values):
    center = jnp.mean(values, -1, keepdims=True)
    shifted = values - center
    inverse = lax.rsqrt(jnp.mean(shifted * shifted, -1, keepdims=True) + EPSILON)
    return shifted * inverse, inverse


def norm_back(grad_out, normal, inverse, gain):
    grad_normal = grad_out * gain
    grad_in = inverse * (
        grad_normal
        - jnp.mean(grad_normal, -1, keepdims=True)
        - normal * jnp.mean(grad_normal * normal, -1, keepdims=True)
    )
    return (
        grad_in,
        jnp.sum(grad_out * normal, 0, keepdims=True),
        jnp.sum(grad_out, 0, keepdims=True),
    )


def four_heads(rows, head_mask):
    return jnp.concatenate([rows] * 4, axis=0) * head_mask


def own_blocks(full):
    return [full[HD * h : HD * h + HD, SLOT * h : SLOT * h + SLOT] for h in range(4)]


def beside(upper, lower):
    return jnp.concatenate([upper, lower], axis=1)


def pad_rows(rows, count):
    return jnp.concatenate([rows, jnp.zeros((count - rows.shape[0], rows.shape[1]), F32)], axis=0)


def pack_kernel(red_ref, qkv_ref, proj_ref, fc1_ref, fc2_ref, pack_ref):
    qkv = qkv_ref[...].astype(F32)
    one = [red_ref[...].astype(F32), beside(qkv[:40], pad_rows(qkv[40:], 40))]
    pack_ref[:ROWS_ONE, :] = jnp.concatenate(one, axis=0).astype(BF16)
    proj, fc2 = proj_ref[...].astype(F32), fc2_ref[...].astype(F32)
    count = fc1_ref.shape[1]
    same = lax.broadcasted_iota(jnp.int32, (count, count), 0) == lax.broadcasted_iota(jnp.int32, (count, count), 1)
    fc1 = nt(jnp.where(same, 1.0, 0.0).astype(BF16), fc1_ref[...])
    two = [beside(proj[:16], pad_rows(proj[16:], 16)), beside(fc1[:48], fc1[48:]), fc2[:, :C], fc2[:, C:]]
    pack_ref[ROWS_ONE:, :] = jnp.concatenate(two, axis=0).astype(BF16)


def pack_weights(w_red, w_qkv, w_proj, w_fc1, w_fc2):
    return pl.pallas_call(
        pack_kernel,
        out_shape=jax.ShapeDtypeStruct((ROWS_ONE + ROWS_TWO, C), BF16),
    )(w_red.T, w_qkv.T, w_proj.T, w_fc1, w_fc2.T)


def each_block(place_ref):
    spot = place_ref[0]
    z, y, core = spot // 4, spot // 2 % 2, spot % 2
    for dc in range(2):
        for dy in range(2):
            for dz in range(4):
                yield dc, dz, dy, ((z ^ dz) * 2 + (y ^ dy)) * 2 + (core ^ dc)


def spots(block, stride, first, count):
    return pl.ds(pl.multiple_of(block * stride + first, 8), count)


def two_halves(place_ref, refs, dc, dz, dy):
    even = (place_ref[0] + dc) % 2 == 0
    first = place_ref[1] == 0
    blocks = []
    for dx in range(2):
        plane = 2 * dy + dx
        if plane == dz:
            blocks.append(refs[4 * dc + plane][dz].astype(F32))
        else:
            blocks.append(jnp.where(even, refs[4 * dc + plane][dz], refs[4 * dc + dz][plane]).astype(F32))
    return jnp.where(first, blocks[0], blocks[1]), jnp.where(first, blocks[1], blocks[0])


def unpack_one(place_ref, packs, red_ref, qkv_ref, red_f32, qkv_f32):
    for dc, dz, dy, block in each_block(place_ref):
        a, b = two_halves(place_ref, packs, dc, dz, dy)
        red_f32[0, spots(block, 24, 0, 24), :] = a[:24]
        red_f32[1, spots(block, 24, 0, 24), :] = b[:24]
        qkv_f32[spots(block, 72, 0, 40), :] = beside(a[24:, :C2], b[24:, :C2])
        qkv_f32[spots(block, 72, 40, 32), :] = beside(a[24:56, C2:], b[24:56, C2:])
    red_ref[...] = red_f32[...].astype(BF16)
    qkv_ref[...] = qkv_f32[...].astype(BF16)


def unpack_two(place_ref, packs, proj_ref, fc1_ref, fc2_ref, proj_f32, fc1_f32, fc2_f32):
    for dc, dz, dy, block in each_block(place_ref):
        a, b = two_halves(place_ref, packs, dc, dz, dy)
        proj_f32[spots(block, 24, 0, 16), :] = beside(a[:16, :C2], b[:16, :C2])
        proj_f32[spots(block, 24, 16, 8), :] = beside(a[:8, C2:], b[:8, C2:])
        fc1_f32[spots(block, 96, 0, 48), :] = beside(a[16:64, :C2], b[16:64, :C2])
        fc1_f32[spots(block, 96, 48, 48), :] = beside(a[16:64, C2:], b[16:64, C2:])
        for d, half in enumerate((a, b)):
            fc2_f32[spots(block, 24, 0, 24), 2 * d * C : 2 * d * C + C] = half[64:88]
            fc2_f32[spots(block, 24, 0, 24), 2 * d * C + C : 2 * d * C + 2 * C] = half[88:]
    proj_ref[...] = proj_f32[...].astype(BF16)
    fc1_ref[...] = fc1_f32[...].astype(BF16)
    fc2_ref[...] = fc2_f32[...].astype(BF16)


def put_block(place_ref, dc, dz, dy, halves, mine_ref, theirs_ref):
    first = place_ref[1] == 0
    out_ref = theirs_ref if dc else mine_ref
    count = halves[0].shape[0]
    even = (place_ref[0] + dc) % 2 == 0
    for dx in range(2):
        plane = 2 * dy + dx
        at = jnp.where(even, plane * 4 + dz, dz * 4 + plane) * count
        out_ref[pl.ds(pl.multiple_of(at, 16), count), :] = jnp.where(first, halves[dx], halves[1 - dx]).astype(BF16)


def two_terms(values):
    high = values.astype(BF16)
    return jnp.concatenate([high.astype(F32), values - high.astype(F32)], axis=0).astype(BF16)


def pack_one_grads(place_ref, red_ref, qkv_ref, small, mine_ref, theirs_ref):
    for dc, dz, dy, block in each_block(place_ref):
        top, low = qkv_ref[spots(block, 72, 0, 40), :], pad_rows(qkv_ref[spots(block, 72, 40, 32), :], 40)
        halves = []
        for d in range(2):
            lanes = slice(d * C2, d * C2 + C2)
            red = red_ref[d, spots(block, 24, 0, 24), :]
            halves.append(jnp.concatenate([red, beside(top[:, lanes], low[:, lanes])], axis=0))
        put_block(place_ref, dc, dz, dy, halves, mine_ref, theirs_ref)
    theirs_ref[16 * ROWS_ONE :, :] = two_terms(small)


def pack_two_grads(place_ref, proj_ref, fc1_ref, fc2_ref, small, mine_ref, theirs_ref):
    for dc, dz, dy, block in each_block(place_ref):
        proj_top, proj_low = proj_ref[spots(block, 24, 0, 16), :], pad_rows(proj_ref[spots(block, 24, 16, 8), :], 16)
        fc1_top, fc1_low = fc1_ref[spots(block, 96, 0, 48), :], fc1_ref[spots(block, 96, 48, 48), :]
        fc2 = fc2_ref[spots(block, 24, 0, 24), :]
        halves = []
        for d in range(2):
            lanes = slice(d * C2, d * C2 + C2)
            parts = [beside(proj_top[:, lanes], proj_low[:, lanes]), beside(fc1_top[:, lanes], fc1_low[:, lanes])]
            parts += [fc2[:, 2 * d * C : 2 * d * C + C], fc2[:, 2 * d * C + C : 2 * d * C + 2 * C]]
            halves.append(jnp.concatenate(parts, axis=0))
        put_block(place_ref, dc, dz, dy, halves, mine_ref, theirs_ref)
    theirs_ref[16 * ROWS_TWO :, :] = two_terms(small)


def small_sum(small, refs, first, count):
    for ref in refs:
        small = small + (ref[first : first + count, :].astype(F32) + ref[first + count : first + 2 * count, :].astype(F32))
    return small


def core_sum_kernel(rows, count, mine_ref, other_ref, small_ref, own_ref, small_out_ref, *send_refs):
    small = small_sum(small_ref[...], [other_ref], 16 * rows, count)
    small_out_ref[...] = small
    for k in range(4):
        at = slice(4 * k * rows, 4 * k * rows + 4 * rows)
        total = mine_ref[at, :].astype(F32) + other_ref[at, :].astype(F32)
        if k == 0:
            own_ref[...] = total
        else:
            send_refs[k - 1][: 4 * rows, :] = total.astype(BF16)
            send_refs[k - 1][4 * rows :, :] = two_terms(small)


def plane_sum_kernel(rows, count, own_ref, small_ref, *refs):
    got, own_out_ref, small_out_ref, send_refs = refs[:3], refs[3], refs[4], refs[5:]
    small = small_sum(small_ref[...], got, 4 * rows, count)
    small_out_ref[...] = small
    for k in range(4):
        at = slice(k * rows, k * rows + rows)
        total = own_ref[at, :]
        for ref in got:
            total = total + ref[at, :].astype(F32)
        if k == 0:
            own_out_ref[...] = total
        else:
            send_refs[k - 1][:rows, :] = total.astype(BF16)
            send_refs[k - 1][rows:, :] = two_terms(small)


def line_sum(rows, count, own_ref, small_ref, got):
    total = own_ref[...]
    for ref in got:
        total = total + ref[:rows, :].astype(F32)
    return total, small_sum(small_ref[...], got, rows, count)


def finish_one_kernel(own_ref, small_ref, g1, g2, g3, red_ref, qkv_ref, rgain_ref, rshift_ref, gain_ref, shift_ref, bqkv_ref, table_ref):
    rows, small = line_sum(ROWS_ONE, SMALL_ONE, own_ref, small_ref, (g1, g2, g3))
    red_ref[...] = rows[:24]
    qkv_ref[...] = jnp.concatenate([rows[24:, :C2], rows[24:56, C2:]], axis=0)
    for at, ref in ((0, rgain_ref), (2, rshift_ref), (4, gain_ref), (5, shift_ref), (6, bqkv_ref)):
        for k in range(ref.shape[0] // C):
            ref[pl.ds(k * C, C)] = small[at + k]
    table_ref[: HEADS // 2, :] = small[9:15, :169]
    table_ref[HEADS // 2 :, :] = small[9:15, C2 : C2 + 169]


def finish_two_kernel(near_ref, far_ref, own_ref, small_ref, g1, g2, g3, grad_input_ref, proj_ref, fc1_ref, fc2_ref, bfc1_ref, bproj_ref, gain_ref, shift_ref, bfc2_ref):
    grad_input_ref[...] = near_ref[...] + far_ref[...]
    rows, small = line_sum(ROWS_TWO, SMALL_TWO, own_ref, small_ref, (g1, g2, g3))
    proj_ref[...] = jnp.concatenate([rows[:16, :C2], rows[:8, C2:]], axis=0)
    fc1_ref[...] = jnp.concatenate([rows[16:64, :C2], rows[16:64, C2:]], axis=0).T
    fc2_ref[...] = beside(rows[64:88], rows[88:])
    for at, ref in ((0, bfc1_ref), (4, bproj_ref), (5, gain_ref), (6, shift_ref), (7, bfc2_ref)):
        for k in range(ref.shape[0] // C):
            ref[pl.ds(k * C, C)] = small[at + k]


def merge_norm_kernel(
    place_ref, table_ref, section_ref, incoming_ref, normal_ref, inverse_ref, bias_ref,
    parts_ref, wide_ref, reach_ref,
):
    @pl.when(pl.program_id(0) == 0)
    def _():
        wide_ref[...] = jnp.zeros_like(wide_ref)
        wide_ref[:, :169] = table_ref[...]
        reach_ref[...] = reach_of()

    bias_part(pl.program_id(0), wide_ref, reach_ref, bias_ref)
    is_left = place_ref[0] % 2 == 0
    split = split_of(place_ref[0] % 2)
    bands = []
    for r in range(14):
        own, other = section_ref[0, r % 7], incoming_ref[0, r % 7]
        bands.append(jnp.where(is_left, own, other) if r < 7 else jnp.where(is_left, other, own))
    for r in range(7):
        apart = nt(split, jnp.concatenate(bands[2 * r : 2 * r + 2], axis=0))
        parts_ref[0, r * 56 : r * 56 + 56, :] = apart[:56]
        parts_ref[1, r * 56 : r * 56 + 56, :] = apart[56:]
    total = jnp.sum(parts_ref[0] + parts_ref[1], -1, keepdims=True)
    shifted = [parts_ref[d] - total * (1.0 / (2 * C)) for d in range(2)]
    spread = jnp.sum(shifted[0] * shifted[0] + shifted[1] * shifted[1], -1, keepdims=True)
    inverse = lax.rsqrt(spread * (1.0 / (2 * C)) + EPSILON)
    inverse_ref[0] = inverse
    for d in range(2):
        normal_ref[0, d] = shifted[d] * inverse


def reach_of():
    at = lax.broadcasted_iota(jnp.int32, (256, 1024), 0)
    lane = lax.broadcasted_iota(jnp.int32, (256, 1024), 1)
    query = at & (SLOT - 1)
    target = (at >> 6) * 256 + 84 + query + 6 * ((query * 37) >> 8)
    return jnp.where((lane == target) & (query < 49), 1.0, 0.0).astype(BF16)


def ungroup_of():
    at = lax.broadcasted_iota(jnp.int32, (SLOT, SLOT), 0)
    lane = lax.broadcasted_iota(jnp.int32, (SLOT, SLOT), 1)
    return jnp.where((lane == at + ((at * 37) >> 8)) & (at < 49), 1.0, 0.0).astype(BF16)


def bias_part(t, wide_ref, reach_ref, bias_ref):
    ungroup, reach = ungroup_of(), reach_ref[...]
    heads = []
    for h in range(4):
        rows = jnp.broadcast_to(wide_ref[pl.ds(4 * t + h, 1), :], (8, 256))
        rows = pltpu.roll(rows, 0, axis=1, stride=1, stride_axis=0)
        blocks = [pltpu.roll(rows, 13 * r, axis=1) if r else rows for r in range(7)]
        heads.append(jnp.concatenate(blocks + [jnp.zeros((8, 256), F32)], axis=0))
    rest = jnp.concatenate(heads, axis=1)
    total = jnp.where(lax.broadcasted_iota(jnp.int32, (SLOT, 256), 0) < 49, 0.0, DEAD)
    for _ in range(3):
        term = rest.astype(BF16)
        rest = rest - term.astype(F32)
        total = total + nt(nn(ungroup, term).astype(BF16), reach)
    bias_ref[0] = total


def stack_kernel(a_ref, b_ref, c_ref, d_ref, one_ref, two_ref):
    for k, ref in enumerate((a_ref, b_ref, c_ref, d_ref)):
        one_ref[k] = ref[:ROWS_ONE, :]
        two_ref[k] = ref[ROWS_ONE:, :]


def forward_kernel(direct, *refs):
    (
        place_ref, widths_ref, normal_ref, red_gain_ref, red_shift_ref, gain_ref, shift_ref,
        b_qkv_ref, bias_ref, to_window_ref, to_natural_ref, head_mask_ref,
    ) = refs[:12]
    cut = 20 if direct else 14
    packs, refs = refs[12:cut], refs[cut:]
    stream_ref, qkv_ref, soft_ref, attended_ref, w_red_ref, w_qkv_ref, turned_ref = refs[:7]
    core = place_ref[0] % 2
    if direct:
        unpack_one(place_ref, packs, w_red_ref, w_qkv_ref, *refs[7:])
    else:
        w_red_ref[...] = packs[0][...]
        w_qkv_ref[...] = packs[1][...]

    red_gain, red_shift = row(red_gain_ref), row(red_shift_ref)

    def micro(m, none):
        stream = 0.0
        for d in range(2):
            lanes = slice(d * C, d * C + C)
            normed = normal_ref[m, d] * red_gain[:, lanes] + red_shift[:, lanes]
            stream = stream + nt(normed.astype(BF16), w_red_ref[d])
        stream_ref[m] = stream
        normal, _ = norm_of(stream)
        first = (normal * row(gain_ref) + row(shift_ref)).astype(BF16)
        first = nn(to_window_ref[...], first).astype(BF16)
        projected = nt(first, w_qkv_ref[...]) + row(b_qkv_ref)
        qkv_ref[m, :, :C] = (projected[:, :C] * (HD**-0.5)).astype(BF16)
        qkv_ref[m, :, C:] = projected[:, C:].astype(BF16)
        width = widths_ref[m]
        key_col = key_column((SLOT, 128))

        def pair(i, carry):
            head_mask = head_mask_ref[...]
            outs = [[None, None] for _ in range(HEADS)]
            for j in range(2):
                w = 2 * i + j
                rows = pl.ds(pl.multiple_of(w * SLOT, SLOT), SLOT)
                live = jnp.where(key_col + (core * 56 + w * 7) < width, 0.0, DEAD)
                for t in range(3):
                    q = qkv_ref[m, rows, 128 * t : 128 * t + 128]
                    k = qkv_ref[m, rows, C + 128 * t : C + 128 * t + 128]
                    v = qkv_ref[m, rows, 2 * C + 128 * t : 2 * C + 128 * t + 128]
                    scores = nt(k, four_heads(q, head_mask)) + bias_ref[t]
                    parts = []
                    for half in range(2):
                        part = scores[:, 128 * half : 128 * half + 128] + live
                        exponent = jnp.exp(part - jnp.max(part, 0, keepdims=True))
                        share = 1.0 / jnp.sum(exponent, 0, keepdims=True)
                        parts.append((exponent * share).astype(BF16))
                    soft = jnp.concatenate(parts, axis=1)
                    soft_ref[m, w, t] = soft
                    for h, block in enumerate(own_blocks(tn(v, soft))):
                        outs[4 * t + h][j] = block
            lanes = pl.ds(pl.multiple_of(i * 128, 128), 128)
            for h in range(HEADS):
                turned_ref[HD * h : HD * h + HD, lanes] = beside(*outs[h]).astype(BF16)
            return carry

        lax.fori_loop(0, WH // 2, pair, 0, unroll=UNROLL)
        attended_ref[m] = nt(to_natural_ref[...], turned_ref[...]).astype(BF16)
        return none

    lax.fori_loop(0, MB, micro, 0, unroll=MICRO_UNROLL)


def feed_kernel(direct, *refs):
    (
        place_ref, widths_ref, stream_ref, attended_ref, cotangent_ref,
        b_proj_ref, gain_ref, shift_ref, b_fc1_ref, b_fc2_ref,
    ) = refs[:10]
    cut = 18 if direct else 13
    packs, refs = refs[10:cut], refs[cut:]
    output_ref, grad_middle_ref, grad_att_ref, small_ref = refs[:4]
    if direct:
        mine_ref, theirs_ref, g_proj_ref, g_fc1_ref, g_fc2_ref = refs[4:9]
        refs = refs[9:]
    else:
        g_proj_ref, g_fc1_ref, g_fc2_ref = refs[4:7]
        refs = refs[7:]
    second_ref, grad_feed_ref, grad_second_ref, inverse_ref, bias_fc1_ref, g_bfc1_ref, w_proj_ref, w_fc1_ref, w_fc2_ref = refs
    step = pl.program_id(0)
    place_col = column_of((TOK, 1), 56, 1171, 16) + (place_ref[0] % 2) * 56
    keep = jnp.concatenate([jnp.where(place_col < widths_ref[m], 1.0, 0.0) for m in range(MB)], axis=0)

    @pl.when(step == 0)
    def _():
        if direct:
            unpack_two(place_ref, packs, w_proj_ref, w_fc1_ref, w_fc2_ref, g_proj_ref, g_fc1_ref, g_fc2_ref)
        else:
            w_proj_ref[...] = packs[0][...]
            w_fc1_ref[...] = packs[1][...]
            w_fc2_ref[...] = packs[2][...]
        bias_fc1_ref[...] = row(b_fc1_ref)
        middle = stream_ref[...] + nt(attended_ref[...], w_proj_ref[...]) + row(b_proj_ref)
        normal, inverse = norm_of(middle)
        inverse_ref[...] = inverse
        grad_middle_ref[...] = normal
        second_ref[...] = (normal * row(gain_ref) + row(shift_ref)).astype(BF16)
        grad_feed = (cotangent_ref[...] * keep).astype(BF16)
        grad_feed_ref[...] = grad_feed
        small_ref[7:8] = jnp.sum(grad_feed.astype(F32), 0, keepdims=True)
        output_ref[...] = middle + row(b_fc2_ref)
        grad_second_ref[...] = jnp.zeros_like(grad_second_ref)

    units = pl.ds(pl.multiple_of(step * CHUNK, CHUNK), CHUNK)
    w_fc1 = w_fc1_ref[units, :]
    w_fc2 = w_fc2_ref[:, units]
    second = second_ref[...]
    feed = grad_feed_ref[...]
    pre = nt(second, w_fc1) + bias_fc1_ref[:, units]
    cdf = 0.5 * (1.0 + lax.erf(pre * 0.7071067811865476))
    density = 0.3989422804014327 * jnp.exp(-0.5 * pre * pre)
    act = (pre * cdf).astype(BF16)
    output_ref[...] += nt(act, w_fc2)
    g_fc2_ref[:, units] = tn(feed, act)
    grad_pre = (nn(feed, w_fc2) * (cdf + pre * density)).astype(BF16)
    g_bfc1_ref[:, units] = jnp.sum(grad_pre.astype(F32), 0, keepdims=True)
    g_fc1_ref[units, :] = tn(grad_pre, second)
    grad_second_ref[...] += nn(grad_pre, w_fc1)

    @pl.when(step == FF // CHUNK - 1)
    def _():
        output_ref[...] = output_ref[...] * keep
        grad_norm, g_gain, g_shift = norm_back(grad_second_ref[...], grad_middle_ref[...], inverse_ref[...], row(gain_ref))
        small_ref[5:6] = g_gain
        small_ref[6:7] = g_shift
        grad_middle = cotangent_ref[...] * keep + grad_norm
        grad_middle_ref[...] = grad_middle
        branch = grad_middle.astype(BF16)
        small_ref[4:5] = jnp.sum(branch.astype(F32), 0, keepdims=True)
        g_proj_ref[...] = tn(branch, attended_ref[...])
        grad_att_ref[...] = nn(branch, w_proj_ref[...]).astype(BF16)
        for k in range(4):
            small_ref[k : k + 1] = g_bfc1_ref[:, k * C : k * C + C]
        if direct:
            pack_two_grads(place_ref, g_proj_ref, g_fc1_ref, g_fc2_ref, small_ref[...], mine_ref, theirs_ref)


def table_rows(pairs_ref, regroup, reach):
    rows = []
    for t in range(3):
        sums = pairs_ref[t]
        high = sums.astype(BF16)
        low = (sums - high.astype(F32)).astype(BF16)
        spread = nn(nn(regroup, high).astype(BF16), reach) + nn(nn(regroup, low).astype(BF16), reach)
        for h in range(4):
            total = 0.0
            for r in range(7):
                part = spread[8 * r : 8 * r + 8, 256 * h : 256 * h + 256]
                total = total + (pltpu.roll(part, 256 - 13 * r, axis=1) if r else part)
            total = pltpu.roll(total, 249, axis=1, stride=1, stride_axis=0)
            rows.append(jnp.sum(total, 0, keepdims=True))
    rows = jnp.concatenate(rows, axis=0)[:, :C2]
    return beside(rows[: HEADS // 2], rows[HEADS // 2 :])


def attention_kernel(first, last, *refs):
    to_window_ref, to_natural_ref, head_mask_ref, regroup_ref, reach_ref, qkv_ref, soft_ref, grad_att_ref = refs[:8]
    refs = refs[8:]
    if first:
        before_ref, small_in_ref, pairs_in_ref = refs[:3]
        refs = refs[3:]
    grad_projected_ref, small_ref, pairs_ref, window_ref, turned_ref, grad_window_ref = refs
    if first:
        grad_projected_ref[:first] = before_ref[...]
        small_ref[...] = small_in_ref[...]
        pairs_ref[...] = pairs_in_ref[...]
    else:
        small_ref[...] = jnp.zeros_like(small_ref)
        pairs_ref[...] = jnp.zeros_like(pairs_ref)

    def micro(m, none):
        window_ref[...] = nn(to_window_ref[...], grad_att_ref[m]).astype(BF16)

        def pair(i, carry):
            head_mask = head_mask_ref[...]
            outs = [[None, None] for _ in range(HEADS)]
            for t in range(3):
                scores_sum = 0.0
                for j in range(2):
                    w = 2 * i + j
                    rows = pl.ds(pl.multiple_of(w * SLOT, SLOT), SLOT)
                    q = qkv_ref[m, rows, 128 * t : 128 * t + 128]
                    k = qkv_ref[m, rows, C + 128 * t : C + 128 * t + 128]
                    v = qkv_ref[m, rows, 2 * C + 128 * t : 2 * C + 128 * t + 128]
                    grad = four_heads(window_ref[rows, 128 * t : 128 * t + 128], head_mask)
                    soft_low = soft_ref[m, w, t]
                    soft = soft_low.astype(F32)
                    grad_soft = nt(v, grad)
                    inner = jnp.sum(grad_soft * soft, 0, keepdims=True)
                    scores = (soft * (grad_soft - inner)).astype(BF16)
                    scores_sum = scores_sum + scores.astype(F32)
                    grad_key = nn(scores, four_heads(q, head_mask))
                    grad_value = nn(soft_low, grad)
                    grad_window_ref[rows, 128 * t : 128 * t + 128] = grad_key.astype(BF16)
                    grad_window_ref[rows, C + 128 * t : C + 128 * t + 128] = grad_value.astype(BF16)
                    for h, block in enumerate(own_blocks(tn(k, scores))):
                        outs[4 * t + h][j] = block
                pairs_ref[t] += scores_sum
            lanes = pl.ds(pl.multiple_of(i * 128, 128), 128)
            for h in range(HEADS):
                turned_ref[HD * h : HD * h + HD, lanes] = (beside(*outs[h]) * (HD**-0.5)).astype(BF16)
            return carry

        lax.fori_loop(0, WH // 2, pair, 0, unroll=UNROLL)
        to_natural = to_natural_ref[...]
        grad_query = nt(to_natural, turned_ref[...])
        grad_rest = nn(to_natural, grad_window_ref[...])
        grad_projected_ref[m, :, :C] = grad_query.astype(BF16)
        grad_projected_ref[m, :, C:] = grad_rest.astype(BF16)
        small_ref[0:1] += jnp.sum(grad_query, 0, keepdims=True)
        sums = jnp.sum(grad_rest, 0, keepdims=True)
        small_ref[1:2] += sums[:, :C]
        small_ref[2:3] += sums[:, C:]
        return none

    lax.fori_loop(first, last, micro, 0, unroll=last - first)
    if last == MB:
        small_ref[3 : 3 + HEADS // 2] = table_rows(pairs_ref, regroup_ref[...], reach_ref[...])


def reduction_kernel(direct, *refs):
    (
        place_ref, red_gain_ref, red_shift_ref, w_red_ref, gain_ref, shift_ref, w_qkv_ref,
        stream_ref, grad_middle_ref, grad_projected_ref, normal_ref, small_in_ref,
    ) = refs[:12]
    refs = refs[12:]
    grad_stream_ref, small_ref = refs[:2]
    if direct:
        mine_ref, theirs_ref, g_red_ref, g_qkv_ref, sums_ref = refs[2:]
    else:
        g_red_ref, g_qkv_ref, sums_ref = refs[2:]
    grad_projected = grad_projected_ref[...]
    normal, inverse = norm_of(stream_ref[...])
    gain = row(gain_ref)
    first = (normal * gain + row(shift_ref)).astype(BF16)
    g_qkv_ref[...] = tn(grad_projected, first)
    grad_norm, g_gain, g_shift = norm_back(nn(grad_projected, w_qkv_ref[...]), normal, inverse, gain)
    grad_stream = (grad_middle_ref[...] + grad_norm).astype(BF16)
    grad_stream_ref[...] = grad_stream
    red_gain, red_shift = row(red_gain_ref), row(red_shift_ref)
    sums_ref[...] = tn(grad_stream, jnp.ones((ALL, 128), BF16))
    column = sums_ref[:, :1]
    small_ref[...] = jnp.zeros_like(small_ref)
    small_ref[4:5] = g_gain
    small_ref[5:6] = g_shift
    small_ref[6:15] = small_in_ref[:9]
    for d in range(2):
        lanes = slice(d * C, d * C + C)
        weight = w_red_ref[d].astype(F32)
        product = sum(tn(grad_stream[m * TOK : m * TOK + TOK], normal_ref[m, d].astype(BF16)) for m in range(MB))
        small_ref[d : d + 1] = jnp.sum(weight * product, 0, keepdims=True)
        small_ref[2 + d : 3 + d] = jnp.sum(weight * column, 0, keepdims=True)
        g_red_ref[d] = product * red_gain[:, lanes] + column * red_shift[:, lanes]
    if direct:
        pack_one_grads(place_ref, g_red_ref, g_qkv_ref, small_ref[...], mine_ref, theirs_ref)


def merge_kernel(
    place_ref, red_gain_ref, w_red_ref, grad_stream_ref, normal_ref, inverse_ref, own_ref, send_ref,
    parts_ref, rows_ref,
):
    core = place_ref[0] % 2
    red_gain = row(red_gain_ref)
    grad_stream = grad_stream_ref[0]
    grads = [nn(grad_stream, w_red_ref[d]) * red_gain[:, d * C : d * C + C] for d in range(2)]
    normals = [normal_ref[0, d] for d in range(2)]
    mean_one = jnp.sum(grads[0] + grads[1], -1, keepdims=True) * (1.0 / (2 * C))
    mean_two = jnp.sum(grads[0] * normals[0] + grads[1] * normals[1], -1, keepdims=True) * (1.0 / (2 * C))
    for d in range(2):
        parts_ref[d] = inverse_ref[0] * (grads[d] - mean_one - normals[d] * mean_two)
    join = split_of(core)
    for r in range(7):
        at = slice(r * 56, r * 56 + 56)
        apart = jnp.concatenate([parts_ref[0, at, :], parts_ref[1, at, :]], axis=0).astype(BF16)
        rows = tn(apart, join).astype(BF16)
        rows_ref[2 * r], rows_ref[2 * r + 1] = rows[:C2], rows[C2:]
    is_left = core == 0
    for r in range(7):
        upper, lower = rows_ref[r], rows_ref[7 + r]
        own_ref[0, r] = jnp.where(is_left, upper, lower)
        send_ref[0, r] = jnp.where(is_left, lower, upper)


SCALARS = pl.BlockSpec(memory_space=pltpu.SMEM)


def whole(shape):
    return pl.BlockSpec(shape, lambda m: (0,) * len(shape), pipeline_mode=pl.Buffered(1))


def each(shape):
    return pl.BlockSpec((1,) + shape, lambda m: (m,) + (0,) * len(shape))


def scalar(array):
    return (array, SCALARS)


def fixed(array):
    return (array, whole(array.shape))


def stepped(array):
    return (array, each(array.shape[1:]))


def out_fixed(shape, dtype):
    return (shape, dtype, whole(shape))


def out_stepped(shape, dtype):
    return ((MB,) + shape, dtype, each(shape))


def run_kernel(kernel, ins, outs, scratch, micros, vmem, steps=MB):
    return pl.pallas_call(
        kernel,
        grid=(steps,),
        in_specs=[spec for _, spec in ins],
        out_specs=[spec for _, _, spec in outs],
        out_shape=[jax.ShapeDtypeStruct(shape, dtype) for shape, dtype, _ in outs],
        scratch_shapes=scratch,
        compiler_params=pltpu.CompilerParams(vmem_limit_bytes=vmem * MIB),
        cost_estimate=pl.CostEstimate(flops=int(micros * 1.15e9), bytes_accessed=0, transcendentals=0),
    )(*[array for array, _ in ins])


def whole_call(kernel, ins, outs):
    return pl.pallas_call(
        kernel,
        out_shape=[jax.ShapeDtypeStruct(shape, dtype) for shape, dtype in outs],
        compiler_params=pltpu.CompilerParams(vmem_limit_bytes=VMEM_SUM * MIB),
    )(*ins)


def merge_norm_call(place, table, section, incoming):
    return run_kernel(
        merge_norm_kernel,
        [
            scalar(place), fixed(table), stepped(section), stepped(incoming),
        ],
        [out_stepped((2, TOK, C), F32), out_stepped((TOK, 1), F32), out_stepped((SLOT, 256), F32)],
        [pltpu.VMEM((2, TOK, C), F32), pltpu.VMEM((HEADS, 256), F32), pltpu.VMEM((256, 1024), BF16)],
        COST_NORM,
        VMEM_NORM,
    )


def stack(blocks):
    return whole_call(stack_kernel, blocks, [((4, ROWS_ONE, C), BF16), ((4, ROWS_TWO, C), BF16)])


def forward_call(direct, const, place, widths, normal, red_gain, red_shift, gain, shift, b_qkv, bias, weights):
    return run_kernel(
        lambda *refs: forward_kernel(direct, *refs),
        [
            scalar(place), scalar(widths), fixed(normal), fixed(red_gain), fixed(red_shift), fixed(gain), fixed(shift), fixed(b_qkv), fixed(bias), fixed(const["to_window"]),
            fixed(const["to_natural"]), fixed(const["head_mask"]),
        ] + [fixed(w) for w in weights],
        [
            out_fixed((MB, TOK, C), F32),
            out_fixed((MB, WROWS, 3 * C), BF16),
            out_fixed((MB, WH, 3, SLOT, 256), BF16),
            out_fixed((MB, TOK, C), BF16),
            out_fixed((2, C, C), BF16),
            out_fixed((3 * C, C), BF16),
        ],
        [pltpu.VMEM((C, WROWS), BF16)]
        + ([pltpu.VMEM((2, C, C), F32), pltpu.VMEM((3 * C, C), F32)] if direct else []),
        COST_FORWARD,
        VMEM_FORWARD,
        1,
    )


def feed_call(direct, place, widths, stream, attended, cotangent, b_proj, gain, shift, b_fc1, b_fc2, weights):
    grads = [((C, C), F32), ((FF, C), F32), ((C, FF), F32)]
    packed = [((16 * ROWS_TWO, C), BF16), ((16 * ROWS_TWO + 2 * SMALL_TWO, C), BF16)]
    scratch = [
        pltpu.VMEM((ALL, C), BF16), pltpu.VMEM((ALL, C), BF16), pltpu.VMEM((ALL, C), F32), pltpu.VMEM((ALL, 1), F32),
        pltpu.VMEM((1, FF), F32), pltpu.VMEM((1, FF), F32),
        pltpu.VMEM((C, C), BF16), pltpu.VMEM((FF, C), BF16), pltpu.VMEM((C, FF), BF16),
    ]
    if direct:
        scratch = [pltpu.VMEM(*g) for g in grads] + scratch
    flat = lambda array: array.reshape(ALL, C)
    output, grad_middle, grad_att, *rest = run_kernel(
        lambda *refs: feed_kernel(direct, *refs),
        [
            scalar(place), scalar(widths), fixed(flat(stream)), fixed(flat(attended)), fixed(flat(cotangent)),
            fixed(b_proj), fixed(gain), fixed(shift), fixed(b_fc1), fixed(b_fc2),
        ] + [fixed(w) for w in weights],
        [
            out_fixed((ALL, C), F32),
            out_fixed((ALL, C), F32),
            out_fixed((ALL, C), BF16),
            out_fixed((SMALL_TWO, C), F32),
        ] + [out_fixed(*o) for o in (packed if direct else grads)],
        scratch,
        COST_FEED,
        VMEM_FEED,
        FF // CHUNK,
    )
    return output, grad_middle.reshape(MB, TOK, C), grad_att.reshape(MB, TOK, C), *rest


def attention_call(const, first, last, qkv, soft, grad_att, before=()):
    return run_kernel(
        lambda *refs: attention_kernel(first, last, *refs),
        [fixed(const[n]) for n in ("to_window", "to_natural", "head_mask", "regroup", "reach")]
        + [fixed(qkv), fixed(soft), fixed(grad_att)]
        + [fixed(part) for part in before],
        [out_fixed((last, TOK, 3 * C), BF16), out_fixed((16, C), F32), out_fixed((3, SLOT, 256), F32)],
        [
            pltpu.VMEM((WROWS, C), BF16),
            pltpu.VMEM((C, WROWS), BF16),
            pltpu.VMEM((WROWS, 2 * C), BF16),
        ],
        COST_ATTENTION * (last - first) // MB,
        VMEM_ATTENTION,
        1,
    )


def reduction_call(direct, place, red_gain, red_shift, w_red, gain, shift, w_qkv, stream, grad_middle, grad_projected, normal, small):
    grads = [((2, C, C), F32), ((3 * C, C), F32)]
    packed = [((16 * ROWS_ONE, C), BF16), ((16 * ROWS_ONE + 2 * SMALL_ONE, C), BF16)]
    flat = lambda array: array.reshape(ALL, array.shape[-1])
    grad_stream, *rest = run_kernel(
        lambda *refs: reduction_kernel(direct, *refs),
        [
            scalar(place), fixed(red_gain), fixed(red_shift), fixed(w_red), fixed(gain), fixed(shift), fixed(w_qkv),
            fixed(flat(stream)), fixed(flat(grad_middle)), fixed(flat(grad_projected)), fixed(normal), fixed(small),
        ],
        [out_fixed((ALL, C), BF16), out_fixed((SMALL_ONE, C), F32)]
        + [out_fixed(*o) for o in (packed if direct else grads)],
        ([pltpu.VMEM(*g) for g in grads] if direct else []) + [pltpu.VMEM((C, 128), F32)],
        COST_REDUCTION,
        VMEM_REDUCTION,
        1,
    )
    return grad_stream.reshape(MB, TOK, C), *rest


def merge_call(place, red_gain, w_red, grad_stream, normal, inverse):
    return run_kernel(
        merge_kernel,
        [
            scalar(place), fixed(red_gain), fixed(w_red),
            stepped(grad_stream), stepped(normal), stepped(inverse),
        ],
        [out_stepped((7, C2, W2), BF16), out_stepped((7, C2, W2), BF16)],
        [pltpu.VMEM((2, TOK, C), F32), pltpu.VMEM((14, C2, W2), BF16)],
        COST_MERGE,
        VMEM_MERGE,
    )


def from_core(block):
    count = lax.axis_size("sp")
    return lax.ppermute(block, "sp", [(i, i ^ 1) for i in range(count)])


def move(block, swapped, k):
    route = []
    for spot in range(16):
        for x in range(2):
            if (spot % 2 == 0) != swapped:
                other, far = spot ^ (4 * k), x
            else:
                other, far = spot ^ (2 * PLANE[k][0]), x ^ PLANE[k][1]
            route.append((2 * spot + x, 2 * other + far))
    return lax.ppermute(block, ("sp", "dp"), route)


def others(block, swapped):
    return [move(block, swapped, k) for k in range(1, 4)]


def core_spread(mine):
    return mine + [from_core(part) for part in mine]


def after(value, *others):
    return lax.optimization_barrier((value,) + others)[0]


def core_sum(rows, count, mine, other, small):
    send = ((4 * rows + 2 * count, C), BF16)
    own, small, *sends = whole_call(
        lambda *refs: core_sum_kernel(rows, count, *refs),
        [mine, other, small],
        [((4 * rows, C), F32), ((count, C), F32), send, send, send],
    )
    return own, small, sends


def plane_sum(rows, count, own, small, got):
    send = ((rows + 2 * count, C), BF16)
    own, small, *sends = whole_call(
        lambda *refs: plane_sum_kernel(rows, count, *refs),
        [own, small, *got],
        [((rows, C), F32), ((count, C), F32), send, send, send],
    )
    return own, small, sends


def exchange(sends, swapped):
    return [move(send, swapped, k) for k, send in zip(range(1, 4), sends)]


def gather_weight(shard):
    rows = lax.all_gather(shard.T, "sp", axis=0, tiled=True)
    return lax.all_gather(rows, "dp", axis=1, tiled=True)


def scatter_grad(grad):
    share = lax.psum_scatter(grad.astype(BF16), "sp", scatter_dimension=0, tiled=True)
    share = lax.psum_scatter(share, "dp", scatter_dimension=1, tiled=True)
    return share.astype(F32).T


def shards(
    section_two, widths, red_gain, red_shift, w_red, norm1_gain, norm1_shift, w_qkv, b_qkv,
    bias_table, w_proj, b_proj, norm2_gain, norm2_shift, w_fc1, b_fc1, w_fc2, b_fc2, cotangent,
):
    direct = lax.axis_size("sp") == 16 and lax.axis_size("dp") == 2
    const = constants()
    place = jnp.stack([lax.axis_index("sp"), lax.axis_index("dp")]).astype(jnp.int32)
    widths = widths.reshape(MB)
    section = section_two.reshape(MB, 7, W2, C2).transpose(0, 1, 3, 2)
    incoming = from_core(section)
    if direct:
        pack = pack_weights(w_red, w_qkv, w_proj, w_fc1, w_fc2)
        line = [pack] + others(pack, False)
    normal, inverse, bias = merge_norm_call(place, bias_table.T, section, incoming)
    if direct:
        line[1:] = [after(part, normal) for part in line[1:]]
        column_one, column_two = stack(line)
        weights_one = core_spread([column_one] + others(column_one, True))
        plane_two = [column_two] + others(column_two, True)
    else:
        wt_red = gather_weight(w_red)
        weights_one = [jnp.stack([wt_red[:, :C], wt_red[:, C:]]), gather_weight(w_qkv)]
        weights_two = [gather_weight(w) for w in (w_proj, w_fc1, w_fc2)]
    stream, qkv, soft, attended, wt_red, wt_qkv = forward_call(
        direct, const, place, widths, normal, red_gain, red_shift, norm1_gain, norm1_shift, b_qkv, bias, weights_one,
    )
    if direct:
        plane_two[1:] = [after(part, stream) for part in plane_two[1:]]
        weights_two = core_spread(plane_two)
    output, grad_middle, grad_att, small_two, *large_two = feed_call(
        direct, place, widths, stream, attended, cotangent, b_proj, norm2_gain, norm2_shift,
        b_fc1, b_fc2, weights_two,
    )
    if direct:
        mine, theirs = large_two
        other = from_core(theirs)
    before = attention_call(const, 0, 1, qkv, soft, grad_att)
    if direct:
        own_two, small_two, sends = core_sum(ROWS_TWO, SMALL_TWO, mine, after(other, before[0]), small_two)
        got_two = exchange(sends, True)
        grad_att = after(grad_att, own_two)
    grad_projected, small, _ = attention_call(const, 1, MB, qkv, soft, grad_att, before)
    grad_stream, small_one, *large_one = reduction_call(
        direct, place, red_gain, red_shift, wt_red, norm1_gain, norm1_shift, wt_qkv, stream, grad_middle,
        grad_projected, normal, small,
    )
    if direct:
        mine, theirs = large_one
        got_two = [after(got, grad_stream) for got in got_two]
        other = from_core(after(theirs, *got_two))
        own_two, small_two, sends = plane_sum(ROWS_TWO, SMALL_TWO, own_two, small_two, got_two)
        got_two = exchange(sends, False)
        other = after(other, own_two)
        own_one, small_one, sends = core_sum(ROWS_ONE, SMALL_ONE, mine, other, small_one)
        got_one = exchange(sends, True)
        grad_stream = after(grad_stream, own_one)
    grad_own, grad_send = merge_call(place, red_gain, wt_red, grad_stream, normal, inverse)
    if direct:
        grad_send = after(grad_send, *got_one, *got_two)
    grad_far = from_core(grad_send)
    output = output.reshape(MB, 1, 1, 7, 7 * WH, C)

    if direct:
        own_one, small_one, sends = plane_sum(ROWS_ONE, SMALL_ONE, own_one, small_one, got_one)
        got_one = exchange(sends, False)
        vector = lambda n: ((n,), F32)
        grad_input, g_proj, g_fc1, g_fc2, g_bfc1, g_bproj, g_n2g, g_n2b, g_bfc2 = whole_call(
            finish_two_kernel,
            [grad_own, grad_far, own_two, small_two, *got_two],
            [(grad_own.shape, BF16), (w_proj.T.shape, F32), (w_fc1.shape, F32), (w_fc2.T.shape, F32), vector(FF)] + [vector(C)] * 4,
        )
        g_red, g_qkv, g_rgain, g_rshift, g_n1g, g_n1b, g_bqkv, g_table = whole_call(
            finish_one_kernel,
            [after(own_one, g_proj), small_one, *got_one],
            [(w_red.T.shape, F32), (w_qkv.T.shape, F32), vector(2 * C), vector(2 * C), vector(C), vector(C)]
            + [vector(3 * C), ((HEADS, 169), F32)],
        )
        grad_input = grad_input.transpose(0, 1, 3, 2).reshape(MB, 1, 7, W2, C2)
        return (
            output, grad_input, g_rgain, g_rshift, g_red.T, g_n1g, g_n1b, g_qkv.T, g_bqkv, g_table.T, g_proj.T,
            g_bproj, g_n2g, g_n2b, g_fc1, g_bfc1, g_fc2.T, g_bfc2,
        )
    g_red, g_qkv, g_proj, g_fc1, g_fc2 = (
        scatter_grad(g) for g in (jnp.concatenate([large_one[0][0], large_one[0][1]], axis=1), large_one[1], *large_two)
    )
    one, two = lax.psum((small_one, small_two), ("sp", "dp"))
    grad_input = (grad_own + grad_far).transpose(0, 1, 3, 2).reshape(MB, 1, 7, W2, C2)
    flat = lambda rows: rows.reshape(-1)
    return (
        output, grad_input, flat(one[:2]), flat(one[2:4]), g_red, one[4], one[5], g_qkv, flat(one[6:9]),
        jnp.concatenate([one[9:15, :169], one[9:15, C2 : C2 + 169]]).T, g_proj, two[4], two[5], two[6], g_fc1, flat(two[:4]), g_fc2, two[7],
    )


def solution(mesh):
    weight = P("dp", "sp")
    placed = (
        P(None, "dp", "sp", None, None), P(None, "dp"), P(), P(), weight, P(), P(), weight, P(), P(),
        weight, P(), P(), P(), weight, P(), weight, P(), P(None, "dp", "sp", None, None, None),
    )
    out_specs = (
        P(None, "dp", "sp", None, None, None), P(None, "dp", "sp", None, None), P(), P(), weight,
        P(), P(), weight, P(), P(), weight, P(), P(), P(), weight, P(), weight, P(),
    )
    return jax.shard_map(shards, mesh=mesh, in_specs=placed, out_specs=out_specs, check_vma=False)
```

```python
import jax
import jax.numpy as jnp
import numpy as np
from jax import lax
from jax.experimental import pallas as pl
from jax.experimental.pallas import tpu as pltpu
from jax.sharding import PartitionSpec as P

C2 = 192
C = 384
HEADS = 12
HD = 32
FF = 1536
MB = 3
WH = 8
TOK = 7 * 7 * WH
ALL = MB * TOK
SLOT = 64
WROWS = WH * SLOT
W2 = 4 * 7 * WH
CHUNK = 768
EPSILON = 1e-05
DEAD = -1e30
HIGHEST = lax.Precision.HIGHEST
F32 = jnp.float32
BF16 = jnp.bfloat16
UNROLL = 4
MICRO_UNROLL = 1
COST_NORM, COST_FORWARD, COST_FEED, COST_ATTENTION, COST_REDUCTION, COST_MERGE = 3, 1, 20, 10, 9, 5
MIB = 1024 * 1024
VMEM_NORM, VMEM_FORWARD, VMEM_FEED, VMEM_ATTENTION, VMEM_REDUCTION, VMEM_MERGE, VMEM_SUM = 12, 24, 34, 24, 24, 12, 10

ROWS_ONE = 64
ROWS_TWO = 112
SMALL_ONE = 16
SMALL_TWO = 8
PLANE = [(0, 0), (0, 1), (1, 0), (1, 1)]


def nn(left, right):
    return lax.dot_general(left, right, (((1,), (0,)), ((), ())), preferred_element_type=F32)


def nt(left, right):
    return lax.dot_general(left, right, (((1,), (1,)), ((), ())), preferred_element_type=F32)


def tn(left, right):
    return lax.dot_general(left, right, (((0,), (0,)), ((), ())), preferred_element_type=F32)


def constants():
    to_window = np.zeros((WROWS, TOK), np.float32)
    for w in range(WH):
        for r in range(7):
            for c in range(7):
                to_window[w * SLOT + 7 * r + c, r * 56 + 7 * w + c] = 1
    head_mask = (np.arange(256)[:, None] // SLOT == np.arange(128)[None] // HD).astype(np.float32)
    regroup = np.zeros((SLOT, SLOT), np.float32)
    reach = np.zeros((256, 1024), np.float32)
    for p in range(49):
        regroup[p // 7 * 8 + 7 - p % 7, p] = 1
        for h in range(4):
            reach[h * SLOT + p, h * 256 + 84 + 13 * (p // 7) + p % 7] = 1
    low = lambda a: jnp.asarray(a, BF16)
    return dict(
        to_window=low(to_window),
        to_natural=low(to_window.T),
        head_mask=low(head_mask),
        regroup=low(regroup),
        reach=low(reach),
    )


def column_of(shape, width, factor, shift):
    at = lax.broadcasted_iota(jnp.int32, shape, 0)
    return at - width * ((at * factor) >> shift)


def key_column(shape):
    return jnp.where(lax.broadcasted_iota(jnp.int32, shape, 0) < 49, column_of(shape, 7, 37, 8), 1 << 20)


def split_of(core):
    at = lax.broadcasted_iota(jnp.int32, (112, W2), 0)
    column = lax.broadcasted_iota(jnp.int32, (112, W2), 1) - core * 112
    return jnp.where(column == jnp.where(at < 56, 2 * at, 2 * at - 111), 1.0, 0.0).astype(BF16)


def row(ref):
    return ref[...].reshape(1, -1)


def norm_of(values):
    center = jnp.mean(values, -1, keepdims=True)
    shifted = values - center
    inverse = lax.rsqrt(jnp.mean(shifted * shifted, -1, keepdims=True) + EPSILON)
    return shifted * inverse, inverse


def norm_back(grad_out, normal, inverse, gain):
    grad_normal = grad_out * gain
    grad_in = inverse * (
        grad_normal
        - jnp.mean(grad_normal, -1, keepdims=True)
        - normal * jnp.mean(grad_normal * normal, -1, keepdims=True)
    )
    return (
        grad_in,
        jnp.sum(grad_out * normal, 0, keepdims=True),
        jnp.sum(grad_out, 0, keepdims=True),
    )


def four_heads(rows, head_mask):
    return jnp.concatenate([rows] * 4, axis=0) * head_mask


def own_blocks(full):
    return [full[HD * h : HD * h + HD, SLOT * h : SLOT * h + SLOT] for h in range(4)]


def beside(upper, lower):
    return jnp.concatenate([upper, lower], axis=1)


def pad_rows(rows, count):
    return jnp.concatenate([rows, jnp.zeros((count - rows.shape[0], rows.shape[1]), F32)], axis=0)


def pack_kernel(red_ref, qkv_ref, proj_ref, fc1_ref, fc2_ref, pack_ref):
    qkv = qkv_ref[...].astype(F32)
    one = [red_ref[...].astype(F32), beside(qkv[:40], pad_rows(qkv[40:], 40))]
    pack_ref[:ROWS_ONE, :] = jnp.concatenate(one, axis=0).astype(BF16)
    proj, fc2 = proj_ref[...].astype(F32), fc2_ref[...].astype(F32)
    count = fc1_ref.shape[1]
    same = lax.broadcasted_iota(jnp.int32, (count, count), 0) == lax.broadcasted_iota(jnp.int32, (count, count), 1)
    fc1 = nt(jnp.where(same, 1.0, 0.0).astype(BF16), fc1_ref[...])
    two = [beside(proj[:16], pad_rows(proj[16:], 16)), beside(fc1[:48], fc1[48:]), fc2[:, :C], fc2[:, C:]]
    pack_ref[ROWS_ONE:, :] = jnp.concatenate(two, axis=0).astype(BF16)


def pack_weights(w_red, w_qkv, w_proj, w_fc1, w_fc2):
    return pl.pallas_call(
        pack_kernel,
        out_shape=jax.ShapeDtypeStruct((ROWS_ONE + ROWS_TWO, C), BF16),
    )(w_red.T, w_qkv.T, w_proj.T, w_fc1, w_fc2.T)


def each_block(place_ref):
    spot = place_ref[0]
    z, y, core = spot // 4, spot // 2 % 2, spot % 2
    for dc in range(2):
        for dy in range(2):
            for dz in range(4):
                yield dc, dz, dy, ((z ^ dz) * 2 + (y ^ dy)) * 2 + (core ^ dc)


def spots(block, stride, first, count):
    return pl.ds(pl.multiple_of(block * stride + first, 8), count)


def two_halves(place_ref, refs, dc, dz, dy):
    even = (place_ref[0] + dc) % 2 == 0
    first = place_ref[1] == 0
    blocks = []
    for dx in range(2):
        plane = 2 * dy + dx
        if plane == dz:
            blocks.append(refs[4 * dc + plane][dz].astype(F32))
        else:
            blocks.append(jnp.where(even, refs[4 * dc + plane][dz], refs[4 * dc + dz][plane]).astype(F32))
    return jnp.where(first, blocks[0], blocks[1]), jnp.where(first, blocks[1], blocks[0])


def unpack_one(place_ref, packs, red_ref, qkv_ref, red_f32, qkv_f32):
    for dc, dz, dy, block in each_block(place_ref):
        a, b = two_halves(place_ref, packs, dc, dz, dy)
        red_f32[0, spots(block, 24, 0, 24), :] = a[:24]
        red_f32[1, spots(block, 24, 0, 24), :] = b[:24]
        qkv_f32[spots(block, 72, 0, 40), :] = beside(a[24:, :C2], b[24:, :C2])
        qkv_f32[spots(block, 72, 40, 32), :] = beside(a[24:56, C2:], b[24:56, C2:])
    red_ref[...] = red_f32[...].astype(BF16)
    qkv_ref[...] = qkv_f32[...].astype(BF16)


def unpack_two(place_ref, packs, proj_ref, fc1_ref, fc2_ref, proj_f32, fc1_f32, fc2_f32):
    for dc, dz, dy, block in each_block(place_ref):
        a, b = two_halves(place_ref, packs, dc, dz, dy)
        proj_f32[spots(block, 24, 0, 16), :] = beside(a[:16, :C2], b[:16, :C2])
        proj_f32[spots(block, 24, 16, 8), :] = beside(a[:8, C2:], b[:8, C2:])
        fc1_f32[spots(block, 96, 0, 48), :] = beside(a[16:64, :C2], b[16:64, :C2])
        fc1_f32[spots(block, 96, 48, 48), :] = beside(a[16:64, C2:], b[16:64, C2:])
        for d, half in enumerate((a, b)):
            fc2_f32[spots(block, 24, 0, 24), 2 * d * C : 2 * d * C + C] = half[64:88]
            fc2_f32[spots(block, 24, 0, 24), 2 * d * C + C : 2 * d * C + 2 * C] = half[88:]
    proj_ref[...] = proj_f32[...].astype(BF16)
    fc1_ref[...] = fc1_f32[...].astype(BF16)
    fc2_ref[...] = fc2_f32[...].astype(BF16)


def put_block(place_ref, dc, dz, dy, halves, mine_ref, theirs_ref):
    first = place_ref[1] == 0
    out_ref = theirs_ref if dc else mine_ref
    count = halves[0].shape[0]
    even = (place_ref[0] + dc) % 2 == 0
    for dx in range(2):
        plane = 2 * dy + dx
        at = jnp.where(even, plane * 4 + dz, dz * 4 + plane) * count
        out_ref[pl.ds(pl.multiple_of(at, 16), count), :] = jnp.where(first, halves[dx], halves[1 - dx]).astype(BF16)


def two_terms(values):
    high = values.astype(BF16)
    return jnp.concatenate([high.astype(F32), values - high.astype(F32)], axis=0).astype(BF16)


def pack_one_grads(place_ref, red_ref, qkv_ref, small, mine_ref, theirs_ref):
    for dc, dz, dy, block in each_block(place_ref):
        top, low = qkv_ref[spots(block, 72, 0, 40), :], pad_rows(qkv_ref[spots(block, 72, 40, 32), :], 40)
        halves = []
        for d in range(2):
            lanes = slice(d * C2, d * C2 + C2)
            red = red_ref[d, spots(block, 24, 0, 24), :]
            halves.append(jnp.concatenate([red, beside(top[:, lanes], low[:, lanes])], axis=0))
        put_block(place_ref, dc, dz, dy, halves, mine_ref, theirs_ref)
    theirs_ref[16 * ROWS_ONE :, :] = two_terms(small)


def pack_two_grads(place_ref, proj_ref, fc1_ref, fc2_ref, small, mine_ref, theirs_ref):
    for dc, dz, dy, block in each_block(place_ref):
        proj_top, proj_low = proj_ref[spots(block, 24, 0, 16), :], pad_rows(proj_ref[spots(block, 24, 16, 8), :], 16)
        fc1_top, fc1_low = fc1_ref[spots(block, 96, 0, 48), :], fc1_ref[spots(block, 96, 48, 48), :]
        fc2 = fc2_ref[spots(block, 24, 0, 24), :]
        halves = []
        for d in range(2):
            lanes = slice(d * C2, d * C2 + C2)
            parts = [beside(proj_top[:, lanes], proj_low[:, lanes]), beside(fc1_top[:, lanes], fc1_low[:, lanes])]
            parts += [fc2[:, 2 * d * C : 2 * d * C + C], fc2[:, 2 * d * C + C : 2 * d * C + 2 * C]]
            halves.append(jnp.concatenate(parts, axis=0))
        put_block(place_ref, dc, dz, dy, halves, mine_ref, theirs_ref)
    theirs_ref[16 * ROWS_TWO :, :] = two_terms(small)


def small_sum(small, refs, first, count):
    for ref in refs:
        small = small + (ref[first : first + count, :].astype(F32) + ref[first + count : first + 2 * count, :].astype(F32))
    return small


def core_sum_kernel(rows, count, mine_ref, other_ref, small_ref, own_ref, small_out_ref, *send_refs):
    small = small_sum(small_ref[...], [other_ref], 16 * rows, count)
    small_out_ref[...] = small
    for k in range(4):
        at = slice(4 * k * rows, 4 * k * rows + 4 * rows)
        total = mine_ref[at, :].astype(F32) + other_ref[at, :].astype(F32)
        if k == 0:
            own_ref[...] = total
        else:
            send_refs[k - 1][: 4 * rows, :] = total.astype(BF16)
            send_refs[k - 1][4 * rows :, :] = two_terms(small)


def plane_sum_kernel(rows, count, own_ref, small_ref, *refs):
    got, own_out_ref, small_out_ref, send_refs = refs[:3], refs[3], refs[4], refs[5:]
    small = small_sum(small_ref[...], got, 4 * rows, count)
    small_out_ref[...] = small
    for k in range(4):
        at = slice(k * rows, k * rows + rows)
        total = own_ref[at, :]
        for ref in got:
            total = total + ref[at, :].astype(F32)
        if k == 0:
            own_out_ref[...] = total
        else:
            send_refs[k - 1][:rows, :] = total.astype(BF16)
            send_refs[k - 1][rows:, :] = two_terms(small)


def line_sum(rows, count, own_ref, small_ref, got):
    total = own_ref[...]
    for ref in got:
        total = total + ref[:rows, :].astype(F32)
    return total, small_sum(small_ref[...], got, rows, count)


def finish_one_kernel(own_ref, small_ref, g1, g2, g3, red_ref, qkv_ref, rgain_ref, rshift_ref, gain_ref, shift_ref, bqkv_ref, table_ref):
    rows, small = line_sum(ROWS_ONE, SMALL_ONE, own_ref, small_ref, (g1, g2, g3))
    red_ref[...] = rows[:24]
    qkv_ref[...] = jnp.concatenate([rows[24:, :C2], rows[24:56, C2:]], axis=0)
    for at, ref in ((0, rgain_ref), (2, rshift_ref), (4, gain_ref), (5, shift_ref), (6, bqkv_ref)):
        for k in range(ref.shape[0] // C):
            ref[pl.ds(k * C, C)] = small[at + k]
    table_ref[: HEADS // 2, :] = small[9:15, :169]
    table_ref[HEADS // 2 :, :] = small[9:15, C2 : C2 + 169]


def finish_two_kernel(near_ref, far_ref, own_ref, small_ref, g1, g2, g3, grad_input_ref, proj_ref, fc1_ref, fc2_ref, bfc1_ref, bproj_ref, gain_ref, shift_ref, bfc2_ref):
    grad_input_ref[...] = near_ref[...] + far_ref[...]
    rows, small = line_sum(ROWS_TWO, SMALL_TWO, own_ref, small_ref, (g1, g2, g3))
    proj_ref[...] = jnp.concatenate([rows[:16, :C2], rows[:8, C2:]], axis=0)
    fc1_ref[...] = jnp.concatenate([rows[16:64, :C2], rows[16:64, C2:]], axis=0).T
    fc2_ref[...] = beside(rows[64:88], rows[88:])
    for at, ref in ((0, bfc1_ref), (4, bproj_ref), (5, gain_ref), (6, shift_ref), (7, bfc2_ref)):
        for k in range(ref.shape[0] // C):
            ref[pl.ds(k * C, C)] = small[at + k]


def merge_norm_kernel(
    place_ref, table_ref, section_ref, incoming_ref, normal_ref, inverse_ref, bias_ref,
    parts_ref, wide_ref, reach_ref,
):
    @pl.when(pl.program_id(0) == 0)
    def _():
        wide_ref[...] = jnp.zeros_like(wide_ref)
        wide_ref[:, :169] = table_ref[...]
        reach_ref[...] = reach_of()

    bias_part(pl.program_id(0), wide_ref, reach_ref, bias_ref)
    is_left = place_ref[0] % 2 == 0
    split = split_of(place_ref[0] % 2)
    bands = []
    for r in range(14):
        own, other = section_ref[0, r % 7], incoming_ref[0, r % 7]
        bands.append(jnp.where(is_left, own, other) if r < 7 else jnp.where(is_left, other, own))
    for r in range(7):
        apart = nt(split, jnp.concatenate(bands[2 * r : 2 * r + 2], axis=0))
        parts_ref[0, r * 56 : r * 56 + 56, :] = apart[:56]
        parts_ref[1, r * 56 : r * 56 + 56, :] = apart[56:]
    total = jnp.sum(parts_ref[0] + parts_ref[1], -1, keepdims=True)
    shifted = [parts_ref[d] - total * (1.0 / (2 * C)) for d in range(2)]
    spread = jnp.sum(shifted[0] * shifted[0] + shifted[1] * shifted[1], -1, keepdims=True)
    inverse = lax.rsqrt(spread * (1.0 / (2 * C)) + EPSILON)
    inverse_ref[0] = inverse
    for d in range(2):
        normal_ref[0, d] = shifted[d] * inverse


def reach_of():
    at = lax.broadcasted_iota(jnp.int32, (256, 1024), 0)
    lane = lax.broadcasted_iota(jnp.int32, (256, 1024), 1)
    query = at & (SLOT - 1)
    target = (at >> 6) * 256 + 84 + query + 6 * ((query * 37) >> 8)
    return jnp.where((lane == target) & (query < 49), 1.0, 0.0).astype(BF16)


def ungroup_of():
    at = lax.broadcasted_iota(jnp.int32, (SLOT, SLOT), 0)
    lane = lax.broadcasted_iota(jnp.int32, (SLOT, SLOT), 1)
    return jnp.where((lane == at + ((at * 37) >> 8)) & (at < 49), 1.0, 0.0).astype(BF16)


def bias_part(t, wide_ref, reach_ref, bias_ref):
    ungroup, reach = ungroup_of(), reach_ref[...]
    heads = []
    for h in range(4):
        rows = jnp.broadcast_to(wide_ref[pl.ds(4 * t + h, 1), :], (8, 256))
        rows = pltpu.roll(rows, 0, axis=1, stride=1, stride_axis=0)
        blocks = [pltpu.roll(rows, 13 * r, axis=1) if r else rows for r in range(7)]
        heads.append(jnp.concatenate(blocks + [jnp.zeros((8, 256), F32)], axis=0))
    rest = jnp.concatenate(heads, axis=1)
    total = jnp.where(lax.broadcasted_iota(jnp.int32, (SLOT, 256), 0) < 49, 0.0, DEAD)
    for _ in range(2):
        term = rest.astype(BF16)
        rest = rest - term.astype(F32)
        total = total + nt(nn(ungroup, term).astype(BF16), reach)
    bias_ref[0] = total


def stack_kernel(a_ref, b_ref, c_ref, d_ref, one_ref, two_ref):
    for k, ref in enumerate((a_ref, b_ref, c_ref, d_ref)):
        one_ref[k] = ref[:ROWS_ONE, :]
        two_ref[k] = ref[ROWS_ONE:, :]


def forward_kernel(direct, *refs):
    (
        place_ref, widths_ref, normal_ref, red_gain_ref, red_shift_ref, gain_ref, shift_ref,
        b_qkv_ref, bias_ref, to_window_ref, to_natural_ref, head_mask_ref,
    ) = refs[:12]
    cut = 20 if direct else 14
    packs, refs = refs[12:cut], refs[cut:]
    stream_ref, qkv_ref, soft_ref, attended_ref, w_red_ref, w_qkv_ref, turned_ref = refs[:7]
    core = place_ref[0] % 2
    if direct:
        unpack_one(place_ref, packs, w_red_ref, w_qkv_ref, *refs[7:])
    else:
        w_red_ref[...] = packs[0][...]
        w_qkv_ref[...] = packs[1][...]

    red_gain, red_shift = row(red_gain_ref), row(red_shift_ref)

    def micro(m, none):
        stream = 0.0
        for d in range(2):
            lanes = slice(d * C, d * C + C)
            normed = normal_ref[m, d] * red_gain[:, lanes] + red_shift[:, lanes]
            stream = stream + nt(normed.astype(BF16), w_red_ref[d])
        stream_ref[m] = stream
        normal, _ = norm_of(stream)
        first = (normal * row(gain_ref) + row(shift_ref)).astype(BF16)
        first = nn(to_window_ref[...], first).astype(BF16)
        projected = nt(first, w_qkv_ref[...]) + row(b_qkv_ref)
        qkv_ref[m, :, :C] = (projected[:, :C] * (HD**-0.5)).astype(BF16)
        qkv_ref[m, :, C:] = projected[:, C:].astype(BF16)
        width = widths_ref[m]
        key_col = key_column((SLOT, 128))

        def pair(i, carry):
            head_mask = head_mask_ref[...]
            outs = [[None, None] for _ in range(HEADS)]
            for j in range(2):
                w = 2 * i + j
                rows = pl.ds(pl.multiple_of(w * SLOT, SLOT), SLOT)
                live = jnp.where(key_col + (core * 56 + w * 7) < width, 0.0, DEAD)
                for t in range(3):
                    q = qkv_ref[m, rows, 128 * t : 128 * t + 128]
                    k = qkv_ref[m, rows, C + 128 * t : C + 128 * t + 128]
                    v = qkv_ref[m, rows, 2 * C + 128 * t : 2 * C + 128 * t + 128]
                    scores = nt(k, four_heads(q, head_mask)) + bias_ref[t]
                    parts = []
                    for half in range(2):
                        part = scores[:, 128 * half : 128 * half + 128] + live
                        exponent = jnp.exp(part - jnp.max(part, 0, keepdims=True))
                        share = 1.0 / jnp.sum(exponent, 0, keepdims=True)
                        parts.append((exponent * share).astype(BF16))
                    soft = jnp.concatenate(parts, axis=1)
                    soft_ref[m, w, t] = soft
                    for h, block in enumerate(own_blocks(tn(v, soft))):
                        outs[4 * t + h][j] = block
            lanes = pl.ds(pl.multiple_of(i * 128, 128), 128)
            for h in range(HEADS):
                turned_ref[HD * h : HD * h + HD, lanes] = beside(*outs[h]).astype(BF16)
            return carry

        lax.fori_loop(0, WH // 2, pair, 0, unroll=UNROLL)
        attended_ref[m] = nt(to_natural_ref[...], turned_ref[...]).astype(BF16)
        return none

    lax.fori_loop(0, MB, micro, 0, unroll=MICRO_UNROLL)


def feed_kernel(direct, *refs):
    (
        place_ref, widths_ref, stream_ref, attended_ref, cotangent_ref,
        b_proj_ref, gain_ref, shift_ref, b_fc1_ref, b_fc2_ref,
    ) = refs[:10]
    cut = 18 if direct else 13
    packs, refs = refs[10:cut], refs[cut:]
    output_ref, grad_middle_ref, grad_att_ref, small_ref = refs[:4]
    if direct:
        mine_ref, theirs_ref, g_proj_ref, g_fc1_ref, g_fc2_ref = refs[4:9]
        refs = refs[9:]
    else:
        g_proj_ref, g_fc1_ref, g_fc2_ref = refs[4:7]
        refs = refs[7:]
    second_ref, grad_feed_ref, grad_second_ref, inverse_ref, bias_fc1_ref, g_bfc1_ref, w_proj_ref, w_fc1_ref, w_fc2_ref = refs
    step = pl.program_id(0)
    place_col = column_of((TOK, 1), 56, 1171, 16) + (place_ref[0] % 2) * 56
    keep = jnp.concatenate([jnp.where(place_col < widths_ref[m], 1.0, 0.0) for m in range(MB)], axis=0)

    @pl.when(step == 0)
    def _():
        if direct:
            unpack_two(place_ref, packs, w_proj_ref, w_fc1_ref, w_fc2_ref, g_proj_ref, g_fc1_ref, g_fc2_ref)
        else:
            w_proj_ref[...] = packs[0][...]
            w_fc1_ref[...] = packs[1][...]
            w_fc2_ref[...] = packs[2][...]
        bias_fc1_ref[...] = row(b_fc1_ref)
        middle = stream_ref[...] + nt(attended_ref[...], w_proj_ref[...]) + row(b_proj_ref)
        normal, inverse = norm_of(middle)
        inverse_ref[...] = inverse
        grad_middle_ref[...] = normal
        second_ref[...] = (normal * row(gain_ref) + row(shift_ref)).astype(BF16)
        grad_feed = (cotangent_ref[...] * keep).astype(BF16)
        grad_feed_ref[...] = grad_feed
        small_ref[7:8] = jnp.sum(grad_feed.astype(F32), 0, keepdims=True)
        output_ref[...] = middle + row(b_fc2_ref)
        grad_second_ref[...] = jnp.zeros_like(grad_second_ref)

    units = pl.ds(pl.multiple_of(step * CHUNK, CHUNK), CHUNK)
    w_fc1 = w_fc1_ref[units, :]
    w_fc2 = w_fc2_ref[:, units]
    second = second_ref[...]
    feed = grad_feed_ref[...]
    pre = nt(second, w_fc1) + bias_fc1_ref[:, units]
    cdf = 0.5 * (1.0 + lax.erf(pre * 0.7071067811865476))
    density = 0.3989422804014327 * jnp.exp(-0.5 * pre * pre)
    act = (pre * cdf).astype(BF16)
    output_ref[...] += nt(act, w_fc2)
    g_fc2_ref[:, units] = tn(feed, act)
    grad_pre = (nn(feed, w_fc2) * (cdf + pre * density)).astype(BF16)
    g_bfc1_ref[:, units] = jnp.sum(grad_pre.astype(F32), 0, keepdims=True)
    g_fc1_ref[units, :] = tn(grad_pre, second)
    grad_second_ref[...] += nn(grad_pre, w_fc1)

    @pl.when(step == FF // CHUNK - 1)
    def _():
        output_ref[...] = output_ref[...] * keep
        grad_norm, g_gain, g_shift = norm_back(grad_second_ref[...], grad_middle_ref[...], inverse_ref[...], row(gain_ref))
        small_ref[5:6] = g_gain
        small_ref[6:7] = g_shift
        grad_middle = cotangent_ref[...] * keep + grad_norm
        grad_middle_ref[...] = grad_middle
        branch = grad_middle.astype(BF16)
        small_ref[4:5] = jnp.sum(branch.astype(F32), 0, keepdims=True)
        g_proj_ref[...] = tn(branch, attended_ref[...])
        grad_att_ref[...] = nn(branch, w_proj_ref[...]).astype(BF16)
        for k in range(4):
            small_ref[k : k + 1] = g_bfc1_ref[:, k * C : k * C + C]
        if direct:
            pack_two_grads(place_ref, g_proj_ref, g_fc1_ref, g_fc2_ref, small_ref[...], mine_ref, theirs_ref)


def table_rows(pairs_ref, regroup, reach):
    rows = []
    for t in range(3):
        sums = pairs_ref[t]
        high = sums.astype(BF16)
        low = (sums - high.astype(F32)).astype(BF16)
        spread = nn(nn(regroup, high).astype(BF16), reach) + nn(nn(regroup, low).astype(BF16), reach)
        for h in range(4):
            total = 0.0
            for r in range(7):
                part = spread[8 * r : 8 * r + 8, 256 * h : 256 * h + 256]
                total = total + (pltpu.roll(part, 256 - 13 * r, axis=1) if r else part)
            total = pltpu.roll(total, 249, axis=1, stride=1, stride_axis=0)
            rows.append(jnp.sum(total, 0, keepdims=True))
    rows = jnp.concatenate(rows, axis=0)[:, :C2]
    return beside(rows[: HEADS // 2], rows[HEADS // 2 :])


def attention_kernel(first, last, *refs):
    to_window_ref, to_natural_ref, head_mask_ref, regroup_ref, reach_ref, qkv_ref, soft_ref, grad_att_ref = refs[:8]
    refs = refs[8:]
    if first:
        before_ref, small_in_ref, pairs_in_ref = refs[:3]
        refs = refs[3:]
    grad_projected_ref, small_ref, pairs_ref, window_ref, turned_ref, grad_window_ref = refs
    if first:
        grad_projected_ref[:first] = before_ref[...]
        small_ref[...] = small_in_ref[...]
        pairs_ref[...] = pairs_in_ref[...]
    else:
        small_ref[...] = jnp.zeros_like(small_ref)
        pairs_ref[...] = jnp.zeros_like(pairs_ref)

    def micro(m, none):
        window_ref[...] = nn(to_window_ref[...], grad_att_ref[m]).astype(BF16)

        def pair(i, carry):
            head_mask = head_mask_ref[...]
            outs = [[None, None] for _ in range(HEADS)]
            for t in range(3):
                scores_sum = 0.0
                for j in range(2):
                    w = 2 * i + j
                    rows = pl.ds(pl.multiple_of(w * SLOT, SLOT), SLOT)
                    q = qkv_ref[m, rows, 128 * t : 128 * t + 128]
                    k = qkv_ref[m, rows, C + 128 * t : C + 128 * t + 128]
                    v = qkv_ref[m, rows, 2 * C + 128 * t : 2 * C + 128 * t + 128]
                    grad = four_heads(window_ref[rows, 128 * t : 128 * t + 128], head_mask)
                    soft_low = soft_ref[m, w, t]
                    soft = soft_low.astype(F32)
                    grad_soft = nt(v, grad)
                    inner = jnp.sum(grad_soft * soft, 0, keepdims=True)
                    scores = (soft * (grad_soft - inner)).astype(BF16)
                    scores_sum = scores_sum + scores.astype(F32)
                    grad_key = nn(scores, four_heads(q, head_mask))
                    grad_value = nn(soft_low, grad)
                    grad_window_ref[rows, 128 * t : 128 * t + 128] = grad_key.astype(BF16)
                    grad_window_ref[rows, C + 128 * t : C + 128 * t + 128] = grad_value.astype(BF16)
                    for h, block in enumerate(own_blocks(tn(k, scores))):
                        outs[4 * t + h][j] = block
                pairs_ref[t] += scores_sum
            lanes = pl.ds(pl.multiple_of(i * 128, 128), 128)
            for h in range(HEADS):
                turned_ref[HD * h : HD * h + HD, lanes] = (beside(*outs[h]) * (HD**-0.5)).astype(BF16)
            return carry

        lax.fori_loop(0, WH // 2, pair, 0, unroll=UNROLL)
        to_natural = to_natural_ref[...]
        grad_query = nt(to_natural, turned_ref[...])
        grad_rest = nn(to_natural, grad_window_ref[...])
        grad_projected_ref[m, :, :C] = grad_query.astype(BF16)
        grad_projected_ref[m, :, C:] = grad_rest.astype(BF16)
        small_ref[0:1] += jnp.sum(grad_query, 0, keepdims=True)
        sums = jnp.sum(grad_rest, 0, keepdims=True)
        small_ref[1:2] += sums[:, :C]
        small_ref[2:3] += sums[:, C:]
        return none

    lax.fori_loop(first, last, micro, 0, unroll=last - first)
    if last == MB:
        small_ref[3 : 3 + HEADS // 2] = table_rows(pairs_ref, regroup_ref[...], reach_ref[...])


def reduction_kernel(direct, *refs):
    (
        place_ref, red_gain_ref, red_shift_ref, w_red_ref, gain_ref, shift_ref, w_qkv_ref,
        stream_ref, grad_middle_ref, grad_projected_ref, normal_ref, small_in_ref,
    ) = refs[:12]
    refs = refs[12:]
    grad_stream_ref, small_ref = refs[:2]
    if direct:
        mine_ref, theirs_ref, g_red_ref, g_qkv_ref, sums_ref = refs[2:]
    else:
        g_red_ref, g_qkv_ref, sums_ref = refs[2:]
    grad_projected = grad_projected_ref[...]
    normal, inverse = norm_of(stream_ref[...])
    gain = row(gain_ref)
    first = (normal * gain + row(shift_ref)).astype(BF16)
    g_qkv_ref[...] = tn(grad_projected, first)
    grad_norm, g_gain, g_shift = norm_back(nn(grad_projected, w_qkv_ref[...]), normal, inverse, gain)
    grad_stream = (grad_middle_ref[...] + grad_norm).astype(BF16)
    grad_stream_ref[...] = grad_stream
    red_gain, red_shift = row(red_gain_ref), row(red_shift_ref)
    sums_ref[...] = jnp.broadcast_to(jnp.sum(grad_stream.astype(F32), 0, keepdims=True), (8, C)).T
    column = sums_ref[:, :1]
    small_ref[...] = jnp.zeros_like(small_ref)
    small_ref[4:5] = g_gain
    small_ref[5:6] = g_shift
    small_ref[6:15] = small_in_ref[:9]
    for d in range(2):
        lanes = slice(d * C, d * C + C)
        weight = w_red_ref[d].astype(F32)
        product = sum(tn(grad_stream[m * TOK : m * TOK + TOK], normal_ref[m, d].astype(BF16)) for m in range(MB))
        small_ref[d : d + 1] = jnp.sum(weight * product, 0, keepdims=True)
        small_ref[2 + d : 3 + d] = jnp.sum(weight * column, 0, keepdims=True)
        g_red_ref[d] = product * red_gain[:, lanes] + column * red_shift[:, lanes]
    if direct:
        pack_one_grads(place_ref, g_red_ref, g_qkv_ref, small_ref[...], mine_ref, theirs_ref)


def merge_kernel(
    place_ref, red_gain_ref, w_red_ref, grad_stream_ref, normal_ref, inverse_ref, own_ref, send_ref,
    parts_ref, rows_ref,
):
    core = place_ref[0] % 2
    red_gain = row(red_gain_ref)
    grad_stream = grad_stream_ref[0]
    grads = [nn(grad_stream, w_red_ref[d]) * red_gain[:, d * C : d * C + C] for d in range(2)]
    normals = [normal_ref[0, d] for d in range(2)]
    mean_one = jnp.sum(grads[0] + grads[1], -1, keepdims=True) * (1.0 / (2 * C))
    mean_two = jnp.sum(grads[0] * normals[0] + grads[1] * normals[1], -1, keepdims=True) * (1.0 / (2 * C))
    for d in range(2):
        parts_ref[d] = inverse_ref[0] * (grads[d] - mean_one - normals[d] * mean_two)
    join = split_of(core)
    for r in range(7):
        at = slice(r * 56, r * 56 + 56)
        apart = jnp.concatenate([parts_ref[0, at, :], parts_ref[1, at, :]], axis=0).astype(BF16)
        rows = tn(apart, join).astype(BF16)
        rows_ref[2 * r], rows_ref[2 * r + 1] = rows[:C2], rows[C2:]
    is_left = core == 0
    for r in range(7):
        upper, lower = rows_ref[r], rows_ref[7 + r]
        own_ref[0, r] = jnp.where(is_left, upper, lower)
        send_ref[0, r] = jnp.where(is_left, lower, upper)


SCALARS = pl.BlockSpec(memory_space=pltpu.SMEM)


def whole(shape):
    return pl.BlockSpec(shape, lambda m: (0,) * len(shape), pipeline_mode=pl.Buffered(1))


def each(shape):
    return pl.BlockSpec((1,) + shape, lambda m: (m,) + (0,) * len(shape))


def scalar(array):
    return (array, SCALARS)


def fixed(array):
    return (array, whole(array.shape))


def stepped(array):
    return (array, each(array.shape[1:]))


def out_fixed(shape, dtype):
    return (shape, dtype, whole(shape))


def out_stepped(shape, dtype):
    return ((MB,) + shape, dtype, each(shape))


def run_kernel(kernel, ins, outs, scratch, micros, vmem, steps=MB):
    return pl.pallas_call(
        kernel,
        grid=(steps,),
        in_specs=[spec for _, spec in ins],
        out_specs=[spec for _, _, spec in outs],
        out_shape=[jax.ShapeDtypeStruct(shape, dtype) for shape, dtype, _ in outs],
        scratch_shapes=scratch,
        compiler_params=pltpu.CompilerParams(vmem_limit_bytes=vmem * MIB),
        cost_estimate=pl.CostEstimate(flops=int(micros * 1.15e9), bytes_accessed=0, transcendentals=0),
    )(*[array for array, _ in ins])


def whole_call(kernel, ins, outs):
    return pl.pallas_call(
        kernel,
        out_shape=[jax.ShapeDtypeStruct(shape, dtype) for shape, dtype in outs],
        compiler_params=pltpu.CompilerParams(vmem_limit_bytes=VMEM_SUM * MIB),
    )(*ins)


def merge_norm_call(place, table, section, incoming):
    return run_kernel(
        merge_norm_kernel,
        [
            scalar(place), fixed(table), stepped(section), stepped(incoming),
        ],
        [out_stepped((2, TOK, C), F32), out_stepped((TOK, 1), F32), out_stepped((SLOT, 256), F32)],
        [pltpu.VMEM((2, TOK, C), F32), pltpu.VMEM((HEADS, 256), F32), pltpu.VMEM((256, 1024), BF16)],
        COST_NORM,
        VMEM_NORM,
    )


def stack(blocks):
    return whole_call(stack_kernel, blocks, [((4, ROWS_ONE, C), BF16), ((4, ROWS_TWO, C), BF16)])


def forward_call(direct, const, place, widths, normal, red_gain, red_shift, gain, shift, b_qkv, bias, weights):
    return run_kernel(
        lambda *refs: forward_kernel(direct, *refs),
        [
            scalar(place), scalar(widths), fixed(normal), fixed(red_gain), fixed(red_shift), fixed(gain), fixed(shift), fixed(b_qkv), fixed(bias), fixed(const["to_window"]),
            fixed(const["to_natural"]), fixed(const["head_mask"]),
        ] + [fixed(w) for w in weights],
        [
            out_fixed((MB, TOK, C), F32),
            out_fixed((MB, WROWS, 3 * C), BF16),
            out_fixed((MB, WH, 3, SLOT, 256), BF16),
            out_fixed((MB, TOK, C), BF16),
            out_fixed((2, C, C), BF16),
            out_fixed((3 * C, C), BF16),
        ],
        [pltpu.VMEM((C, WROWS), BF16)]
        + ([pltpu.VMEM((2, C, C), F32), pltpu.VMEM((3 * C, C), F32)] if direct else []),
        COST_FORWARD,
        VMEM_FORWARD,
        1,
    )


def feed_call(direct, place, widths, stream, attended, cotangent, b_proj, gain, shift, b_fc1, b_fc2, weights):
    grads = [((C, C), F32), ((FF, C), F32), ((C, FF), F32)]
    packed = [((16 * ROWS_TWO, C), BF16), ((16 * ROWS_TWO + 2 * SMALL_TWO, C), BF16)]
    scratch = [
        pltpu.VMEM((ALL, C), BF16), pltpu.VMEM((ALL, C), BF16), pltpu.VMEM((ALL, C), F32), pltpu.VMEM((ALL, 1), F32),
        pltpu.VMEM((1, FF), F32), pltpu.VMEM((1, FF), F32),
        pltpu.VMEM((C, C), BF16), pltpu.VMEM((FF, C), BF16), pltpu.VMEM((C, FF), BF16),
    ]
    if direct:
        scratch = [pltpu.VMEM(*g) for g in grads] + scratch
    flat = lambda array: array.reshape(ALL, C)
    output, grad_middle, grad_att, *rest = run_kernel(
        lambda *refs: feed_kernel(direct, *refs),
        [
            scalar(place), scalar(widths), fixed(flat(stream)), fixed(flat(attended)), fixed(flat(cotangent)),
            fixed(b_proj), fixed(gain), fixed(shift), fixed(b_fc1), fixed(b_fc2),
        ] + [fixed(w) for w in weights],
        [
            out_fixed((ALL, C), F32),
            out_fixed((ALL, C), F32),
            out_fixed((ALL, C), BF16),
            out_fixed((SMALL_TWO, C), F32),
        ] + [out_fixed(*o) for o in (packed if direct else grads)],
        scratch,
        COST_FEED,
        VMEM_FEED,
        FF // CHUNK,
    )
    return output, grad_middle.reshape(MB, TOK, C), grad_att.reshape(MB, TOK, C), *rest


def attention_call(const, first, last, qkv, soft, grad_att, before=()):
    return run_kernel(
        lambda *refs: attention_kernel(first, last, *refs),
        [fixed(const[n]) for n in ("to_window", "to_natural", "head_mask", "regroup", "reach")]
        + [fixed(qkv), fixed(soft), fixed(grad_att)]
        + [fixed(part) for part in before],
        [out_fixed((last, TOK, 3 * C), BF16), out_fixed((16, C), F32), out_fixed((3, SLOT, 256), F32)],
        [
            pltpu.VMEM((WROWS, C), BF16),
            pltpu.VMEM((C, WROWS), BF16),
            pltpu.VMEM((WROWS, 2 * C), BF16),
        ],
        COST_ATTENTION * (last - first) // MB,
        VMEM_ATTENTION,
        1,
    )


def reduction_call(direct, place, red_gain, red_shift, w_red, gain, shift, w_qkv, stream, grad_middle, grad_projected, normal, small):
    grads = [((2, C, C), F32), ((3 * C, C), F32)]
    packed = [((16 * ROWS_ONE, C), BF16), ((16 * ROWS_ONE + 2 * SMALL_ONE, C), BF16)]
    flat = lambda array: array.reshape(ALL, array.shape[-1])
    grad_stream, *rest = run_kernel(
        lambda *refs: reduction_kernel(direct, *refs),
        [
            scalar(place), fixed(red_gain), fixed(red_shift), fixed(w_red), fixed(gain), fixed(shift), fixed(w_qkv),
            fixed(flat(stream)), fixed(flat(grad_middle)), fixed(flat(grad_projected)), fixed(normal), fixed(small),
        ],
        [out_fixed((ALL, C), BF16), out_fixed((SMALL_ONE, C), F32)]
        + [out_fixed(*o) for o in (packed if direct else grads)],
        ([pltpu.VMEM(*g) for g in grads] if direct else []) + [pltpu.VMEM((C, 8), F32)],
        COST_REDUCTION,
        VMEM_REDUCTION,
        1,
    )
    return grad_stream.reshape(MB, TOK, C), *rest


def merge_call(place, red_gain, w_red, grad_stream, normal, inverse):
    return run_kernel(
        merge_kernel,
        [
            scalar(place), fixed(red_gain), fixed(w_red),
            stepped(grad_stream), stepped(normal), stepped(inverse),
        ],
        [out_stepped((7, C2, W2), BF16), out_stepped((7, C2, W2), BF16)],
        [pltpu.VMEM((2, TOK, C), F32), pltpu.VMEM((14, C2, W2), BF16)],
        COST_MERGE,
        VMEM_MERGE,
    )


def from_core(block):
    count = lax.axis_size("sp")
    return lax.ppermute(block, "sp", [(i, i ^ 1) for i in range(count)])


def move(block, swapped, k):
    route = []
    for spot in range(16):
        for x in range(2):
            if (spot % 2 == 0) != swapped:
                other, far = spot ^ (4 * k), x
            else:
                other, far = spot ^ (2 * PLANE[k][0]), x ^ PLANE[k][1]
            route.append((2 * spot + x, 2 * other + far))
    return lax.ppermute(block, ("sp", "dp"), route)


def others(block, swapped):
    return [move(block, swapped, k) for k in range(1, 4)]


def core_spread(mine):
    return mine + [from_core(part) for part in mine]


def after(value, *others):
    return lax.optimization_barrier((value,) + others)[0]


def core_sum(rows, count, mine, other, small):
    send = ((4 * rows + 2 * count, C), BF16)
    own, small, *sends = whole_call(
        lambda *refs: core_sum_kernel(rows, count, *refs),
        [mine, other, small],
        [((4 * rows, C), F32), ((count, C), F32), send, send, send],
    )
    return own, small, sends


def plane_sum(rows, count, own, small, got):
    send = ((rows + 2 * count, C), BF16)
    own, small, *sends = whole_call(
        lambda *refs: plane_sum_kernel(rows, count, *refs),
        [own, small, *got],
        [((rows, C), F32), ((count, C), F32), send, send, send],
    )
    return own, small, sends


def exchange(sends, swapped):
    return [move(send, swapped, k) for k, send in zip(range(1, 4), sends)]


def gather_weight(shard):
    rows = lax.all_gather(shard.T, "sp", axis=0, tiled=True)
    return lax.all_gather(rows, "dp", axis=1, tiled=True)


def scatter_grad(grad):
    share = lax.psum_scatter(grad.astype(BF16), "sp", scatter_dimension=0, tiled=True)
    share = lax.psum_scatter(share, "dp", scatter_dimension=1, tiled=True)
    return share.astype(F32).T


def shards(
    section_two, widths, red_gain, red_shift, w_red, norm1_gain, norm1_shift, w_qkv, b_qkv,
    bias_table, w_proj, b_proj, norm2_gain, norm2_shift, w_fc1, b_fc1, w_fc2, b_fc2, cotangent,
):
    direct = lax.axis_size("sp") == 16 and lax.axis_size("dp") == 2
    const = constants()
    place = jnp.stack([lax.axis_index("sp"), lax.axis_index("dp")]).astype(jnp.int32)
    widths = widths.reshape(MB)
    section = section_two.reshape(MB, 7, W2, C2).transpose(0, 1, 3, 2)
    incoming = from_core(section)
    if direct:
        pack = pack_weights(w_red, w_qkv, w_proj, w_fc1, w_fc2)
        line = [pack] + others(pack, False)
    normal, inverse, bias = merge_norm_call(place, bias_table.T, section, incoming)
    if direct:
        line[1:] = [after(part, normal) for part in line[1:]]
        column_one, column_two = stack(line)
        weights_one = core_spread([column_one] + others(column_one, True))
        plane_two = [column_two] + others(column_two, True)
    else:
        wt_red = gather_weight(w_red)
        weights_one = [jnp.stack([wt_red[:, :C], wt_red[:, C:]]), gather_weight(w_qkv)]
        weights_two = [gather_weight(w) for w in (w_proj, w_fc1, w_fc2)]
    stream, qkv, soft, attended, wt_red, wt_qkv = forward_call(
        direct, const, place, widths, normal, red_gain, red_shift, norm1_gain, norm1_shift, b_qkv, bias, weights_one,
    )
    if direct:
        plane_two[1:] = [after(part, stream) for part in plane_two[1:]]
        weights_two = core_spread(plane_two)
    output, grad_middle, grad_att, small_two, *large_two = feed_call(
        direct, place, widths, stream, attended, cotangent, b_proj, norm2_gain, norm2_shift,
        b_fc1, b_fc2, weights_two,
    )
    if direct:
        mine, theirs = large_two
        other = from_core(theirs)
    before = attention_call(const, 0, 1, qkv, soft, grad_att)
    if direct:
        own_two, small_two, sends = core_sum(ROWS_TWO, SMALL_TWO, mine, after(other, before[0]), small_two)
        got_two = exchange(sends, True)
        grad_att = after(grad_att, own_two)
    grad_projected, small, _ = attention_call(const, 1, MB, qkv, soft, grad_att, before)
    grad_stream, small_one, *large_one = reduction_call(
        direct, place, red_gain, red_shift, wt_red, norm1_gain, norm1_shift, wt_qkv, stream, grad_middle,
        grad_projected, normal, small,
    )
    if direct:
        mine, theirs = large_one
        got_two = [after(got, grad_stream) for got in got_two]
        other = from_core(after(theirs, *got_two))
        own_two, small_two, sends = plane_sum(ROWS_TWO, SMALL_TWO, own_two, small_two, got_two)
        got_two = exchange(sends, False)
        other = after(other, own_two)
        own_one, small_one, sends = core_sum(ROWS_ONE, SMALL_ONE, mine, other, small_one)
        got_one = exchange(sends, True)
        grad_stream = after(grad_stream, own_one)
    grad_own, grad_send = merge_call(place, red_gain, wt_red, grad_stream, normal, inverse)
    if direct:
        grad_send = after(grad_send, *got_one, *got_two)
    grad_far = from_core(grad_send)
    output = output.reshape(MB, 1, 1, 7, 7 * WH, C)

    if direct:
        own_one, small_one, sends = plane_sum(ROWS_ONE, SMALL_ONE, own_one, small_one, got_one)
        got_one = exchange(sends, False)
        vector = lambda n: ((n,), F32)
        grad_input, g_proj, g_fc1, g_fc2, g_bfc1, g_bproj, g_n2g, g_n2b, g_bfc2 = whole_call(
            finish_two_kernel,
            [grad_own, grad_far, own_two, small_two, *got_two],
            [(grad_own.shape, BF16), (w_proj.T.shape, F32), (w_fc1.shape, F32), (w_fc2.T.shape, F32), vector(FF)] + [vector(C)] * 4,
        )
        g_red, g_qkv, g_rgain, g_rshift, g_n1g, g_n1b, g_bqkv, g_table = whole_call(
            finish_one_kernel,
            [after(own_one, g_proj), small_one, *got_one],
            [(w_red.T.shape, F32), (w_qkv.T.shape, F32), vector(2 * C), vector(2 * C), vector(C), vector(C)]
            + [vector(3 * C), ((HEADS, 169), F32)],
        )
        grad_input = grad_input.transpose(0, 1, 3, 2).reshape(MB, 1, 7, W2, C2)
        return (
            output, grad_input, g_rgain, g_rshift, g_red.T, g_n1g, g_n1b, g_qkv.T, g_bqkv, g_table.T, g_proj.T,
            g_bproj, g_n2g, g_n2b, g_fc1, g_bfc1, g_fc2.T, g_bfc2,
        )
    g_red, g_qkv, g_proj, g_fc1, g_fc2 = (
        scatter_grad(g) for g in (jnp.concatenate([large_one[0][0], large_one[0][1]], axis=1), large_one[1], *large_two)
    )
    one, two = lax.psum((small_one, small_two), ("sp", "dp"))
    grad_input = (grad_own + grad_far).transpose(0, 1, 3, 2).reshape(MB, 1, 7, W2, C2)
    flat = lambda rows: rows.reshape(-1)
    return (
        output, grad_input, flat(one[:2]), flat(one[2:4]), g_red, one[4], one[5], g_qkv, flat(one[6:9]),
        jnp.concatenate([one[9:15, :169], one[9:15, C2 : C2 + 169]]).T, g_proj, two[4], two[5], two[6], g_fc1, flat(two[:4]), g_fc2, two[7],
    )


def solution(mesh):
    weight = P("dp", "sp")
    placed = (
        P(None, "dp", "sp", None, None), P(None, "dp"), P(), P(), weight, P(), P(), weight, P(), P(),
        weight, P(), P(), P(), weight, P(), weight, P(), P(None, "dp", "sp", None, None, None),
    )
    out_specs = (
        P(None, "dp", "sp", None, None, None), P(None, "dp", "sp", None, None), P(), P(), weight,
        P(), P(), weight, P(), P(), weight, P(), P(), P(), weight, P(), weight, P(),
    )
    return jax.shard_map(shards, mesh=mesh, in_specs=placed, out_specs=out_specs, check_vma=False)
```

```python
import jax
import jax.numpy as jnp
import numpy as np
from jax import lax
from jax.experimental import pallas as pl
from jax.experimental.pallas import tpu as pltpu
from jax.sharding import PartitionSpec as P

C2 = 192
C = 384
HEADS = 12
HD = 32
FF = 1536
MB = 3
WH = 8
TOK = 7 * 7 * WH
ALL = MB * TOK
SLOT = 64
WROWS = WH * SLOT
W2 = 4 * 7 * WH
CHUNK = 768
EPSILON = 1e-05
DEAD = -1e30
HIGHEST = lax.Precision.HIGHEST
F32 = jnp.float32
BF16 = jnp.bfloat16
UNROLL = 4
MICRO_UNROLL = 1
COST_NORM, COST_FORWARD, COST_FEED, COST_ATTENTION, COST_REDUCTION, COST_MERGE = 3, 1, 20, 10, 9, 5
MIB = 1024 * 1024
VMEM_NORM, VMEM_FORWARD, VMEM_FEED, VMEM_ATTENTION, VMEM_REDUCTION, VMEM_MERGE, VMEM_SUM = 12, 24, 34, 24, 24, 12, 10

ROWS_ONE = 64
ROWS_TWO = 112
SMALL_ONE = 16
SMALL_TWO = 8
PLANE = [(0, 0), (0, 1), (1, 0), (1, 1)]


def nn(left, right):
    return lax.dot_general(left, right, (((1,), (0,)), ((), ())), preferred_element_type=F32)


def nt(left, right):
    return lax.dot_general(left, right, (((1,), (1,)), ((), ())), preferred_element_type=F32)


def tn(left, right):
    return lax.dot_general(left, right, (((0,), (0,)), ((), ())), preferred_element_type=F32)


def constants():
    to_window = np.zeros((WROWS, TOK), np.float32)
    for w in range(WH):
        for r in range(7):
            for c in range(7):
                to_window[w * SLOT + 7 * r + c, r * 56 + 7 * w + c] = 1
    head_mask = (np.arange(256)[:, None] // SLOT == np.arange(128)[None] // HD).astype(np.float32)
    regroup = np.zeros((SLOT, SLOT), np.float32)
    reach = np.zeros((256, 1024), np.float32)
    for p in range(49):
        regroup[p // 7 * 8 + 7 - p % 7, p] = 1
        for h in range(4):
            reach[h * SLOT + p, h * 256 + 84 + 13 * (p // 7) + p % 7] = 1
    low = lambda a: jnp.asarray(a, BF16)
    return dict(
        to_window=low(to_window),
        to_natural=low(to_window.T),
        head_mask=low(head_mask),
        regroup=low(regroup),
        reach=low(reach),
    )


def column_of(shape, width, factor, shift):
    at = lax.broadcasted_iota(jnp.int32, shape, 0)
    return at - width * ((at * factor) >> shift)


def key_column(shape):
    return jnp.where(lax.broadcasted_iota(jnp.int32, shape, 0) < 49, column_of(shape, 7, 37, 8), 1 << 20)


def split_of(core):
    at = lax.broadcasted_iota(jnp.int32, (112, W2), 0)
    column = lax.broadcasted_iota(jnp.int32, (112, W2), 1) - core * 112
    return jnp.where(column == jnp.where(at < 56, 2 * at, 2 * at - 111), 1.0, 0.0).astype(BF16)


def row(ref):
    return ref[...].reshape(1, -1)


def norm_of(values):
    center = jnp.mean(values, -1, keepdims=True)
    shifted = values - center
    inverse = lax.rsqrt(jnp.mean(shifted * shifted, -1, keepdims=True) + EPSILON)
    return shifted * inverse, inverse


def norm_back(grad_out, normal, inverse, gain):
    grad_normal = grad_out * gain
    grad_in = inverse * (
        grad_normal
        - jnp.mean(grad_normal, -1, keepdims=True)
        - normal * jnp.mean(grad_normal * normal, -1, keepdims=True)
    )
    return (
        grad_in,
        jnp.sum(grad_out * normal, 0, keepdims=True),
        jnp.sum(grad_out, 0, keepdims=True),
    )


def four_heads(rows, head_mask):
    return jnp.concatenate([rows] * 4, axis=0) * head_mask


def own_blocks(full):
    return [full[HD * h : HD * h + HD, SLOT * h : SLOT * h + SLOT] for h in range(4)]


def beside(upper, lower):
    return jnp.concatenate([upper, lower], axis=1)


def pad_rows(rows, count):
    return jnp.concatenate([rows, jnp.zeros((count - rows.shape[0], rows.shape[1]), F32)], axis=0)


def pack_kernel(red_ref, qkv_ref, proj_ref, fc1_ref, fc2_ref, pack_ref):
    qkv = qkv_ref[...].astype(F32)
    one = [red_ref[...].astype(F32), beside(qkv[:40], pad_rows(qkv[40:], 40))]
    pack_ref[:ROWS_ONE, :] = jnp.concatenate(one, axis=0).astype(BF16)
    proj, fc2 = proj_ref[...].astype(F32), fc2_ref[...].astype(F32)
    count = fc1_ref.shape[1]
    same = lax.broadcasted_iota(jnp.int32, (count, count), 0) == lax.broadcasted_iota(jnp.int32, (count, count), 1)
    fc1 = nt(jnp.where(same, 1.0, 0.0).astype(BF16), fc1_ref[...])
    two = [beside(proj[:16], pad_rows(proj[16:], 16)), beside(fc1[:48], fc1[48:]), fc2[:, :C], fc2[:, C:]]
    pack_ref[ROWS_ONE:, :] = jnp.concatenate(two, axis=0).astype(BF16)


def pack_weights(w_red, w_qkv, w_proj, w_fc1, w_fc2):
    return pl.pallas_call(
        pack_kernel,
        out_shape=jax.ShapeDtypeStruct((ROWS_ONE + ROWS_TWO, C), BF16),
    )(w_red.T, w_qkv.T, w_proj.T, w_fc1, w_fc2.T)


def each_block(place_ref):
    spot = place_ref[0]
    z, y, core = spot // 4, spot // 2 % 2, spot % 2
    for dc in range(2):
        for dy in range(2):
            for dz in range(4):
                yield dc, dz, dy, ((z ^ dz) * 2 + (y ^ dy)) * 2 + (core ^ dc)


def spots(block, stride, first, count):
    return pl.ds(pl.multiple_of(block * stride + first, 8), count)


def two_halves(place_ref, refs, dc, dz, dy):
    even = (place_ref[0] + dc) % 2 == 0
    first = place_ref[1] == 0
    blocks = []
    for dx in range(2):
        plane = 2 * dy + dx
        if plane == dz:
            blocks.append(refs[4 * dc + plane][dz].astype(F32))
        else:
            blocks.append(jnp.where(even, refs[4 * dc + plane][dz], refs[4 * dc + dz][plane]).astype(F32))
    return jnp.where(first, blocks[0], blocks[1]), jnp.where(first, blocks[1], blocks[0])


def unpack_one(place_ref, packs, red_ref, qkv_ref, red_f32, qkv_f32):
    for dc, dz, dy, block in each_block(place_ref):
        a, b = two_halves(place_ref, packs, dc, dz, dy)
        red_f32[0, spots(block, 24, 0, 24), :] = a[:24]
        red_f32[1, spots(block, 24, 0, 24), :] = b[:24]
        qkv_f32[spots(block, 72, 0, 40), :] = beside(a[24:, :C2], b[24:, :C2])
        qkv_f32[spots(block, 72, 40, 32), :] = beside(a[24:56, C2:], b[24:56, C2:])
    red_ref[...] = red_f32[...].astype(BF16)
    qkv_ref[...] = qkv_f32[...].astype(BF16)


def unpack_two(place_ref, packs, proj_ref, fc1_ref, fc2_ref, proj_f32, fc1_f32, fc2_f32):
    for dc, dz, dy, block in each_block(place_ref):
        a, b = two_halves(place_ref, packs, dc, dz, dy)
        proj_f32[spots(block, 24, 0, 16), :] = beside(a[:16, :C2], b[:16, :C2])
        proj_f32[spots(block, 24, 16, 8), :] = beside(a[:8, C2:], b[:8, C2:])
        fc1_f32[spots(block, 96, 0, 48), :] = beside(a[16:64, :C2], b[16:64, :C2])
        fc1_f32[spots(block, 96, 48, 48), :] = beside(a[16:64, C2:], b[16:64, C2:])
        for d, half in enumerate((a, b)):
            fc2_f32[spots(block, 24, 0, 24), 2 * d * C : 2 * d * C + C] = half[64:88]
            fc2_f32[spots(block, 24, 0, 24), 2 * d * C + C : 2 * d * C + 2 * C] = half[88:]
    proj_ref[...] = proj_f32[...].astype(BF16)
    fc1_ref[...] = fc1_f32[...].astype(BF16)
    fc2_ref[...] = fc2_f32[...].astype(BF16)


def put_block(place_ref, dc, dz, dy, halves, mine_ref, theirs_ref):
    first = place_ref[1] == 0
    out_ref = theirs_ref if dc else mine_ref
    count = halves[0].shape[0]
    even = (place_ref[0] + dc) % 2 == 0
    for dx in range(2):
        plane = 2 * dy + dx
        at = jnp.where(even, plane * 4 + dz, dz * 4 + plane) * count
        out_ref[pl.ds(pl.multiple_of(at, 16), count), :] = jnp.where(first, halves[dx], halves[1 - dx]).astype(BF16)


def two_terms(values):
    high = values.astype(BF16)
    return jnp.concatenate([high.astype(F32), values - high.astype(F32)], axis=0).astype(BF16)


def pack_one_grads(place_ref, red_ref, qkv_ref, small, mine_ref, theirs_ref):
    for dc, dz, dy, block in each_block(place_ref):
        top, low = qkv_ref[spots(block, 72, 0, 40), :], pad_rows(qkv_ref[spots(block, 72, 40, 32), :], 40)
        halves = []
        for d in range(2):
            lanes = slice(d * C2, d * C2 + C2)
            red = red_ref[d, spots(block, 24, 0, 24), :]
            halves.append(jnp.concatenate([red, beside(top[:, lanes], low[:, lanes])], axis=0))
        put_block(place_ref, dc, dz, dy, halves, mine_ref, theirs_ref)
    theirs_ref[16 * ROWS_ONE :, :] = two_terms(small)


def pack_two_grads(place_ref, proj_ref, fc1_ref, fc2_ref, small, mine_ref, theirs_ref):
    for dc, dz, dy, block in each_block(place_ref):
        proj_top, proj_low = proj_ref[spots(block, 24, 0, 16), :], pad_rows(proj_ref[spots(block, 24, 16, 8), :], 16)
        fc1_top, fc1_low = fc1_ref[spots(block, 96, 0, 48), :], fc1_ref[spots(block, 96, 48, 48), :]
        fc2 = fc2_ref[spots(block, 24, 0, 24), :]
        halves = []
        for d in range(2):
            lanes = slice(d * C2, d * C2 + C2)
            parts = [beside(proj_top[:, lanes], proj_low[:, lanes]), beside(fc1_top[:, lanes], fc1_low[:, lanes])]
            parts += [fc2[:, 2 * d * C : 2 * d * C + C], fc2[:, 2 * d * C + C : 2 * d * C + 2 * C]]
            halves.append(jnp.concatenate(parts, axis=0))
        put_block(place_ref, dc, dz, dy, halves, mine_ref, theirs_ref)
    theirs_ref[16 * ROWS_TWO :, :] = two_terms(small)


def small_sum(small, refs, first, count):
    for ref in refs:
        small = small + (ref[first : first + count, :].astype(F32) + ref[first + count : first + 2 * count, :].astype(F32))
    return small


def core_sum_kernel(rows, count, mine_ref, other_ref, small_ref, own_ref, small_out_ref, *send_refs):
    small = small_sum(small_ref[...], [other_ref], 16 * rows, count)
    small_out_ref[...] = small
    for k in range(4):
        at = slice(4 * k * rows, 4 * k * rows + 4 * rows)
        total = mine_ref[at, :].astype(F32) + other_ref[at, :].astype(F32)
        if k == 0:
            own_ref[...] = total
        else:
            send_refs[k - 1][: 4 * rows, :] = total.astype(BF16)
            send_refs[k - 1][4 * rows :, :] = two_terms(small)


def plane_sum_kernel(rows, count, own_ref, small_ref, *refs):
    got, own_out_ref, small_out_ref, send_refs = refs[:3], refs[3], refs[4], refs[5:]
    small = small_sum(small_ref[...], got, 4 * rows, count)
    small_out_ref[...] = small
    for k in range(4):
        at = slice(k * rows, k * rows + rows)
        total = own_ref[at, :]
        for ref in got:
            total = total + ref[at, :].astype(F32)
        if k == 0:
            own_out_ref[...] = total
        else:
            send_refs[k - 1][:rows, :] = total.astype(BF16)
            send_refs[k - 1][rows:, :] = two_terms(small)


def line_sum(rows, count, own_ref, small_ref, got):
    total = own_ref[...]
    for ref in got:
        total = total + ref[:rows, :].astype(F32)
    return total, small_sum(small_ref[...], got, rows, count)


def finish_one_kernel(own_ref, small_ref, g1, g2, g3, red_ref, qkv_ref, rgain_ref, rshift_ref, gain_ref, shift_ref, bqkv_ref, table_ref):
    rows, small = line_sum(ROWS_ONE, SMALL_ONE, own_ref, small_ref, (g1, g2, g3))
    red_ref[...] = rows[:24]
    qkv_ref[...] = jnp.concatenate([rows[24:, :C2], rows[24:56, C2:]], axis=0)
    for at, ref in ((0, rgain_ref), (2, rshift_ref), (4, gain_ref), (5, shift_ref), (6, bqkv_ref)):
        for k in range(ref.shape[0] // C):
            ref[pl.ds(k * C, C)] = small[at + k]
    table_ref[: HEADS // 2, :] = small[9:15, :169]
    table_ref[HEADS // 2 :, :] = small[9:15, C2 : C2 + 169]


def finish_two_kernel(near_ref, far_ref, own_ref, small_ref, g1, g2, g3, grad_input_ref, proj_ref, fc1_ref, fc2_ref, bfc1_ref, bproj_ref, gain_ref, shift_ref, bfc2_ref):
    grad_input_ref[...] = near_ref[...] + far_ref[...]
    rows, small = line_sum(ROWS_TWO, SMALL_TWO, own_ref, small_ref, (g1, g2, g3))
    proj_ref[...] = jnp.concatenate([rows[:16, :C2], rows[:8, C2:]], axis=0)
    fc1_ref[...] = jnp.concatenate([rows[16:64, :C2], rows[16:64, C2:]], axis=0).T
    fc2_ref[...] = beside(rows[64:88], rows[88:])
    for at, ref in ((0, bfc1_ref), (4, bproj_ref), (5, gain_ref), (6, shift_ref), (7, bfc2_ref)):
        for k in range(ref.shape[0] // C):
            ref[pl.ds(k * C, C)] = small[at + k]


def merge_norm_kernel(
    place_ref, table_ref, section_ref, incoming_ref, normal_ref, inverse_ref, bias_ref,
    parts_ref, wide_ref, reach_ref,
):
    @pl.when(pl.program_id(0) == 0)
    def _():
        wide_ref[...] = jnp.zeros_like(wide_ref)
        wide_ref[:, :169] = table_ref[...]
        reach = reach_of()
        reach_ref[:, :1024] = reach
        reach_ref[:, 1024:] = reach

    bias_part(pl.program_id(0), wide_ref, reach_ref, bias_ref)
    is_left = place_ref[0] % 2 == 0
    split = split_of(place_ref[0] % 2)
    bands = []
    for r in range(14):
        own, other = section_ref[0, r % 7], incoming_ref[0, r % 7]
        bands.append(jnp.where(is_left, own, other) if r < 7 else jnp.where(is_left, other, own))
    for r in range(7):
        apart = nt(split, jnp.concatenate(bands[2 * r : 2 * r + 2], axis=0))
        parts_ref[0, r * 56 : r * 56 + 56, :] = apart[:56]
        parts_ref[1, r * 56 : r * 56 + 56, :] = apart[56:]
    total = jnp.sum(parts_ref[0] + parts_ref[1], -1, keepdims=True)
    shifted = [parts_ref[d] - total * (1.0 / (2 * C)) for d in range(2)]
    spread = jnp.sum(shifted[0] * shifted[0] + shifted[1] * shifted[1], -1, keepdims=True)
    inverse = lax.rsqrt(spread * (1.0 / (2 * C)) + EPSILON)
    inverse_ref[0] = inverse
    for d in range(2):
        normal_ref[0, d] = shifted[d] * inverse


def reach_of():
    at = lax.broadcasted_iota(jnp.int32, (256, 1024), 0)
    lane = lax.broadcasted_iota(jnp.int32, (256, 1024), 1)
    query = at & (SLOT - 1)
    target = (at >> 6) * 256 + 84 + query + 6 * ((query * 37) >> 8)
    return jnp.where((lane == target) & (query < 49), 1.0, 0.0).astype(BF16)


def ungroup_of():
    at = lax.broadcasted_iota(jnp.int32, (SLOT, SLOT), 0)
    lane = lax.broadcasted_iota(jnp.int32, (SLOT, SLOT), 1)
    return jnp.where((lane == at + ((at * 37) >> 8)) & (at < 49), 1.0, 0.0).astype(BF16)


def bias_part(t, wide_ref, reach_ref, bias_ref):
    ungroup, reach = ungroup_of(), reach_ref[...]
    heads = []
    for h in range(4):
        rows = jnp.broadcast_to(wide_ref[pl.ds(4 * t + h, 1), :], (8, 256))
        rows = pltpu.roll(rows, 0, axis=1, stride=1, stride_axis=0)
        blocks = [pltpu.roll(rows, 13 * r, axis=1) if r else rows for r in range(7)]
        heads.append(jnp.concatenate(blocks + [jnp.zeros((8, 256), F32)], axis=0))
    rest = jnp.concatenate(heads, axis=1)
    unused = jnp.where(lax.broadcasted_iota(jnp.int32, (SLOT, 256), 0) < 49, 0.0, DEAD)
    high = rest.astype(BF16)
    terms = jnp.concatenate([high, (rest - high.astype(F32)).astype(BF16)], axis=1)
    bias_ref[0] = unused + nt(nn(ungroup, terms).astype(BF16), reach)


def stack_kernel(a_ref, b_ref, c_ref, d_ref, one_ref, two_ref):
    for k, ref in enumerate((a_ref, b_ref, c_ref, d_ref)):
        one_ref[k] = ref[:ROWS_ONE, :]
        two_ref[k] = ref[ROWS_ONE:, :]


def forward_kernel(direct, *refs):
    (
        place_ref, widths_ref, normal_ref, red_gain_ref, red_shift_ref, gain_ref, shift_ref,
        b_qkv_ref, bias_ref, to_window_ref, to_natural_ref, head_mask_ref,
    ) = refs[:12]
    cut = 20 if direct else 14
    packs, refs = refs[12:cut], refs[cut:]
    stream_ref, qkv_ref, soft_ref, attended_ref, w_red_ref, w_qkv_ref, turned_ref = refs[:7]
    core = place_ref[0] % 2
    if direct:
        unpack_one(place_ref, packs, w_red_ref, w_qkv_ref, *refs[7:])
    else:
        w_red_ref[...] = packs[0][...]
        w_qkv_ref[...] = packs[1][...]

    red_gain, red_shift = row(red_gain_ref), row(red_shift_ref)

    def micro(m, none):
        stream = 0.0
        for d in range(2):
            lanes = slice(d * C, d * C + C)
            normed = normal_ref[m, d] * red_gain[:, lanes] + red_shift[:, lanes]
            stream = stream + nt(normed.astype(BF16), w_red_ref[d])
        stream_ref[m] = stream
        normal, _ = norm_of(stream)
        first = (normal * row(gain_ref) + row(shift_ref)).astype(BF16)
        first = nn(to_window_ref[...], first).astype(BF16)
        projected = nt(first, w_qkv_ref[...]) + row(b_qkv_ref)
        qkv_ref[m, :, :C] = (projected[:, :C] * (HD**-0.5)).astype(BF16)
        qkv_ref[m, :, C:] = projected[:, C:].astype(BF16)
        width = widths_ref[m]
        key_col = key_column((SLOT, 128))

        def pair(i, carry):
            head_mask = head_mask_ref[...]
            outs = [[None, None] for _ in range(HEADS)]
            for j in range(2):
                w = 2 * i + j
                rows = pl.ds(pl.multiple_of(w * SLOT, SLOT), SLOT)
                live = jnp.where(key_col + (core * 56 + w * 7) < width, 0.0, DEAD)
                for t in range(3):
                    q = qkv_ref[m, rows, 128 * t : 128 * t + 128]
                    k = qkv_ref[m, rows, C + 128 * t : C + 128 * t + 128]
                    v = qkv_ref[m, rows, 2 * C + 128 * t : 2 * C + 128 * t + 128]
                    scores = nt(k, four_heads(q, head_mask)) + bias_ref[t]
                    parts = []
                    for half in range(2):
                        part = scores[:, 128 * half : 128 * half + 128] + live
                        exponent = jnp.exp(part - jnp.max(part, 0, keepdims=True))
                        share = 1.0 / jnp.sum(exponent, 0, keepdims=True)
                        parts.append((exponent * share).astype(BF16))
                    soft = jnp.concatenate(parts, axis=1)
                    soft_ref[m, w, t] = soft
                    for h, block in enumerate(own_blocks(tn(v, soft))):
                        outs[4 * t + h][j] = block
            lanes = pl.ds(pl.multiple_of(i * 128, 128), 128)
            for h in range(HEADS):
                turned_ref[HD * h : HD * h + HD, lanes] = beside(*outs[h]).astype(BF16)
            return carry

        lax.fori_loop(0, WH // 2, pair, 0, unroll=UNROLL)
        attended_ref[m] = nt(to_natural_ref[...], turned_ref[...]).astype(BF16)
        return none

    lax.fori_loop(0, MB, micro, 0, unroll=MICRO_UNROLL)


def feed_kernel(direct, *refs):
    (
        place_ref, widths_ref, stream_ref, attended_ref, cotangent_ref,
        b_proj_ref, gain_ref, shift_ref, b_fc1_ref, b_fc2_ref,
    ) = refs[:10]
    cut = 18 if direct else 13
    packs, refs = refs[10:cut], refs[cut:]
    output_ref, grad_middle_ref, grad_att_ref, small_ref = refs[:4]
    if direct:
        mine_ref, theirs_ref, g_proj_ref, g_fc1_ref, g_fc2_ref = refs[4:9]
        refs = refs[9:]
    else:
        g_proj_ref, g_fc1_ref, g_fc2_ref = refs[4:7]
        refs = refs[7:]
    second_ref, grad_feed_ref, grad_second_ref, inverse_ref, bias_fc1_ref, g_bfc1_ref, w_proj_ref, w_fc1_ref, w_fc2_ref = refs
    step = pl.program_id(0)
    place_col = column_of((TOK, 1), 56, 1171, 16) + (place_ref[0] % 2) * 56
    keep = jnp.concatenate([jnp.where(place_col < widths_ref[m], 1.0, 0.0) for m in range(MB)], axis=0)

    @pl.when(step == 0)
    def _():
        if direct:
            unpack_two(place_ref, packs, w_proj_ref, w_fc1_ref, w_fc2_ref, g_proj_ref, g_fc1_ref, g_fc2_ref)
        else:
            w_proj_ref[...] = packs[0][...]
            w_fc1_ref[...] = packs[1][...]
            w_fc2_ref[...] = packs[2][...]
        bias_fc1_ref[...] = row(b_fc1_ref)
        middle = stream_ref[...] + nt(attended_ref[...], w_proj_ref[...]) + row(b_proj_ref)
        normal, inverse = norm_of(middle)
        inverse_ref[...] = inverse
        grad_middle_ref[...] = normal
        second_ref[...] = (normal * row(gain_ref) + row(shift_ref)).astype(BF16)
        grad_feed = (cotangent_ref[...] * keep).astype(BF16)
        grad_feed_ref[...] = grad_feed
        small_ref[7:8] = jnp.sum(grad_feed.astype(F32), 0, keepdims=True)
        output_ref[...] = middle + row(b_fc2_ref)
        grad_second_ref[...] = jnp.zeros_like(grad_second_ref)

    units = pl.ds(pl.multiple_of(step * CHUNK, CHUNK), CHUNK)
    w_fc1 = w_fc1_ref[units, :]
    w_fc2 = w_fc2_ref[:, units]
    second = second_ref[...]
    feed = grad_feed_ref[...]
    pre = nt(second, w_fc1) + bias_fc1_ref[:, units]
    cdf = 0.5 * (1.0 + lax.erf(pre * 0.7071067811865476))
    density = 0.3989422804014327 * jnp.exp(-0.5 * pre * pre)
    act = (pre * cdf).astype(BF16)
    output_ref[...] += nt(act, w_fc2)
    g_fc2_ref[:, units] = tn(feed, act)
    grad_pre = (nn(feed, w_fc2) * (cdf + pre * density)).astype(BF16)
    g_bfc1_ref[:, units] = jnp.sum(grad_pre.astype(F32), 0, keepdims=True)
    g_fc1_ref[units, :] = tn(grad_pre, second)
    grad_second_ref[...] += nn(grad_pre, w_fc1)

    @pl.when(step == FF // CHUNK - 1)
    def _():
        output_ref[...] = output_ref[...] * keep
        grad_norm, g_gain, g_shift = norm_back(grad_second_ref[...], grad_middle_ref[...], inverse_ref[...], row(gain_ref))
        small_ref[5:6] = g_gain
        small_ref[6:7] = g_shift
        grad_middle = cotangent_ref[...] * keep + grad_norm
        grad_middle_ref[...] = grad_middle
        branch = grad_middle.astype(BF16)
        small_ref[4:5] = jnp.sum(branch.astype(F32), 0, keepdims=True)
        g_proj_ref[...] = tn(branch, attended_ref[...])
        grad_att_ref[...] = nn(branch, w_proj_ref[...]).astype(BF16)
        for k in range(4):
            small_ref[k : k + 1] = g_bfc1_ref[:, k * C : k * C + C]
        if direct:
            pack_two_grads(place_ref, g_proj_ref, g_fc1_ref, g_fc2_ref, small_ref[...], mine_ref, theirs_ref)


def table_rows(pairs_ref, regroup, reach):
    rows = []
    for t in range(3):
        sums = pairs_ref[t]
        high = sums.astype(BF16)
        low = (sums - high.astype(F32)).astype(BF16)
        spread = nn(nn(regroup, high).astype(BF16), reach) + nn(nn(regroup, low).astype(BF16), reach)
        for h in range(4):
            total = 0.0
            for r in range(7):
                part = spread[8 * r : 8 * r + 8, 256 * h : 256 * h + 256]
                total = total + (pltpu.roll(part, 256 - 13 * r, axis=1) if r else part)
            total = pltpu.roll(total, 249, axis=1, stride=1, stride_axis=0)
            rows.append(jnp.sum(total, 0, keepdims=True))
    rows = jnp.concatenate(rows, axis=0)[:, :C2]
    return beside(rows[: HEADS // 2], rows[HEADS // 2 :])


def attention_kernel(first, last, *refs):
    to_window_ref, to_natural_ref, head_mask_ref, regroup_ref, reach_ref, qkv_ref, soft_ref, grad_att_ref = refs[:8]
    refs = refs[8:]
    if first:
        before_ref, small_in_ref, pairs_in_ref = refs[:3]
        refs = refs[3:]
    grad_projected_ref, small_ref, pairs_ref, window_ref, turned_ref, grad_window_ref = refs
    if first:
        grad_projected_ref[:first] = before_ref[...]
        small_ref[...] = small_in_ref[...]
        pairs_ref[...] = pairs_in_ref[...]
    else:
        small_ref[...] = jnp.zeros_like(small_ref)
        pairs_ref[...] = jnp.zeros_like(pairs_ref)

    def micro(m, none):
        window_ref[...] = nn(to_window_ref[...], grad_att_ref[m]).astype(BF16)

        def pair(i, carry):
            head_mask = head_mask_ref[...]
            outs = [[None, None] for _ in range(HEADS)]
            for t in range(3):
                scores_sum = 0.0
                for j in range(2):
                    w = 2 * i + j
                    rows = pl.ds(pl.multiple_of(w * SLOT, SLOT), SLOT)
                    q = qkv_ref[m, rows, 128 * t : 128 * t + 128]
                    k = qkv_ref[m, rows, C + 128 * t : C + 128 * t + 128]
                    v = qkv_ref[m, rows, 2 * C + 128 * t : 2 * C + 128 * t + 128]
                    grad = four_heads(window_ref[rows, 128 * t : 128 * t + 128], head_mask)
                    soft_low = soft_ref[m, w, t]
                    soft = soft_low.astype(F32)
                    grad_soft = nt(v, grad)
                    inner = jnp.sum(grad_soft * soft, 0, keepdims=True)
                    scores = (soft * (grad_soft - inner)).astype(BF16)
                    scores_sum = scores_sum + scores.astype(F32)
                    grad_key = nn(scores, four_heads(q, head_mask))
                    grad_value = nn(soft_low, grad)
                    grad_window_ref[rows, 128 * t : 128 * t + 128] = grad_key.astype(BF16)
                    grad_window_ref[rows, C + 128 * t : C + 128 * t + 128] = grad_value.astype(BF16)
                    for h, block in enumerate(own_blocks(tn(k, scores))):
                        outs[4 * t + h][j] = block
                pairs_ref[t] += scores_sum
            lanes = pl.ds(pl.multiple_of(i * 128, 128), 128)
            for h in range(HEADS):
                turned_ref[HD * h : HD * h + HD, lanes] = (beside(*outs[h]) * (HD**-0.5)).astype(BF16)
            return carry

        lax.fori_loop(0, WH // 2, pair, 0, unroll=UNROLL)
        to_natural = to_natural_ref[...]
        grad_query = nt(to_natural, turned_ref[...])
        grad_rest = nn(to_natural, grad_window_ref[...])
        grad_projected_ref[m, :, :C] = grad_query.astype(BF16)
        grad_projected_ref[m, :, C:] = grad_rest.astype(BF16)
        small_ref[0:1] += jnp.sum(grad_query, 0, keepdims=True)
        sums = jnp.sum(grad_rest, 0, keepdims=True)
        small_ref[1:2] += sums[:, :C]
        small_ref[2:3] += sums[:, C:]
        return none

    lax.fori_loop(first, last, micro, 0, unroll=last - first)
    if last == MB:
        small_ref[3 : 3 + HEADS // 2] = table_rows(pairs_ref, regroup_ref[...], reach_ref[...])


def reduction_kernel(direct, *refs):
    (
        place_ref, red_gain_ref, red_shift_ref, w_red_ref, gain_ref, shift_ref, w_qkv_ref,
        stream_ref, grad_middle_ref, grad_projected_ref, normal_ref, small_in_ref,
    ) = refs[:12]
    refs = refs[12:]
    grad_stream_ref, small_ref = refs[:2]
    if direct:
        mine_ref, theirs_ref, g_red_ref, g_qkv_ref, sums_ref = refs[2:]
    else:
        g_red_ref, g_qkv_ref, sums_ref = refs[2:]
    grad_projected = grad_projected_ref[...]
    normal, inverse = norm_of(stream_ref[...])
    gain = row(gain_ref)
    first = (normal * gain + row(shift_ref)).astype(BF16)
    g_qkv_ref[...] = tn(grad_projected, first)
    grad_norm, g_gain, g_shift = norm_back(nn(grad_projected, w_qkv_ref[...]), normal, inverse, gain)
    grad_stream = (grad_middle_ref[...] + grad_norm).astype(BF16)
    grad_stream_ref[...] = grad_stream
    red_gain, red_shift = row(red_gain_ref), row(red_shift_ref)
    sums_ref[...] = jnp.broadcast_to(jnp.sum(grad_stream.astype(F32), 0, keepdims=True), (8, C)).T
    column = sums_ref[:, :1]
    small_ref[...] = jnp.zeros_like(small_ref)
    small_ref[4:5] = g_gain
    small_ref[5:6] = g_shift
    small_ref[6:15] = small_in_ref[:9]
    for d in range(2):
        lanes = slice(d * C, d * C + C)
        weight = w_red_ref[d].astype(F32)
        product = sum(tn(grad_stream[m * TOK : m * TOK + TOK], normal_ref[m, d].astype(BF16)) for m in range(MB))
        small_ref[d : d + 1] = jnp.sum(weight * product, 0, keepdims=True)
        small_ref[2 + d : 3 + d] = jnp.sum(weight * column, 0, keepdims=True)
        g_red_ref[d] = product * red_gain[:, lanes] + column * red_shift[:, lanes]
    if direct:
        pack_one_grads(place_ref, g_red_ref, g_qkv_ref, small_ref[...], mine_ref, theirs_ref)


def merge_kernel(
    place_ref, red_gain_ref, w_red_ref, grad_stream_ref, normal_ref, inverse_ref, own_ref, send_ref,
    parts_ref, rows_ref,
):
    core = place_ref[0] % 2
    red_gain = row(red_gain_ref)
    grad_stream = grad_stream_ref[0]
    grads = [nn(grad_stream, w_red_ref[d]) * red_gain[:, d * C : d * C + C] for d in range(2)]
    normals = [normal_ref[0, d] for d in range(2)]
    mean_one = jnp.sum(grads[0] + grads[1], -1, keepdims=True) * (1.0 / (2 * C))
    mean_two = jnp.sum(grads[0] * normals[0] + grads[1] * normals[1], -1, keepdims=True) * (1.0 / (2 * C))
    for d in range(2):
        parts_ref[d] = inverse_ref[0] * (grads[d] - mean_one - normals[d] * mean_two)
    join = split_of(core)
    for r in range(7):
        at = slice(r * 56, r * 56 + 56)
        apart = jnp.concatenate([parts_ref[0, at, :], parts_ref[1, at, :]], axis=0).astype(BF16)
        rows = tn(apart, join).astype(BF16)
        rows_ref[2 * r], rows_ref[2 * r + 1] = rows[:C2], rows[C2:]
    is_left = core == 0
    for r in range(7):
        upper, lower = rows_ref[r], rows_ref[7 + r]
        own_ref[0, r] = jnp.where(is_left, upper, lower)
        send_ref[0, r] = jnp.where(is_left, lower, upper)


SCALARS = pl.BlockSpec(memory_space=pltpu.SMEM)


def whole(shape):
    return pl.BlockSpec(shape, lambda m: (0,) * len(shape), pipeline_mode=pl.Buffered(1))


def each(shape):
    return pl.BlockSpec((1,) + shape, lambda m: (m,) + (0,) * len(shape))


def scalar(array):
    return (array, SCALARS)


def fixed(array):
    return (array, whole(array.shape))


def stepped(array):
    return (array, each(array.shape[1:]))


def out_fixed(shape, dtype):
    return (shape, dtype, whole(shape))


def out_stepped(shape, dtype):
    return ((MB,) + shape, dtype, each(shape))


def run_kernel(kernel, ins, outs, scratch, micros, vmem, steps=MB):
    return pl.pallas_call(
        kernel,
        grid=(steps,),
        in_specs=[spec for _, spec in ins],
        out_specs=[spec for _, _, spec in outs],
        out_shape=[jax.ShapeDtypeStruct(shape, dtype) for shape, dtype, _ in outs],
        scratch_shapes=scratch,
        compiler_params=pltpu.CompilerParams(vmem_limit_bytes=vmem * MIB),
        cost_estimate=pl.CostEstimate(flops=int(micros * 1.15e9), bytes_accessed=0, transcendentals=0),
    )(*[array for array, _ in ins])


def whole_call(kernel, ins, outs):
    return pl.pallas_call(
        kernel,
        out_shape=[jax.ShapeDtypeStruct(shape, dtype) for shape, dtype in outs],
        compiler_params=pltpu.CompilerParams(vmem_limit_bytes=VMEM_SUM * MIB),
    )(*ins)


def merge_norm_call(place, table, section, incoming):
    return run_kernel(
        merge_norm_kernel,
        [
            scalar(place), fixed(table), stepped(section), stepped(incoming),
        ],
        [out_stepped((2, TOK, C), F32), out_stepped((TOK, 1), F32), out_stepped((SLOT, 256), F32)],
        [pltpu.VMEM((2, TOK, C), F32), pltpu.VMEM((HEADS, 256), F32), pltpu.VMEM((256, 2048), BF16)],
        COST_NORM,
        VMEM_NORM,
    )


def stack(blocks):
    return whole_call(stack_kernel, blocks, [((4, ROWS_ONE, C), BF16), ((4, ROWS_TWO, C), BF16)])


def forward_call(direct, const, place, widths, normal, red_gain, red_shift, gain, shift, b_qkv, bias, weights):
    return run_kernel(
        lambda *refs: forward_kernel(direct, *refs),
        [
            scalar(place), scalar(widths), fixed(normal), fixed(red_gain), fixed(red_shift), fixed(gain), fixed(shift), fixed(b_qkv), fixed(bias), fixed(const["to_window"]),
            fixed(const["to_natural"]), fixed(const["head_mask"]),
        ] + [fixed(w) for w in weights],
        [
            out_fixed((MB, TOK, C), F32),
            out_fixed((MB, WROWS, 3 * C), BF16),
            out_fixed((MB, WH, 3, SLOT, 256), BF16),
            out_fixed((MB, TOK, C), BF16),
            out_fixed((2, C, C), BF16),
            out_fixed((3 * C, C), BF16),
        ],
        [pltpu.VMEM((C, WROWS), BF16)]
        + ([pltpu.VMEM((2, C, C), F32), pltpu.VMEM((3 * C, C), F32)] if direct else []),
        COST_FORWARD,
        VMEM_FORWARD,
        1,
    )


def feed_call(direct, place, widths, stream, attended, cotangent, b_proj, gain, shift, b_fc1, b_fc2, weights):
    grads = [((C, C), F32), ((FF, C), F32), ((C, FF), F32)]
    packed = [((16 * ROWS_TWO, C), BF16), ((16 * ROWS_TWO + 2 * SMALL_TWO, C), BF16)]
    scratch = [
        pltpu.VMEM((ALL, C), BF16), pltpu.VMEM((ALL, C), BF16), pltpu.VMEM((ALL, C), F32), pltpu.VMEM((ALL, 1), F32),
        pltpu.VMEM((1, FF), F32), pltpu.VMEM((1, FF), F32),
        pltpu.VMEM((C, C), BF16), pltpu.VMEM((FF, C), BF16), pltpu.VMEM((C, FF), BF16),
    ]
    if direct:
        scratch = [pltpu.VMEM(*g) for g in grads] + scratch
    flat = lambda array: array.reshape(ALL, C)
    output, grad_middle, grad_att, *rest = run_kernel(
        lambda *refs: feed_kernel(direct, *refs),
        [
            scalar(place), scalar(widths), fixed(flat(stream)), fixed(flat(attended)), fixed(flat(cotangent)),
            fixed(b_proj), fixed(gain), fixed(shift), fixed(b_fc1), fixed(b_fc2),
        ] + [fixed(w) for w in weights],
        [
            out_fixed((ALL, C), F32),
            out_fixed((ALL, C), F32),
            out_fixed((ALL, C), BF16),
            out_fixed((SMALL_TWO, C), F32),
        ] + [out_fixed(*o) for o in (packed if direct else grads)],
        scratch,
        COST_FEED,
        VMEM_FEED,
        FF // CHUNK,
    )
    return output, grad_middle.reshape(MB, TOK, C), grad_att.reshape(MB, TOK, C), *rest


def attention_call(const, first, last, qkv, soft, grad_att, before=()):
    return run_kernel(
        lambda *refs: attention_kernel(first, last, *refs),
        [fixed(const[n]) for n in ("to_window", "to_natural", "head_mask", "regroup", "reach")]
        + [fixed(qkv), fixed(soft), fixed(grad_att)]
        + [fixed(part) for part in before],
        [out_fixed((last, TOK, 3 * C), BF16), out_fixed((16, C), F32), out_fixed((3, SLOT, 256), F32)],
        [
            pltpu.VMEM((WROWS, C), BF16),
            pltpu.VMEM((C, WROWS), BF16),
            pltpu.VMEM((WROWS, 2 * C), BF16),
        ],
        COST_ATTENTION * (last - first) // MB,
        VMEM_ATTENTION,
        1,
    )


def reduction_call(direct, place, red_gain, red_shift, w_red, gain, shift, w_qkv, stream, grad_middle, grad_projected, normal, small):
    grads = [((2, C, C), F32), ((3 * C, C), F32)]
    packed = [((16 * ROWS_ONE, C), BF16), ((16 * ROWS_ONE + 2 * SMALL_ONE, C), BF16)]
    flat = lambda array: array.reshape(ALL, array.shape[-1])
    grad_stream, *rest = run_kernel(
        lambda *refs: reduction_kernel(direct, *refs),
        [
            scalar(place), fixed(red_gain), fixed(red_shift), fixed(w_red), fixed(gain), fixed(shift), fixed(w_qkv),
            fixed(flat(stream)), fixed(flat(grad_middle)), fixed(flat(grad_projected)), fixed(normal), fixed(small),
        ],
        [out_fixed((ALL, C), BF16), out_fixed((SMALL_ONE, C), F32)]
        + [out_fixed(*o) for o in (packed if direct else grads)],
        ([pltpu.VMEM(*g) for g in grads] if direct else []) + [pltpu.VMEM((C, 8), F32)],
        COST_REDUCTION,
        VMEM_REDUCTION,
        1,
    )
    return grad_stream.reshape(MB, TOK, C), *rest


def merge_call(place, red_gain, w_red, grad_stream, normal, inverse):
    return run_kernel(
        merge_kernel,
        [
            scalar(place), fixed(red_gain), fixed(w_red),
            stepped(grad_stream), stepped(normal), stepped(inverse),
        ],
        [out_stepped((7, C2, W2), BF16), out_stepped((7, C2, W2), BF16)],
        [pltpu.VMEM((2, TOK, C), F32), pltpu.VMEM((14, C2, W2), BF16)],
        COST_MERGE,
        VMEM_MERGE,
    )


def from_core(block):
    count = lax.axis_size("sp")
    return lax.ppermute(block, "sp", [(i, i ^ 1) for i in range(count)])


def move(block, swapped, k):
    route = []
    for spot in range(16):
        for x in range(2):
            if (spot % 2 == 0) != swapped:
                other, far = spot ^ (4 * k), x
            else:
                other, far = spot ^ (2 * PLANE[k][0]), x ^ PLANE[k][1]
            route.append((2 * spot + x, 2 * other + far))
    return lax.ppermute(block, ("sp", "dp"), route)


def others(block, swapped):
    return [move(block, swapped, k) for k in range(1, 4)]


def core_spread(mine):
    return mine + [from_core(part) for part in mine]


def after(value, *others):
    return lax.optimization_barrier((value,) + others)[0]


def core_sum(rows, count, mine, other, small):
    send = ((4 * rows + 2 * count, C), BF16)
    own, small, *sends = whole_call(
        lambda *refs: core_sum_kernel(rows, count, *refs),
        [mine, other, small],
        [((4 * rows, C), F32), ((count, C), F32), send, send, send],
    )
    return own, small, sends


def plane_sum(rows, count, own, small, got):
    send = ((rows + 2 * count, C), BF16)
    own, small, *sends = whole_call(
        lambda *refs: plane_sum_kernel(rows, count, *refs),
        [own, small, *got],
        [((rows, C), F32), ((count, C), F32), send, send, send],
    )
    return own, small, sends


def exchange(sends, swapped):
    return [move(send, swapped, k) for k, send in zip(range(1, 4), sends)]


def gather_weight(shard):
    rows = lax.all_gather(shard.T, "sp", axis=0, tiled=True)
    return lax.all_gather(rows, "dp", axis=1, tiled=True)


def scatter_grad(grad):
    share = lax.psum_scatter(grad.astype(BF16), "sp", scatter_dimension=0, tiled=True)
    share = lax.psum_scatter(share, "dp", scatter_dimension=1, tiled=True)
    return share.astype(F32).T


def shards(
    section_two, widths, red_gain, red_shift, w_red, norm1_gain, norm1_shift, w_qkv, b_qkv,
    bias_table, w_proj, b_proj, norm2_gain, norm2_shift, w_fc1, b_fc1, w_fc2, b_fc2, cotangent,
):
    direct = lax.axis_size("sp") == 16 and lax.axis_size("dp") == 2
    const = constants()
    place = jnp.stack([lax.axis_index("sp"), lax.axis_index("dp")]).astype(jnp.int32)
    widths = widths.reshape(MB)
    section = section_two.reshape(MB, 7, W2, C2).transpose(0, 1, 3, 2)
    incoming = from_core(section)
    if direct:
        pack = pack_weights(w_red, w_qkv, w_proj, w_fc1, w_fc2)
        line = [pack] + others(pack, False)
    normal, inverse, bias = merge_norm_call(place, bias_table.T, section, incoming)
    if direct:
        line[1:] = [after(part, normal) for part in line[1:]]
        column_one, column_two = stack(line)
        weights_one = core_spread([column_one] + others(column_one, True))
        plane_two = [column_two] + others(column_two, True)
    else:
        wt_red = gather_weight(w_red)
        weights_one = [jnp.stack([wt_red[:, :C], wt_red[:, C:]]), gather_weight(w_qkv)]
        weights_two = [gather_weight(w) for w in (w_proj, w_fc1, w_fc2)]
    stream, qkv, soft, attended, wt_red, wt_qkv = forward_call(
        direct, const, place, widths, normal, red_gain, red_shift, norm1_gain, norm1_shift, b_qkv, bias, weights_one,
    )
    if direct:
        plane_two[1:] = [after(part, stream) for part in plane_two[1:]]
        weights_two = core_spread(plane_two)
    output, grad_middle, grad_att, small_two, *large_two = feed_call(
        direct, place, widths, stream, attended, cotangent, b_proj, norm2_gain, norm2_shift,
        b_fc1, b_fc2, weights_two,
    )
    if direct:
        mine, theirs = large_two
        other = from_core(theirs)
    before = attention_call(const, 0, 1, qkv, soft, grad_att)
    if direct:
        own_two, small_two, sends = core_sum(ROWS_TWO, SMALL_TWO, mine, after(other, before[0]), small_two)
        got_two = exchange(sends, True)
        grad_att = after(grad_att, own_two)
    grad_projected, small, _ = attention_call(const, 1, MB, qkv, soft, grad_att, before)
    grad_stream, small_one, *large_one = reduction_call(
        direct, place, red_gain, red_shift, wt_red, norm1_gain, norm1_shift, wt_qkv, stream, grad_middle,
        grad_projected, normal, small,
    )
    if direct:
        mine, theirs = large_one
        got_two = [after(got, grad_stream) for got in got_two]
        other = from_core(after(theirs, *got_two))
        own_two, small_two, sends = plane_sum(ROWS_TWO, SMALL_TWO, own_two, small_two, got_two)
        got_two = exchange(sends, False)
        other = after(other, own_two)
        own_one, small_one, sends = core_sum(ROWS_ONE, SMALL_ONE, mine, other, small_one)
        got_one = exchange(sends, True)
        grad_stream = after(grad_stream, own_one)
    grad_own, grad_send = merge_call(place, red_gain, wt_red, grad_stream, normal, inverse)
    if direct:
        grad_send = after(grad_send, *got_one, *got_two)
    grad_far = from_core(grad_send)
    output = output.reshape(MB, 1, 1, 7, 7 * WH, C)

    if direct:
        own_one, small_one, sends = plane_sum(ROWS_ONE, SMALL_ONE, own_one, small_one, got_one)
        got_one = exchange(sends, False)
        vector = lambda n: ((n,), F32)
        grad_input, g_proj, g_fc1, g_fc2, g_bfc1, g_bproj, g_n2g, g_n2b, g_bfc2 = whole_call(
            finish_two_kernel,
            [grad_own, grad_far, own_two, small_two, *got_two],
            [(grad_own.shape, BF16), (w_proj.T.shape, F32), (w_fc1.shape, F32), (w_fc2.T.shape, F32), vector(FF)] + [vector(C)] * 4,
        )
        g_red, g_qkv, g_rgain, g_rshift, g_n1g, g_n1b, g_bqkv, g_table = whole_call(
            finish_one_kernel,
            [after(own_one, g_proj), small_one, *got_one],
            [(w_red.T.shape, F32), (w_qkv.T.shape, F32), vector(2 * C), vector(2 * C), vector(C), vector(C)]
            + [vector(3 * C), ((HEADS, 169), F32)],
        )
        grad_input = grad_input.transpose(0, 1, 3, 2).reshape(MB, 1, 7, W2, C2)
        return (
            output, grad_input, g_rgain, g_rshift, g_red.T, g_n1g, g_n1b, g_qkv.T, g_bqkv, g_table.T, g_proj.T,
            g_bproj, g_n2g, g_n2b, g_fc1, g_bfc1, g_fc2.T, g_bfc2,
        )
    g_red, g_qkv, g_proj, g_fc1, g_fc2 = (
        scatter_grad(g) for g in (jnp.concatenate([large_one[0][0], large_one[0][1]], axis=1), large_one[1], *large_two)
    )
    one, two = lax.psum((small_one, small_two), ("sp", "dp"))
    grad_input = (grad_own + grad_far).transpose(0, 1, 3, 2).reshape(MB, 1, 7, W2, C2)
    flat = lambda rows: rows.reshape(-1)
    return (
        output, grad_input, flat(one[:2]), flat(one[2:4]), g_red, one[4], one[5], g_qkv, flat(one[6:9]),
        jnp.concatenate([one[9:15, :169], one[9:15, C2 : C2 + 169]]).T, g_proj, two[4], two[5], two[6], g_fc1, flat(two[:4]), g_fc2, two[7],
    )


def solution(mesh):
    weight = P("dp", "sp")
    placed = (
        P(None, "dp", "sp", None, None), P(None, "dp"), P(), P(), weight, P(), P(), weight, P(), P(),
        weight, P(), P(), P(), weight, P(), weight, P(), P(None, "dp", "sp", None, None, None),
    )
    out_specs = (
        P(None, "dp", "sp", None, None, None), P(None, "dp", "sp", None, None), P(), P(), weight,
        P(), P(), weight, P(), P(), weight, P(), P(), P(), weight, P(), weight, P(),
    )
    return jax.shard_map(shards, mesh=mesh, in_specs=placed, out_specs=out_specs, check_vma=False)
```
